32 devices in a mesh: dp: 2 (over x), roll: 4 (over z), tp: 4 (over y, core).
Axes of the slice: x: 2, y: 2, z: 4, core: 2. Of those that a mesh axis runs over, the one named last changes fastest.
Arguments:
- train_inputs: bfloat16 [3072, 4096], P(('dp', 'roll'), 'tp'), may hold values from -75 to 75
- train_cotangent: bfloat16 [3072, 4096], P(('dp', 'roll'), 'tp'), may hold values from -75 to 75
- factor_a: float32 [4096, 128], P('tp'), may hold values from -0.09375 to 0.09375
- factor_b: float32 [128, 4096], P(None, 'tp'), may hold values from -0.18 to 0.18
- base_weight: bfloat16 [4096, 4096], P('tp'), may hold values from -0.09375 to 0.09375
- incoming: bfloat16 [2, 2048, 4096], P(None, ('dp', 'roll'), 'tp'), may hold values from -75 to 75
- norm_gain: float32 [4096], P('tp'), may hold values from 0.1 to 1.9
- positions: int32 [2048], P(('dp', 'roll')), may hold values from 0 to 8191
Outputs:
- new_a: float32 [4096, 128], P('tp')
- new_b: float32 [128, 4096], P(None, 'tp')
- queries: bfloat16 [2, 2048, 4096], P(None, ('dp', 'roll'), 'tp')
The draws below stay inside these ranges and needn't reach their ends.
All inputs are finite; a program needn't handle non-finite values.
Results may differ from the reference program's by a relative error of at most 0.015.
Values may be sent and summed in bfloat16 or wider, within the bound.
No kernel may reach another device: no remote copies, remote signals or barrier semaphores. Data moves between devices by JAX's collectives and lax.ppermute only.
A program may use at most 128 MiB of HBM per device.

```python
import math
import jax
import jax.numpy as jnp
from jax import lax

D = 4096
HEAD = 128
R = 128
TRAIN_TOKENS = 3072
ROWS = 2048
N_TP = 4


def ramped(key, rows, cols, row_lo, row_hi):
    first, second = jax.random.split(key, 2)
    base = jnp.clip(jax.random.normal(first, (rows, cols), jnp.float32), -6.0, 6.0)
    ramp = 1.0 + 2.0 * jnp.arange(cols, dtype=jnp.float32) / (cols - 1)
    scale = jnp.exp(jax.random.uniform(second, (rows, 1), jnp.float32, math.log(row_lo), math.log(row_hi)))
    return jnp.clip(base * scale * ramp[None, :], -75.0, 75.0)


def draw_train_inputs(key, part):
    key = jax.random.fold_in(key, 11)
    return ramped(key, TRAIN_TOKENS, D, 0.5, 2.0).astype(jnp.bfloat16)


def draw_train_cotangent(key, part):
    key = jax.random.fold_in(key, 23)
    return ramped(key, TRAIN_TOKENS, D, 0.5, 2.0).astype(jnp.bfloat16)


def draw_incoming(key, part):
    key = jax.random.fold_in(key, 37)
    flat = ramped(key, 2 * ROWS, D, 0.5, 2.0)
    return flat.reshape(2, ROWS, D).astype(jnp.bfloat16)


def touch_ends(entries, own_key, smallest, high):
    longest = entries.shape.index(max(entries.shape))
    spots = []
    for shift in (0, 1):
        where = [jax.random.randint(jax.random.fold_in(own_key, axis), (), 0, length) for axis, length in enumerate(entries.shape)]
        where[longest] = (where[longest] + shift) % entries.shape[longest]
        spots.append(tuple(where))
    return entries.at[spots[0]].set(smallest).at[spots[1]].set(high)


def block_scale(stream_key, shape, pieces, least, largest):
    def one(dim, shards_of):
        heights = jax.random.uniform(jax.random.fold_in(jax.random.fold_in(stream_key, 6), dim), (shards_of,), jnp.float32, least / len(pieces), largest / len(pieces))
        return jnp.repeat(jnp.exp(heights), shape[dim] // shards_of).reshape((-1,) + (1,) * (len(shape) - dim - 1))

    gain = one(*pieces[0])
    for cut in pieces[1:]:
        gain = gain * one(*cut)
    return gain


def gaussian(stream_key, extent, scale, reach, pieces=(), held_as=jnp.bfloat16):
    result = scale * jax.random.normal(stream_key, extent, jnp.float32)
    if pieces:
        result = result * block_scale(stream_key, extent, pieces, -0.22, 0.18)
    return jnp.clip(result, -reach, reach).astype(held_as)


def setup_inputs(seed: int = 0) -> dict:
    streams_of = jax.random.split(jax.random.key(seed), 9)
    train_inputs = draw_train_inputs(jax.random.fold_in(streams_of[8], 71), 0)
    train_cotangent = draw_train_cotangent(jax.random.fold_in(streams_of[8], 71), 0)
    factor_a = gaussian(streams_of[2], (D, R), D ** -0.5, 0.09375, ((0, 4),), jnp.float32)
    factor_b = gaussian(streams_of[3], (R, D), 0.03, 0.18, ((1, 4),), jnp.float32)
    base_weight = gaussian(streams_of[4], (D, D), D ** -0.5, 0.09375, ((0, 4),))
    incoming = draw_incoming(jax.random.fold_in(streams_of[8], 71), 0)
    norm_gain = jnp.clip(1.0 + 0.18 * jax.random.normal(streams_of[6], (D,), jnp.float32), 0.1, 1.9)
    positions = touch_ends(jax.random.randint(streams_of[7], (ROWS,), 0, 8192), jax.random.fold_in(streams_of[7], 1), 0, 8191).astype(jnp.int32)
    return {"train_inputs": train_inputs, "train_cotangent": train_cotangent, "factor_a": factor_a, "factor_b": factor_b, "base_weight": base_weight, "incoming": incoming, "norm_gain": norm_gain, "positions": positions}


SCALE = 2.0
LEARN = 3.0
EPS = 1e-05
NORM_EPS = 1e-06

def rotate(values, angle_pos):
    count = values.shape[0]
    heads = values.reshape(count, -1, HEAD)
    half = HEAD // 2
    freq = 10000.0 ** (-jnp.arange(half, dtype=jnp.float32) / half)
    angle = angle_pos[:, None] * freq[None, :]
    cosine = jnp.cos(angle)[:, None, :]
    sine = jnp.sin(angle)[:, None, :]
    first = heads[..., :half]
    second = heads[..., half:]
    turned = jnp.concatenate([first * cosine - second * sine, second * cosine + first * sine], axis=-1)
    return turned.reshape(count, -1)

def reference(train_inputs, train_cotangent, factor_a, factor_b, base_weight, incoming, norm_gain, positions):
    a_half = factor_a.astype(jnp.bfloat16)
    b_half = factor_b.astype(jnp.bfloat16)
    low_u = jnp.dot(train_inputs, a_half, preferred_element_type=jnp.float32).astype(jnp.bfloat16)
    low_v = jnp.dot(train_cotangent, b_half.T, preferred_element_type=jnp.float32).astype(jnp.bfloat16)
    grad_a = SCALE * jnp.dot(train_inputs.T, low_v, preferred_element_type=jnp.float32)
    grad_b = SCALE * jnp.dot(low_u.T, train_cotangent, preferred_element_type=jnp.float32)
    total = jnp.sum(grad_a * grad_a) + jnp.sum(grad_b * grad_b)
    rate = LEARN * lax.rsqrt(total + NORM_EPS)
    new_a = factor_a - rate * grad_a
    new_b = factor_b - rate * grad_b
    merged = (base_weight.astype(jnp.float32) + SCALE * jnp.dot(new_a.astype(jnp.bfloat16), new_b.astype(jnp.bfloat16), preferred_element_type=jnp.float32)).astype(jnp.bfloat16)
    width = D // N_TP
    results = []
    for stepnum in range(2):
        wide = incoming[stepnum].astype(jnp.float32)
        meansq = lax.optimization_barrier(jnp.mean(wide * wide, axis=-1, keepdims=True))
        normed = (wide * lax.rsqrt(meansq + EPS) * norm_gain[None, :]).astype(jnp.bfloat16)
        query = jnp.zeros((normed.shape[0], D), jnp.float32)
        for shard in range(N_TP):
            block = jnp.dot(normed[:, shard * width:(shard + 1) * width], merged[shard * width:(shard + 1) * width, :], preferred_element_type=jnp.float32).astype(jnp.bfloat16)
            query = query + lax.optimization_barrier(block).astype(jnp.float32)
        angle_pos = positions.astype(jnp.float32) + float(stepnum)
        results.append(rotate(query, angle_pos).astype(jnp.bfloat16))
    return (new_a, new_b, jnp.stack(results))
```

```python
import jax
import jax.numpy as jnp
from jax import lax
from jax.sharding import PartitionSpec as P

D = 4096
HEAD = 128
SCALE = 2.0
LEARN = 3.0
EPS = 1e-05
NORM_EPS = 1e-06

BF = jnp.bfloat16
F32 = jnp.float32


def swap(x, axis, n, k):
    return lax.ppermute(x, axis, [(i, i ^ k) for i in range(n)])


def turn_tables(positions, steps):
    half = HEAD // 2
    freq = 10000.0 ** (-jnp.arange(half, dtype=F32) / half)
    cos, sin = [], []
    for step in range(steps):
        angle = (positions.astype(F32) + float(step))[:, None] * freq[None, :]
        c, s = jnp.cos(angle), jnp.sin(angle)
        cos.append(jnp.concatenate([c, c], axis=-1))
        sin.append(jnp.concatenate([-s, s], axis=-1))
    return jnp.stack(cos), jnp.stack(sin)


def build(n_dp, n_roll, n_tp):
    def scatter_sum(x, axis, n):
        me = lax.axis_index(axis)
        total = lax.dynamic_index_in_dim(x, me, 0, keepdims=False)
        got = [
            swap(lax.dynamic_index_in_dim(x, me ^ k, 0, keepdims=False).astype(BF), axis, n, k)
            for k in range(1, n)
        ]
        for g in got:
            total = total + g.astype(F32)
        return total

    def gather(x, axis, n):
        me = lax.axis_index(axis)
        out = jnp.zeros((n,) + x.shape, x.dtype)
        out = lax.dynamic_update_index_in_dim(out, x, me, 0)
        for k in range(1, n):
            out = lax.dynamic_update_index_in_dim(out, swap(x, axis, n, k), me ^ k, 0)
        return out

    def sum_tp(x):
        x = x + swap(x.astype(BF), "tp", n_tp, 1).astype(F32)
        return x + swap(x.astype(BF), "tp", n_tp, 2).astype(F32)

    def on_device(
        train_inputs, train_cotangent, factor_a, factor_b, base_weight, incoming, norm_gain, positions
    ):
        steps, rows, width = incoming.shape
        rank = factor_a.shape[1]
        tp = lax.axis_index("tp")
        part_u = jnp.dot(train_inputs, factor_a.astype(BF), preferred_element_type=F32)
        part_v = lax.dot_general(
            train_cotangent, factor_b.astype(BF), (((1,), (1,)), ((), ())), preferred_element_type=F32
        )
        low = sum_tp(jnp.stack([part_u, part_v])).astype(BF)

        wide = incoming.reshape(steps * rows, width).astype(F32)
        sumsq = jnp.sum(wide * wide, axis=-1)
        sumsq = sumsq + swap(sumsq, "tp", n_tp, 1)
        sumsq = sumsq + swap(sumsq, "tp", n_tp, 2)
        scale = lax.rsqrt(sumsq / D + EPS)[:, None]
        gained = (wide * norm_gain[None, :]).astype(BF)
        part_q = jnp.dot(gained, base_weight, preferred_element_type=F32).astype(BF)
        blocks = [
            lax.dynamic_slice_in_dim(part_q, (tp ^ k) * width, width, 1) for k in range(n_tp)
        ]
        far = (blocks[2].astype(F32) + swap(blocks[3], "tp", n_tp, 1).astype(F32)).astype(BF)
        base = blocks[0].astype(F32) + swap(blocks[1], "tp", n_tp, 1).astype(F32)
        base = base + swap(far, "tp", n_tp, 2).astype(F32)
        low_q = sum_tp(jnp.dot(gained, factor_a.astype(BF), preferred_element_type=F32))

        grad_a = SCALE * lax.dot_general(
            train_inputs, low[1], (((0,), (0,)), ((), ())), preferred_element_type=F32
        )
        grad_b = SCALE * lax.dot_general(
            train_cotangent, low[0], (((0,), (0,)), ((), ())), preferred_element_type=F32
        )
        grads = jnp.stack([grad_a, grad_b], axis=1)
        chunk = scatter_sum(grads.reshape(n_dp, width // n_dp, 2, rank), "dp", n_dp)
        chunk = scatter_sum(chunk.reshape(n_roll, -1, 2, rank), "roll", n_roll)
        grads = gather(gather(chunk.astype(BF), "roll", n_roll), "dp", n_dp)
        grads = grads.reshape(width, 2, rank)
        grad_a16, grad_b16 = grads[:, 0], grads[:, 1]
        grad_a = grad_a16.astype(F32)
        grad_b = grad_b16.astype(F32)
        total = jnp.sum(grad_a * grad_a) + jnp.sum(grad_b * grad_b)
        total = total + swap(total, "tp", n_tp, 1)
        total = total + swap(total, "tp", n_tp, 2)
        low_g = sum_tp(jnp.dot(gained, grad_a16, preferred_element_type=F32))
        rate = LEARN * lax.rsqrt(total + NORM_EPS)
        new_a = factor_a - rate * grad_a
        new_b = factor_b - rate * grad_b.T
        mix = (low_q - rate * low_g) * scale
        query = base * scale + SCALE * jnp.dot(
            mix.astype(BF), new_b.astype(BF), preferred_element_type=F32
        )
        cos, sin = turn_tables(positions, steps)
        heads = query.reshape(steps, rows, -1, HEAD)
        other = jnp.concatenate([heads[..., HEAD // 2 :], heads[..., : HEAD // 2]], axis=-1)
        turned = heads * cos[:, :, None, :] + other * sin[:, :, None, :]
        return new_a, new_b, turned.reshape(steps, rows, width).astype(BF)

    return on_device


def solution(mesh):
    n_dp, n_roll, n_tp = (mesh.shape[a] for a in ("dp", "roll", "tp"))
    return jax.shard_map(
        build(n_dp, n_roll, n_tp),
        mesh=mesh,
        in_specs=(
            P(("dp", "roll"), "tp"),
            P(("dp", "roll"), "tp"),
            P("tp", None),
            P(None, "tp"),
            P("tp", None),
            P(None, ("dp", "roll"), "tp"),
            P("tp"),
            P(("dp", "roll")),
        ),
        out_specs=(P("tp", None), P(None, "tp"), P(None, ("dp", "roll"), "tp")),
        check_vma=False,
    )
```

```python
import functools

import jax
import jax.numpy as jnp
from jax import lax
from jax.experimental import pallas as pl
from jax.experimental.pallas import tpu as pltpu
from jax.sharding import PartitionSpec as P

D = 4096
HEAD = 128
SCALE = 2.0
LEARN = 3.0
EPS = 1e-05
NORM_EPS = 1e-06
LANES = 128
EXTRA = 32

BF = jnp.bfloat16
F32 = jnp.float32
VMEM = pl.BlockSpec(memory_space=pltpu.VMEM)
SMEM = pl.BlockSpec(memory_space=pltpu.SMEM)
ANY = pl.BlockSpec(memory_space=pl.ANY)
PARAMS = pltpu.CompilerParams(vmem_limit_bytes=32 * 1024 * 1024)


def shape(dims, dtype):
    return jax.ShapeDtypeStruct(dims, dtype)


def dot(a, b, dims=((1,), (0,))):
    return lax.dot_general(a, b, (dims, ((), ())), preferred_element_type=F32)


def swap(x, axis, n, k):
    return lax.ppermute(x, axis, [(i, i ^ k) for i in range(n)])


def split_terms(values):
    high = values.astype(BF)
    rest = values - high.astype(F32)
    middle = rest.astype(BF)
    last = (rest - middle.astype(F32)).astype(BF)
    return jnp.concatenate([high, middle, last, jnp.zeros_like(last)], axis=0)


def join_terms(ref, count):
    x = ref[count : count + EXTRA, :].astype(F32)
    return (x[0:8] + x[8:16]) + x[16:24]


def rank_kernel(x_ref, v_ref, a_ref, b_ref, out_ref):
    count = x_ref.shape[0]
    out_ref[:count] = dot(x_ref[...], a_ref[...].astype(BF)).astype(BF)
    out_ref[count:] = dot(v_ref[...], b_ref[...].astype(BF), ((1,), (1,))).astype(BF)


def store_block(per, block, one_ref, two_ref):
    step = pl.program_id(0)

    @pl.when(step < per)
    def _():
        one_ref[...] = block

    @pl.when(step >= per)
    def _():
        two_ref[...] = block


def first_query_kernel(per, cols, h_ref, gain_ref, w_ref, a_ref, one_ref, two_ref, hg_ref, pack_ref):
    @pl.when(pl.program_id(0) == 0)
    def _():
        wide = h_ref[...].astype(F32)
        hg_ref[...] = (wide * gain_ref[...]).astype(BF)
        count = wide.shape[0]
        sums = jnp.sum(wide * wide, axis=-1, keepdims=True)
        rows = []
        for i in range(count // LANES):
            block = jnp.broadcast_to(sums[i * LANES : (i + 1) * LANES], (LANES, LANES))
            rows.append(block.T[0:1])
        rows.append(jnp.zeros((8 - len(rows), LANES), F32))
        pack_ref[count:] = split_terms(jnp.concatenate(rows, axis=0))
        pack_ref[:count] = dot(hg_ref[...], a_ref[...].astype(BF)).astype(BF)

    store_block(per, dot(hg_ref[...], w_ref[...]).astype(BF), one_ref, two_ref)


def second_query_kernel(per, cols, hg_ref, w_ref, pos_ref, after_ref, one_ref, two_ref, pos_out):
    @pl.when(pl.program_id(0) == 0)
    def _():
        pos_out[...] = pos_ref[...].astype(F32)

    store_block(per, dot(hg_ref[...], w_ref[...]).astype(BF), one_ref, two_ref)


def merge_kernel(a_ref, b_ref, out_ref):
    count = a_ref.shape[0] - EXTRA
    out_ref[:count] = (a_ref[:count].astype(F32) + b_ref[:count].astype(F32)).astype(BF)
    out_ref[count:] = split_terms(join_terms(a_ref, count) + join_terms(b_ref, count))


def grad_kernel(sizes, at, x_ref, v_ref, s_ref, r_ref, *rest):
    n_dp, n_roll = sizes
    outs, (ga, gb) = rest[:-2], rest[-2:]
    count, width = x_ref.shape
    low = (s_ref[...].astype(F32) + r_ref[...].astype(F32)).astype(BF)
    ga[...] = SCALE * dot(x_ref[...], low[count:], ((0,), (0,)))
    turned = SCALE * dot(low[:count], v_ref[...], ((0,), (0,)))
    for j in range(width // LANES):
        gb[j * LANES : (j + 1) * LANES] = turned[:, j * LANES : (j + 1) * LANES]
    size = width // (n_dp * n_roll)
    for kx in range(n_dp):
        for kz in range(n_roll):
            start = ((at[1] ^ kx) * n_roll + (at[2] ^ kz)) * size
            rows = pl.ds(pl.multiple_of(start, size), size)
            out = outs[kx * n_roll + kz]
            out[0] = ga[rows].astype(out.dtype)
            out[1] = gb[rows].astype(out.dtype)


def far_kernel(a_ref, b_ref, after_ref, out_ref):
    out_ref[...] = (a_ref[...].astype(F32) + b_ref[...].astype(F32)).astype(BF)


def low_kernel(sizes, at, hg_ref, *rest):
    n_dp, n_roll = sizes
    pieces, (pack_ref, ga_ref, gb_ref) = rest[:-3], rest[-3:]
    size = pieces[0].shape[1]
    for kx in range(n_dp):
        for kz in range(n_roll):
            start = ((at[1] ^ kx) * n_roll + (at[2] ^ kz)) * size
            rows = pl.ds(pl.multiple_of(start, size), size)
            piece = pieces[kx * n_roll + kz]
            ga_ref[rows] = piece[0]
            gb_ref[rows] = piece[1]
    count = hg_ref.shape[0]
    pack_ref[:count] = dot(hg_ref[...], ga_ref[...]).astype(BF)
    ga = ga_ref[...].astype(F32)
    gb = gb_ref[...].astype(F32)
    total = jnp.sum(ga * ga + gb * gb)
    pack_ref[count:] = split_terms(jnp.broadcast_to(total, (8, LANES)))


def base_kernel(p_ref, near_ref, far_ref, a_ref, b_ref, after_ref, base_ref, low_ref, scale_ref):
    step = pl.program_id(0)
    count = a_ref.shape[0] - EXTRA
    sums = join_terms(a_ref, count) + join_terms(b_ref, count)
    scale = lax.rsqrt(sums / D + EPS)
    row = scale[0:1]
    for i in range(1, count // LANES):
        row = jnp.where(step == i, scale[i : i + 1], row)
    block = jnp.broadcast_to(row, (LANES, LANES)).T
    rows = pl.ds(pl.multiple_of(step * LANES, LANES), LANES)
    scale_ref[...] = block
    low_ref[...] = (a_ref[rows].astype(F32) + b_ref[rows].astype(F32)) * block
    for j in range(p_ref.shape[1] // LANES):
        at = slice(j * LANES, (j + 1) * LANES)
        total = p_ref[:, at].astype(F32) + near_ref[:, at].astype(F32) + far_ref[:, at].astype(F32)
        base_ref[:, at] = total * block


def final_kernel(
    base_ref, low_ref, scale_ref, s_ref, r_ref, ga_ref, gb_ref, a_ref, b_ref, cos_ref, sin_ref,
    new_a, new_b, out_ref, half_b,
):
    step = pl.program_id(0)
    count = s_ref.shape[0] - EXTRA
    total = join_terms(s_ref, count) + join_terms(r_ref, count)
    rate = (LEARN * lax.rsqrt(total + NORM_EPS))[0:1]

    @pl.when(step == 0)
    def _():
        new_a[...] = a_ref[...] - rate * ga_ref[...].astype(F32)
        for j in range(b_ref.shape[1] // LANES):
            at = slice(j * LANES, (j + 1) * LANES)
            fresh = b_ref[:, at] - rate * gb_ref[at].astype(F32)
            new_b[:, at] = fresh
            half_b[:, at] = fresh.astype(BF)

    rows = pl.ds(pl.multiple_of(step * LANES, LANES), LANES)
    low = s_ref[rows].astype(F32) + r_ref[rows].astype(F32)
    mix = (low_ref[...] - rate * (low * scale_ref[...])) * SCALE
    update = dot(mix.astype(BF), half_b[...])
    cos, sin = cos_ref[...], sin_ref[...]
    for j in range(base_ref.shape[1] // HEAD):
        at = slice(j * HEAD, (j + 1) * HEAD)
        query = base_ref[:, at] + update[:, at]
        other = pltpu.roll(query, HEAD // 2, 1)
        out_ref[:, at] = (query * cos + other * sin).astype(BF)


def turn_tables(places, steps):
    half = HEAD // 2
    freq = 10000.0 ** (-jnp.arange(half, dtype=F32) / half)
    cos, sin = [], []
    for step in range(steps):
        angle = (places + float(step))[:, None] * freq[None, :]
        c, s = jnp.cos(angle), jnp.sin(angle)
        cos.append(jnp.concatenate([c, c], axis=-1))
        sin.append(jnp.concatenate([-s, s], axis=-1))
    return jnp.concatenate(cos), jnp.concatenate(sin)


def build(n_dp, n_roll, n_tp):
    def on_device(
        train_inputs, train_cotangent, factor_a, factor_b, base_weight, incoming, norm_gain, positions
    ):
        steps, rows, width = incoming.shape
        tokens = train_inputs.shape[0]
        rank = factor_a.shape[1]
        count = steps * rows
        full = base_weight.shape[1]
        tp, dp, roll = (lax.axis_index(a) for a in ("tp", "dp", "roll"))
        at = jnp.stack([tp, dp, roll]).astype(jnp.int32)

        part = pl.pallas_call(
            rank_kernel,
            out_shape=shape((2 * tokens, rank), BF),
            in_specs=[VMEM] * 4,
            out_specs=VMEM,
            compiler_params=PARAMS,
            name="rank",
        )(train_inputs, train_cotangent, factor_a, factor_b)
        part_got = swap(part, "tp", n_tp, 1)

        cut = 512
        per = width // cut
        whole = lambda *dims: pl.BlockSpec(dims, lambda i, c: (0,) * len(dims))

        def query_call(kernel, top, ins, in_specs, outs, out_specs, name):
            w_spec = pl.BlockSpec(
                (width, cut), lambda i, c: (0, (c[0] ^ (top - i // per)) * per + i % per)
            )
            one_spec = pl.BlockSpec((count, cut), lambda i, c: (0, jnp.minimum(i, per - 1)))
            two_spec = pl.BlockSpec((count, cut), lambda i, c: (0, jnp.maximum(i - per, 0)))
            return pl.pallas_call(
                functools.partial(kernel, per),
                out_shape=[shape((count, width), BF)] * 2 + outs,
                grid_spec=pltpu.PrefetchScalarGridSpec(
                    num_scalar_prefetch=1,
                    grid=(2 * per,),
                    in_specs=[w_spec if s is None else s for s in in_specs],
                    out_specs=[one_spec, two_spec] + out_specs,
                ),
                compiler_params=PARAMS,
                name=name,
            )(at, *ins)

        diag, distant, gained, low_pack = query_call(
            first_query_kernel,
            3,
            (incoming.reshape(count, width), norm_gain[None, :], base_weight, factor_a),
            [whole(count, width), whole(1, width), None, whole(width, rank)],
            [shape((count, width), BF), shape((count + EXTRA, rank), BF)],
            [whole(count, width), whole(count + EXTRA, rank)],
            "query_first",
        )
        diag_got = swap(diag, "tp", n_tp, 1)
        part_sum = (part.astype(F32) + part_got.astype(F32)).astype(BF)
        part_far = swap(part_sum, "tp", n_tp, 2)
        beside, close, places = query_call(
            second_query_kernel,
            1,
            (gained, base_weight, positions.reshape(-1, LANES), part_sum),
            [whole(count, width), None, whole(rows // LANES, LANES), ANY],
            [shape((rows // LANES, LANES), F32)],
            [whole(rows // LANES, LANES)],
            "query_second",
        )
        close_got = swap(beside, "tp", n_tp, 1)
        merge = pl.pallas_call(
            merge_kernel,
            out_shape=shape((count + EXTRA, rank), BF),
            in_specs=[VMEM] * 2,
            out_specs=VMEM,
            compiler_params=PARAMS,
            name="merge",
        )
        low_sum = merge(low_pack, swap(low_pack, "tp", n_tp, 1))
        low_far = swap(low_sum, "tp", n_tp, 2)

        size = width // (n_dp * n_roll)
        piece = (2, size, rank)
        grads = pl.pallas_call(
            functools.partial(grad_kernel, (n_dp, n_roll)),
            out_shape=[shape(piece, F32)] * n_roll + [shape(piece, BF)] * ((n_dp - 1) * n_roll),
            in_specs=[SMEM] + [VMEM] * 4,
            out_specs=[VMEM] * (n_dp * n_roll),
            scratch_shapes=[pltpu.VMEM((width, rank), F32), pltpu.VMEM((width, rank), F32)],
            compiler_params=PARAMS,
            name="grads",
        )(at, train_inputs, train_cotangent, part_sum, part_far)
        sums = list(grads[:n_roll])
        for kz in reversed(range(n_roll)):
            for kx in range(1, n_dp):
                sums[kz] = sums[kz] + swap(grads[kx * n_roll + kz], "dp", n_dp, kx).astype(F32)
        far = pl.pallas_call(
            far_kernel,
            out_shape=shape((count, width), BF),
            grid=(4,),
            in_specs=[pl.BlockSpec((count // 4, width), lambda i: (i, 0)),
                      pl.BlockSpec((count // 4, width), lambda i: (i, 0)), ANY],
            out_specs=pl.BlockSpec((count // 4, width), lambda i: (i, 0)),
            compiler_params=PARAMS,
            name="far",
        )(distant, diag_got, grads[-1])
        far_got = swap(far, "tp", n_tp, 2)

        chunk = sums[0]
        for kz in reversed(range(1, n_roll)):
            chunk = chunk + swap(sums[kz].astype(BF), "roll", n_roll, kz).astype(F32)
        chunk = chunk.astype(BF)
        pieces = [chunk] + [swap(chunk, "roll", n_roll, kz) for kz in range(1, n_roll)]
        for kx in range(1, n_dp):
            pieces += [swap(pieces[kz], "dp", n_dp, kx) for kz in range(n_roll)]
        step_pack, grad_a, grad_b = pl.pallas_call(
            functools.partial(low_kernel, (n_dp, n_roll)),
            out_shape=[shape((count + EXTRA, rank), BF), shape((width, rank), BF), shape((width, rank), BF)],
            in_specs=[SMEM] + [VMEM] * (1 + len(pieces)),
            out_specs=[VMEM] * 3,
            compiler_params=PARAMS,
            name="low_rank",
        )(at, gained, *pieces)
        step_sum = merge(step_pack, swap(step_pack, "tp", n_tp, 1))
        step_far = swap(step_sum, "tp", n_tp, 2)

        tall = lambda cols: pl.BlockSpec((LANES, cols), lambda i: (i, 0))
        fixed = lambda *dims: pl.BlockSpec(dims, lambda i: (0,) * len(dims))
        base, low, scale = pl.pallas_call(
            base_kernel,
            out_shape=[shape((count, width), F32), shape((count, rank), F32), shape((count, LANES), F32)],
            grid=(count // LANES,),
            in_specs=[tall(width), tall(width), tall(width),
                      fixed(count + EXTRA, rank), fixed(count + EXTRA, rank), ANY],
            out_specs=[tall(width), tall(rank), tall(LANES)],
            compiler_params=PARAMS,
            name="base",
        )(close, close_got, far_got, low_sum, low_far, step_pack)
        cos, sin = turn_tables(places.reshape(rows), steps)
        new_a, new_b, queries = pl.pallas_call(
            final_kernel,
            out_shape=[shape((width, rank), F32), shape((rank, width), F32), shape((count, width), BF)],
            grid=(count // LANES,),
            in_specs=[tall(width), tall(rank), tall(LANES), fixed(count + EXTRA, rank), fixed(count + EXTRA, rank),
                      fixed(width, rank), fixed(width, rank), fixed(width, rank), fixed(rank, width),
                      tall(LANES), tall(LANES)],
            out_specs=[fixed(width, rank), fixed(rank, width), tall(width)],
            scratch_shapes=[pltpu.VMEM((rank, width), BF)],
            compiler_params=PARAMS,
            name="final",
        )(base, low, scale, step_sum, step_far, grad_a, grad_b, factor_a, factor_b, cos, sin)
        return new_a, new_b, queries.reshape(steps, rows, width)

    return on_device


def solution(mesh):
    n_dp, n_roll, n_tp = (mesh.shape[a] for a in ("dp", "roll", "tp"))
    return jax.shard_map(
        build(n_dp, n_roll, n_tp),
        mesh=mesh,
        in_specs=(
            P(("dp", "roll"), "tp"),
            P(("dp", "roll"), "tp"),
            P("tp", None),
            P(None, "tp"),
            P("tp", None),
            P(None, ("dp", "roll"), "tp"),
            P("tp"),
            P(("dp", "roll")),
        ),
        out_specs=(P("tp", None), P(None, "tp"), P(None, ("dp", "roll"), "tp")),
        check_vma=False,
    )
```

```python
import functools

import jax
import jax.numpy as jnp
from jax import lax
from jax.experimental import pallas as pl
from jax.experimental.pallas import tpu as pltpu
from jax.sharding import PartitionSpec as P

D = 4096
HEAD = 128
SCALE = 2.0
LEARN = 3.0
EPS = 1e-05
NORM_EPS = 1e-06
LANES = 128
EXTRA = 32

BF = jnp.bfloat16
F32 = jnp.float32
VMEM = pl.BlockSpec(memory_space=pltpu.VMEM)
SMEM = pl.BlockSpec(memory_space=pltpu.SMEM)
ANY = pl.BlockSpec(memory_space=pl.ANY)
HBM = pl.BlockSpec(memory_space=pltpu.HBM)


def shape(dims, dtype):
    return jax.ShapeDtypeStruct(dims, dtype)


def dot(a, b, dims=((1,), (0,))):
    return lax.dot_general(a, b, (dims, ((), ())), preferred_element_type=F32)


def swap(x, axis, n, k):
    return lax.ppermute(x, axis, [(i, i ^ k) for i in range(n)])


def split_terms(values):
    high = values.astype(BF)
    rest = values - high.astype(F32)
    middle = rest.astype(BF)
    last = (rest - middle.astype(F32)).astype(BF)
    return jnp.concatenate([high, middle, last, jnp.zeros_like(last)], axis=0)


def join_terms(terms):
    x = terms.astype(F32)
    return (x[0:8] + x[8:16]) + x[16:24]


def fetch(sources, targets, sems):
    copies = [pltpu.make_async_copy(s, t, sems.at[i]) for i, (s, t) in enumerate(zip(sources, targets))]
    for copy in copies:
        copy.start()
    return copies


def place(at, sizes, kx, kz, size):
    start = ((at[1] ^ kx) * sizes[1] + (at[2] ^ kz)) * size
    return pl.ds(pl.multiple_of(start, size), size)


def blocks_of(count):
    return [slice(i, i + LANES) for i in range(0, count, LANES)]


def rank_kernel(x_hbm, v_hbm, a_hbm, b_hbm, out_ref, x_ref, v_ref, a_ref, b_ref, sems):
    copies = fetch((x_hbm, a_hbm, v_hbm, b_hbm), (x_ref, a_ref, v_ref, b_ref), sems)
    count = x_ref.shape[0]
    copies[0].wait()
    copies[1].wait()
    out_ref[:count] = dot(x_ref[...], a_ref[...].astype(BF)).astype(BF)
    copies[2].wait()
    copies[3].wait()
    out_ref[count:] = dot(v_ref[...], b_ref[...].astype(BF), ((1,), (1,))).astype(BF)


def prep_kernel(h_hbm, gain_hbm, a_hbm, hg_ref, pack_ref, h_ref, gain_ref, a_ref, sems):
    count = h_ref.shape[0]
    blocks = blocks_of(count)
    copies = fetch(
        [gain_hbm] + [h_hbm.at[b] for b in blocks] + [a_hbm],
        [gain_ref] + [h_ref.at[b] for b in blocks] + [a_ref],
        sems,
    )
    copies[0].wait()
    rows = []
    for i, b in enumerate(blocks):
        copies[1 + i].wait()
        wide = h_ref[b].astype(F32)
        hg_ref[b] = (wide * gain_ref[...]).astype(BF)
        sums = jnp.sum(wide * wide, axis=-1, keepdims=True)
        rows.append(jnp.broadcast_to(sums, (LANES, LANES)).T[0:1])
    if len(rows) < 8:
        rows.append(jnp.zeros((8 - len(rows), LANES), F32))
    pack_ref[count:] = split_terms(jnp.concatenate(rows, axis=0))
    copies[-1].wait()
    pack_ref[:count] = dot(hg_ref[...], a_ref[...].astype(BF)).astype(BF)


def query_kernel(peers, cut, at, hg_ref, w_hbm, pack_ref, after_ref, one_ref, two_ref, w_ref, sems):
    count, width = hg_ref.shape
    per = width // cut
    sources = []
    for i in range(2 * per):
        start = (at[0] ^ peers[i // per]) * width + (i % per) * cut
        sources.append(w_hbm.at[:, pl.ds(pl.multiple_of(start, cut), cut)])
    copies = fetch(sources, [w_ref.at[i] for i in range(2 * per)], sems)
    if one_ref.shape[0] > count:
        one_ref[count:, :width] = jnp.zeros((EXTRA, width), BF)
        one_ref[:, width:] = pack_ref[...]
    for i in range(2 * per):
        copies[i].wait()
        out = one_ref if i < per else two_ref
        out[:count, (i % per) * cut : (i % per + 1) * cut] = dot(hg_ref[...], w_ref[i]).astype(BF)


def far_kernel(mine_ref, diag_ref, got_ref, after_ref, out_ref):
    count, width = mine_ref.shape
    out_ref[:count, :width] = (mine_ref[...].astype(F32) + got_ref[:count, :width].astype(F32)).astype(BF)
    out_ref[count:, :width] = jnp.zeros((EXTRA, width), BF)
    out_ref[:count, width:] = (diag_ref[:count, width:].astype(F32) + got_ref[:count, width:].astype(F32)).astype(BF)
    out_ref[count:, width:] = split_terms(join_terms(diag_ref[count:, width:]) + join_terms(got_ref[count:, width:]))


def merge_kernel(a_ref, b_ref, out_ref):
    count = a_ref.shape[0] - EXTRA
    out_ref[:count] = (a_ref[:count].astype(F32) + b_ref[:count].astype(F32)).astype(BF)
    out_ref[count:] = split_terms(join_terms(a_ref[count:]) + join_terms(b_ref[count:]))


def grad_kernel(sizes, at, x_ref, v_ref, s_ref, r_ref, *rest):
    outs, (ga, gb) = rest[:-2], rest[-2:]
    count, width = x_ref.shape
    low = (s_ref[...].astype(F32) + r_ref[...].astype(F32)).astype(BF)
    ga[...] = SCALE * dot(x_ref[...], low[count:], ((0,), (0,)))
    turned = SCALE * dot(low[:count], v_ref[...], ((0,), (0,)))
    for b in blocks_of(width):
        gb[b] = turned[:, b]
    size = width // (sizes[0] * sizes[1])
    for kx, out in enumerate(outs):
        for kz in range(sizes[1]):
            rows = place(at, sizes, kx, kz, size)
            out[kz, 0] = ga[rows].astype(out.dtype)
            out[kz, 1] = gb[rows].astype(out.dtype)


def cross_kernel(n_dp, own_ref, *rest):
    got, (pos_ref, after_ref, keep_ref), sends = rest[: n_dp - 1], rest[n_dp - 1 : n_dp + 2], rest[n_dp + 2 : -1]
    rest[-1][...] = pos_ref[...].astype(F32)
    for kz, out in enumerate((keep_ref,) + sends):
        total = own_ref[kz]
        for g in got:
            total = total + g[kz].astype(F32)
        out[...] = total.astype(out.dtype)


def chunk_kernel(keep_ref, *rest):
    got, (a_ref, b_ref) = rest[:-2], rest[-2:]
    total = keep_ref[...]
    for g in got:
        total = total + g[...].astype(F32)
    size = total.shape[1]
    a_ref[:size] = total[0].astype(BF)
    b_ref[...] = total[1].astype(BF)
    squares = total[0] * total[0] + total[1] * total[1]
    a_ref[size:] = split_terms(jnp.broadcast_to(jnp.sum(squares), (8, LANES)))


def hold_kernel(x_ref, after_ref, out_ref):
    out_ref[...] = x_ref[...]


def stack_kernel(*refs):
    for k, ref in enumerate(refs[:-1]):
        refs[-1][k] = ref[...]


def low_kernel(sizes, at, hg_ref, *rest):
    pieces, (pack_ref, ga_ref, sums_ref) = rest[:-3], rest[-3:]
    size = pieces[0].shape[0] - EXTRA
    for kx in range(sizes[0]):
        for kz in range(sizes[1]):
            piece = pieces[kx * sizes[1] + kz]
            ga_ref[place(at, sizes, kx, kz, size)] = piece[:size]
            sums_ref[place(at, sizes, kx, kz, 8)] = join_terms(piece[size:])
    count = hg_ref.shape[0]
    pack_ref[:count] = dot(hg_ref[...], ga_ref[...]).astype(BF)
    total = sums_ref[0:8]
    for i in range(1, len(pieces)):
        total = total + sums_ref[8 * i : 8 * i + 8]
    pack_ref[count:] = split_terms(total)


def base_kernel(mine_ref, near_ref, far_ref, far_got, after_ref, base_ref, low_ref, scale_ref):
    count, width = mine_ref.shape
    sums = join_terms(far_ref[count:, width:]) + join_terms(far_got[count:, width:])
    scale = lax.rsqrt(sums / D + EPS)
    for i, b in enumerate(blocks_of(count)):
        block = jnp.broadcast_to(scale[i : i + 1], (LANES, LANES)).T
        scale_ref[b] = block
        low_ref[b] = (far_ref[b, width:].astype(F32) + far_got[b, width:].astype(F32)) * block
        for c in blocks_of(width):
            total = mine_ref[b, c].astype(F32) + near_ref[b, c].astype(F32) + far_got[b, c].astype(F32)
            base_ref[b, c] = total * block


def final_kernel(sizes, at, base_ref, low_ref, scale_ref, s_ref, r_ref, ga_ref, a_ref, b_ref, cos_ref, sin_ref, *rest):
    parts, (a_hbm, b_hbm, q_hbm, gb, new_a, new_b, half_b, out, sems) = rest[:-9], rest[-9:]
    count, width = base_ref.shape
    total = join_terms(s_ref[count:]) + join_terms(r_ref[count:])
    rate = (LEARN * lax.rsqrt(total + NORM_EPS))[0:1]
    size = parts[0].shape[1]
    for kx, part in enumerate(parts):
        for kz in range(sizes[1]):
            gb[place(at, sizes, kx, kz, size)] = part[kz]
    for c in blocks_of(width):
        fresh = b_ref[:, c] - rate * gb[c].astype(F32)
        new_b[:, c] = fresh
        half_b[:, c] = fresh.astype(BF)
    copies = [pltpu.make_async_copy(new_b, b_hbm, sems.at[0])]
    copies[-1].start()
    new_a[...] = a_ref[...] - rate * ga_ref[...].astype(F32)
    copies.append(pltpu.make_async_copy(new_a, a_hbm, sems.at[1]))
    copies[-1].start()
    for i, b in enumerate(blocks_of(count)):
        low = s_ref[b].astype(F32) + r_ref[b].astype(F32)
        mix = (low_ref[b] - rate * (low * scale_ref[b])) * SCALE
        update = dot(mix.astype(BF), half_b[...])
        cos, sin = cos_ref[b], sin_ref[b]
        for c in blocks_of(width):
            query = base_ref[b, c] + update[:, c]
            other = pltpu.roll(query, HEAD // 2, 1)
            out[b, c] = (query * cos + other * sin).astype(BF)
        copies.append(pltpu.make_async_copy(out.at[b], q_hbm.at[b], sems.at[2 + i]))
        copies[-1].start()
    for copy in copies:
        copy.wait()


def call(kernel, outs, in_specs, args, name, scratch=(), out_specs=None, limit=32):
    return pl.pallas_call(
        kernel,
        out_shape=outs,
        in_specs=in_specs,
        out_specs=out_specs if out_specs is not None else jax.tree.map(lambda _: VMEM, outs),
        scratch_shapes=list(scratch),
        compiler_params=pltpu.CompilerParams(vmem_limit_bytes=int(limit * 1024 * 1024)),
        name=name,
    )(*args)


def turn_tables(places, steps):
    half = HEAD // 2
    freq = 10000.0 ** (-jnp.arange(half, dtype=F32) / half)
    cos, sin = [], []
    for step in range(steps):
        angle = (places + float(step))[:, None] * freq[None, :]
        c, s = jnp.cos(angle), jnp.sin(angle)
        cos.append(jnp.concatenate([c, c], axis=-1))
        sin.append(jnp.concatenate([-s, s], axis=-1))
    return jnp.concatenate(cos), jnp.concatenate(sin)


def build(n_dp, n_roll, n_tp):
    sizes = (n_dp, n_roll)

    def on_device(
        train_inputs, train_cotangent, factor_a, factor_b, base_weight, incoming, norm_gain, positions
    ):
        steps, rows, width = incoming.shape
        tokens = train_inputs.shape[0]
        rank = factor_a.shape[1]
        count = steps * rows
        tp, dp, roll = (lax.axis_index(a) for a in ("tp", "dp", "roll"))
        at = jnp.stack([tp, dp, roll]).astype(jnp.int32)
        dma = lambda n: pltpu.SemaphoreType.DMA((n,))

        part = call(
            rank_kernel,
            shape((2 * tokens, rank), BF),
            [HBM] * 4,
            (train_inputs, train_cotangent, factor_a, factor_b),
            "rank",
            [pltpu.VMEM(train_inputs.shape, BF), pltpu.VMEM(train_inputs.shape, BF),
             pltpu.VMEM(factor_a.shape, F32), pltpu.VMEM(factor_b.shape, F32), dma(4)],
            limit=63.5,
        )
        part_got = swap(part, "tp", n_tp, 1)
        gained, pack = call(
            prep_kernel,
            [shape((count, width), BF), shape((count + EXTRA, rank), BF)],
            [HBM] * 3,
            (incoming.reshape(count, width), norm_gain[None, :], factor_a),
            "prep",
            [pltpu.VMEM((count, width), BF), pltpu.VMEM((1, width), F32), pltpu.VMEM(factor_a.shape, F32),
             dma(2 + count // LANES)],
            limit=60,
        )
        part_sum = (part.astype(F32) + part_got.astype(F32)).astype(BF)
        part_far = swap(part_sum, "tp", n_tp, 2)

        cut = 512
        wide = shape((count + EXTRA, width + rank), BF)
        tall = shape((count, width), BF)

        def query(peers, outs, after, name):
            return call(
                functools.partial(query_kernel, peers, cut),
                outs,
                [SMEM, VMEM, HBM, VMEM, ANY],
                (at, gained, base_weight, pack, after),
                name,
                [pltpu.VMEM((2 * width // cut, width, cut), BF), dma(2 * width // cut)],
                limit=56,
            )

        diag, distant = query((3, 2), [wide, tall], part_sum, "query_first")
        diag_got = swap(diag, "tp", n_tp, 1)

        size = width // (n_dp * n_roll)
        grads = call(
            functools.partial(grad_kernel, sizes),
            [shape((n_roll, 2, size, rank), F32)] + [shape((n_roll, 2, size, rank), BF)] * (n_dp - 1),
            [SMEM] + [VMEM] * 4,
            (at, train_inputs, train_cotangent, part_sum, part_far),
            "grads",
            [pltpu.VMEM((width, rank), F32), pltpu.VMEM((width, rank), F32)],
        )
        grads_got = [swap(grads[kx], "dp", n_dp, kx) for kx in range(1, n_dp)]
        far = call(far_kernel, wide, [VMEM] * 3 + [ANY], (distant, diag, diag_got, grads[-1]), "far")
        far_got = swap(far, "tp", n_tp, 2)
        beside, close = query((1, 0), [tall, tall], far, "query_second")
        beside_got = swap(beside, "tp", n_tp, 1)

        pos = positions.reshape(-1, LANES)
        crossed = call(
            functools.partial(cross_kernel, n_dp),
            [shape((2, size, rank), F32)] + [shape((2, size, rank), BF)] * (n_roll - 1) + [shape(pos.shape, F32)],
            [VMEM] * (n_dp + 1) + [ANY],
            (grads[0], *grads_got, pos, close),
            "cross",
        )
        places = crossed[-1].reshape(rows)
        chunk_a, chunk_b = call(
            chunk_kernel,
            [shape((size + EXTRA, rank), BF), shape((size, rank), BF)],
            [VMEM] * n_roll,
            (crossed[0], *[swap(crossed[kz], "roll", n_roll, kz) for kz in range(1, n_roll)]),
            "chunk",
        )
        pieces = [chunk_a] + [swap(chunk_a, "roll", n_roll, kz) for kz in range(1, n_roll)]
        chunk_b = call(hold_kernel, shape((size, rank), BF), [VMEM, ANY], (chunk_b, pieces[-1]), "hold")
        for kx in range(1, n_dp):
            pieces += [swap(pieces[kz], "dp", n_dp, kx) for kz in range(n_roll)]
        step_pack, grad_a = call(
            functools.partial(low_kernel, sizes),
            [shape((count + EXTRA, rank), BF), shape((width, rank), BF)],
            [SMEM] + [VMEM] * (1 + len(pieces)),
            (at, gained, *pieces),
            "low_rank",
            [pltpu.VMEM((8 * len(pieces), LANES), F32)],
        )
        step_got = swap(step_pack, "tp", n_tp, 1)
        parts_b = [chunk_b] + [swap(chunk_b, "roll", n_roll, kz) for kz in range(1, n_roll)]
        stack_b = call(stack_kernel, shape((n_roll, size, rank), BF), [VMEM] * n_roll, parts_b, "stack")
        grad_b = [stack_b] + [swap(stack_b, "dp", n_dp, kx) for kx in range(1, n_dp)]
        step_sum = call(merge_kernel, shape((count + EXTRA, rank), BF), [VMEM] * 2, (step_pack, step_got), "merge")
        step_far = swap(step_sum, "tp", n_tp, 2)
        base, low, scale = call(
            base_kernel,
            [shape((count, width), F32), shape((count, rank), F32), shape((count, LANES), F32)],
            [VMEM] * 4 + [ANY],
            (close, beside_got, far, far_got, step_pack),
            "base",
        )
        cos, sin = turn_tables(places, steps)
        new_a, new_b, queries = call(
            functools.partial(final_kernel, sizes),
            [shape((width, rank), F32), shape((rank, width), F32), tall],
            [SMEM] + [VMEM] * (10 + n_dp),
            (at, base, low, scale, step_sum, step_far, grad_a, factor_a, factor_b, cos, sin, *grad_b),
            "final",
            [pltpu.VMEM((width, rank), BF), pltpu.VMEM((width, rank), F32), pltpu.VMEM((rank, width), F32),
             pltpu.VMEM((rank, width), BF), pltpu.VMEM((count, width), BF), dma(2 + count // LANES)],
            [HBM] * 3,
        )
        return new_a, new_b, queries.reshape(steps, rows, width)

    return on_device


def solution(mesh):
    n_dp, n_roll, n_tp = (mesh.shape[a] for a in ("dp", "roll", "tp"))
    return jax.shard_map(
        build(n_dp, n_roll, n_tp),
        mesh=mesh,
        in_specs=(
            P(("dp", "roll"), "tp"),
            P(("dp", "roll"), "tp"),
            P("tp", None),
            P(None, "tp"),
            P("tp", None),
            P(None, ("dp", "roll"), "tp"),
            P("tp"),
            P(("dp", "roll")),
        ),
        out_specs=(P("tp", None), P(None, "tp"), P(None, ("dp", "roll"), "tp")),
        check_vma=False,
    )
```

```python
import functools

import jax
import jax.numpy as jnp
from jax import lax
from jax.experimental import pallas as pl
from jax.experimental.pallas import tpu as pltpu
from jax.sharding import PartitionSpec as P

D = 4096
HEAD = 128
SCALE = 2.0
LEARN = 3.0
EPS = 1e-05
NORM_EPS = 1e-06
LANES = 128
EXTRA = 32

BF = jnp.bfloat16
F32 = jnp.float32
VMEM = pl.BlockSpec(memory_space=pltpu.VMEM)
SMEM = pl.BlockSpec(memory_space=pltpu.SMEM)
ANY = pl.BlockSpec(memory_space=pl.ANY)
HBM = pl.BlockSpec(memory_space=pltpu.HBM)


def shape(dims, dtype):
    return jax.ShapeDtypeStruct(dims, dtype)


def dot(a, b, dims=((1,), (0,))):
    return lax.dot_general(a, b, (dims, ((), ())), preferred_element_type=F32)


def swap(x, axis, n, k):
    return lax.ppermute(x, axis, [(i, i ^ k) for i in range(n)])


def split_terms(values):
    high = values.astype(BF)
    rest = values - high.astype(F32)
    middle = rest.astype(BF)
    last = (rest - middle.astype(F32)).astype(BF)
    return jnp.concatenate([high, middle, last, jnp.zeros_like(last)], axis=0)


def join_terms(terms):
    x = terms.astype(F32)
    return (x[0:8] + x[8:16]) + x[16:24]


def fetch(sources, targets, sems):
    copies = [pltpu.make_async_copy(s, t, sems.at[i]) for i, (s, t) in enumerate(zip(sources, targets))]
    for copy in copies:
        copy.start()
    return copies


def blocks_of(count):
    return [slice(i, i + LANES) for i in range(0, count, LANES)]


def rank_kernel(x_hbm, v_hbm, a_hbm, b_hbm, out_ref, x_ref, v_ref, a_ref, b_ref, sems):
    copies = fetch((x_hbm, a_hbm, v_hbm, b_hbm), (x_ref, a_ref, v_ref, b_ref), sems)
    count = x_ref.shape[0]
    copies[0].wait()
    copies[1].wait()
    out_ref[:count] = dot(x_ref[...], a_ref[...].astype(BF)).astype(BF)
    copies[2].wait()
    copies[3].wait()
    out_ref[count:] = dot(v_ref[...], b_ref[...].astype(BF), ((1,), (1,))).astype(BF)


def weight_blocks(at, peers, w_hbm, w_ref):
    _, width, cut = w_ref.shape
    sources = []
    for peer in peers:
        for i in range(width // cut):
            start = (at[0] ^ peer) * width + i * cut
            sources.append(w_hbm.at[:, pl.ds(pl.multiple_of(start, cut), cut)])
    return sources, [w_ref.at[i] for i in range(len(sources))]


def prep_kernel(at, h_hbm, gain_hbm, a_hbm, w_hbm, after_ref, hg_ref, wide_ref, h_ref, gain_ref, a_ref, w_ref, sems):
    count, width = h_ref.shape
    blocks = blocks_of(count)
    sources, targets = weight_blocks(at, (3,), w_hbm, w_ref)
    copies = fetch(
        [gain_hbm] + [h_hbm.at[b] for b in blocks] + [a_hbm] + sources,
        [gain_ref] + [h_ref.at[b] for b in blocks] + [a_ref] + targets,
        sems,
    )
    copies[0].wait()
    rows = []
    for i, b in enumerate(blocks):
        copies[1 + i].wait()
        wide = h_ref[b].astype(F32)
        hg_ref[b] = (wide * gain_ref[...]).astype(BF)
        sums = jnp.sum(wide * wide, axis=-1, keepdims=True)
        rows.append(jnp.broadcast_to(sums, (LANES, LANES)).T[0:1])
    if len(rows) < 8:
        rows.append(jnp.zeros((8 - len(rows), LANES), F32))
    wide_ref[count:, width:] = split_terms(jnp.concatenate(rows, axis=0))
    wide_ref[count:, :width] = jnp.zeros((EXTRA, width), BF)
    copies[1 + len(blocks)].wait()
    wide_ref[:count, width:] = dot(hg_ref[...], a_ref[...].astype(BF)).astype(BF)
    cut = w_ref.shape[2]
    for i in range(width // cut):
        copies[2 + len(blocks) + i].wait()
        wide_ref[:count, i * cut : (i + 1) * cut] = dot(hg_ref[...], w_ref[i]).astype(BF)


def query_kernel(peers, at, hg_ref, w_hbm, pos_ref, after_ref, *rest):
    outs, (pos_out, w_ref, sems) = rest[:-3], rest[-3:]
    _, width, cut = w_ref.shape
    copies = fetch(*weight_blocks(at, peers, w_hbm, w_ref), sems)
    pos_out[...] = pos_ref[...].astype(F32)
    per = width // cut
    for i, copy in enumerate(copies):
        copy.wait()
        outs[i // per][:, i % per * cut : (i % per + 1) * cut] = dot(hg_ref[...], w_ref[i]).astype(BF)


def far_kernel(mine_ref, diag_ref, got_ref, pass_ref, out_ref, pass_out):
    count, width = mine_ref.shape
    out_ref[:count, :width] = (mine_ref[...].astype(F32) + got_ref[:count, :width].astype(F32)).astype(BF)
    out_ref[count:, :width] = jnp.zeros((EXTRA, width), BF)
    out_ref[:count, width:] = (diag_ref[:count, width:].astype(F32) + got_ref[:count, width:].astype(F32)).astype(BF)
    out_ref[count:, width:] = split_terms(join_terms(diag_ref[count:, width:]) + join_terms(got_ref[count:, width:]))


def merge_kernel(a_ref, b_ref, out_ref):
    count = a_ref.shape[0] - EXTRA
    out_ref[:count] = (a_ref[:count].astype(F32) + b_ref[:count].astype(F32)).astype(BF)
    out_ref[count:] = split_terms(join_terms(a_ref[count:]) + join_terms(b_ref[count:]))


def grad_kernel(x_ref, v_ref, s_ref, r_ref, out_ref):
    count, width = x_ref.shape
    parts, _, size, _ = out_ref.shape
    low = (s_ref[...].astype(F32) + r_ref[...].astype(F32)).astype(BF)
    ga = SCALE * dot(x_ref[...], low[count:], ((0,), (0,)))
    gb = SCALE * dot(low[:count], v_ref[...], ((0,), (0,)))
    per = LANES // size
    for i in range(parts):
        out_ref[i, 0] = ga[i * size : (i + 1) * size].astype(BF)
        col, row = i // per * LANES, i % per * size
        out_ref[i, 1] = gb[row : row + size, col : col + LANES].astype(BF)


def chunk_kernel(x_ref, a_ref, b_ref):
    parts, _, size, _ = x_ref.shape
    total = x_ref[0].astype(F32)
    for i in range(1, parts):
        total = total + x_ref[i].astype(F32)
    squares = total[0] * total[0] + total[1] * total[1]
    terms = split_terms(jnp.broadcast_to(jnp.sum(squares), (8, LANES)))
    half = total.astype(BF)
    for i in range(parts):
        a_ref[i, :size] = half[0]
        a_ref[i, size:] = terms
        b_ref[i] = half[1]


def hold_kernel(x_ref, after_ref, out_ref):
    out_ref[...] = x_ref[...]


def low_kernel(hg_ref, x_ref, pack_ref, ga_ref):
    parts, size, _ = x_ref.shape
    size -= EXTRA
    total = join_terms(x_ref[0, size:])
    for i in range(parts):
        ga_ref[i * size : (i + 1) * size] = x_ref[i, :size]
        if i:
            total = total + join_terms(x_ref[i, size:])
    count = hg_ref.shape[0]
    pack_ref[:count] = dot(hg_ref[...], ga_ref[...]).astype(BF)
    pack_ref[count:] = split_terms(total)


def base_kernel(mine_ref, near_ref, far_ref, far_got, after_ref, base_ref, low_ref, scale_ref):
    count, width = mine_ref.shape
    sums = join_terms(far_ref[count:, width:]) + join_terms(far_got[count:, width:])
    scale = lax.rsqrt(sums / D + EPS)
    for i, b in enumerate(blocks_of(count)):
        block = jnp.broadcast_to(scale[i : i + 1], (LANES, LANES)).T
        scale_ref[b] = block
        low_ref[b] = (far_ref[b, width:].astype(F32) + far_got[b, width:].astype(F32)) * block
        for c in blocks_of(width):
            total = mine_ref[b, c].astype(F32) + near_ref[b, c].astype(F32) + far_got[b, c].astype(F32)
            base_ref[b, c] = total * block


def final_kernel(
    base_ref, low_ref, scale_ref, s_ref, r_ref, ga_ref, gb_ref, a_ref, b_ref, cos_ref, sin_ref,
    a_hbm, b_hbm, q_hbm, new_a, new_b, half_b, out, sems,
):
    count, width = base_ref.shape
    total = join_terms(s_ref[count:]) + join_terms(r_ref[count:])
    rate = (LEARN * lax.rsqrt(total + NORM_EPS))[0:1]
    for c in blocks_of(width):
        fresh = b_ref[:, c] - rate * gb_ref[c].astype(F32)
        new_b[:, c] = fresh
        half_b[:, c] = fresh.astype(BF)
    copies = [pltpu.make_async_copy(new_b, b_hbm, sems.at[0])]
    copies[-1].start()
    new_a[...] = a_ref[...] - rate * ga_ref[...].astype(F32)
    copies.append(pltpu.make_async_copy(new_a, a_hbm, sems.at[1]))
    copies[-1].start()
    for i, b in enumerate(blocks_of(count)):
        low = s_ref[b].astype(F32) + r_ref[b].astype(F32)
        mix = (low_ref[b] - rate * (low * scale_ref[b])) * SCALE
        update = dot(mix.astype(BF), half_b[...])
        cos, sin = cos_ref[b], sin_ref[b]
        for c in blocks_of(width):
            query = base_ref[b, c] + update[:, c]
            other = pltpu.roll(query, HEAD // 2, 1)
            out[b, c] = (query * cos + other * sin).astype(BF)
        copies.append(pltpu.make_async_copy(out.at[b], q_hbm.at[b], sems.at[2 + i]))
        copies[-1].start()
    for copy in copies:
        copy.wait()


def keep_hbm(x):
    return pltpu.with_memory_space_constraint(x, pltpu.HBM)


def call(kernel, outs, in_specs, args, name, scratch=(), out_specs=None, limit=32, aliases=None):
    return pl.pallas_call(
        kernel,
        out_shape=outs,
        in_specs=in_specs,
        out_specs=out_specs if out_specs is not None else jax.tree.map(lambda _: VMEM, outs),
        scratch_shapes=list(scratch),
        compiler_params=pltpu.CompilerParams(vmem_limit_bytes=int(limit * 1024 * 1024)),
        input_output_aliases=aliases or {},
        name=name,
    )(*args)


def turn_tables(places, steps):
    half = HEAD // 2
    freq = 10000.0 ** (-jnp.arange(half, dtype=F32) / half)
    cos, sin = [], []
    for step in range(steps):
        angle = (places + float(step))[:, None] * freq[None, :]
        c, s = jnp.cos(angle), jnp.sin(angle)
        cos.append(jnp.concatenate([c, c], axis=-1))
        sin.append(jnp.concatenate([-s, s], axis=-1))
    return jnp.concatenate(cos), jnp.concatenate(sin)


def build(n_dp, n_roll, n_tp):
    n_parts = n_dp * n_roll
    spread = lambda x: lax.all_to_all(x, ("dp", "roll"), 0, 0, tiled=True)

    def on_device(
        train_inputs, train_cotangent, factor_a, factor_b, base_weight, incoming, norm_gain, positions
    ):
        steps, rows, width = incoming.shape
        tokens = train_inputs.shape[0]
        rank = factor_a.shape[1]
        count = steps * rows
        at = lax.axis_index("tp").astype(jnp.int32)[None]
        dma = lambda n: pltpu.SemaphoreType.DMA((n,))

        part = call(
            rank_kernel,
            shape((2 * tokens, rank), BF),
            [HBM] * 4,
            tuple(map(keep_hbm, (train_inputs, train_cotangent, factor_a, factor_b))),
            "rank",
            [pltpu.VMEM(train_inputs.shape, BF), pltpu.VMEM(train_inputs.shape, BF),
             pltpu.VMEM(factor_a.shape, F32), pltpu.VMEM(factor_b.shape, F32), dma(4)],
        )
        part_got = swap(part, "tp", n_tp, 1)
        cut = 512
        wide = shape((count + EXTRA, width + rank), BF)
        tall = shape((count, width), BF)
        pos = positions.reshape(-1, LANES)
        gained, diag = call(
            prep_kernel,
            [tall, wide],
            [SMEM] + [HBM] * 4 + [ANY],
            (at, *map(keep_hbm, (incoming.reshape(count, width), norm_gain[None, :], factor_a, base_weight)), part),
            "prep",
            [pltpu.VMEM((count, width), BF), pltpu.VMEM((1, width), F32), pltpu.VMEM(factor_a.shape, F32),
             pltpu.VMEM((width // cut, width, cut), BF), dma(2 + count // LANES + width // cut)],
        )
        diag_got = swap(diag, "tp", n_tp, 1)
        part_sum = (part.astype(F32) + part_got.astype(F32)).astype(BF)
        part_far = swap(part_sum, "tp", n_tp, 2)

        def query(peers, pos, after, name):
            blocks = len(peers) * width // cut
            return call(
                functools.partial(query_kernel, peers),
                [tall] * len(peers) + [shape(pos.shape, F32)],
                [SMEM, VMEM, HBM, VMEM, ANY],
                (at, gained, keep_hbm(base_weight), pos, after),
                name,
                [pltpu.VMEM((blocks, width, cut), BF), dma(blocks)],
            )

        distant, beside, places = query((2, 1), pos, part_sum, "query_first")
        beside_got = swap(beside, "tp", n_tp, 1)
        cos, sin = turn_tables(places.reshape(rows), steps)
        size = width // n_parts
        grads = call(
            grad_kernel,
            shape((n_parts, 2, size, rank), BF),
            [VMEM] * 4,
            (train_inputs, train_cotangent, part_sum, part_far),
            "grads",
        )
        far, grads = call(
            far_kernel,
            [wide, shape(grads.shape, BF)],
            [VMEM] * 3 + [ANY],
            (distant, diag, diag_got, grads),
            "far",
            out_specs=[VMEM, ANY],
            aliases={3: 1},
        )
        far_got = swap(far, "tp", n_tp, 2)
        chunk_a, chunk_b = call(
            chunk_kernel,
            [shape((n_parts, size + EXTRA, rank), BF), shape((n_parts, size, rank), BF)],
            [VMEM],
            (spread(grads),),
            "chunk",
        )
        pieces = spread(chunk_a)
        step_pack, grad_a = call(
            low_kernel,
            [shape((count + EXTRA, rank), BF), shape((width, rank), BF)],
            [VMEM] * 2,
            (gained, pieces),
            "low_rank",
        )
        step_got = swap(step_pack, "tp", n_tp, 1)
        step_sum = call(merge_kernel, shape((count + EXTRA, rank), BF), [VMEM] * 2, (step_pack, step_got), "merge")
        step_far = swap(step_sum, "tp", n_tp, 2)
        chunk_b = call(hold_kernel, shape(chunk_b.shape, BF), [VMEM, ANY], (chunk_b, step_sum), "hold")
        grad_b = spread(chunk_b).reshape(width, rank)
        close, _ = query((0,), pos, step_sum, "query_second")
        base, low, scale = call(
            base_kernel,
            [shape((count, width), F32), shape((count, rank), F32), shape((count, LANES), F32)],
            [VMEM] * 4 + [ANY],
            (close, beside_got, far, far_got, step_pack),
            "base",
        )
        new_a, new_b, queries = call(
            final_kernel,
            [shape((width, rank), F32), shape((rank, width), F32), tall],
            [VMEM] * 11,
            (base, low, scale, step_sum, step_far, grad_a, grad_b, factor_a, factor_b, cos, sin),
            "final",
            [pltpu.VMEM((width, rank), F32), pltpu.VMEM((rank, width), F32),
             pltpu.VMEM((rank, width), BF), pltpu.VMEM((count, width), BF), dma(2 + count // LANES)],
            [HBM] * 3,
        )
        return new_a, new_b, queries.reshape(steps, rows, width)

    return on_device


def solution(mesh):
    n_dp, n_roll, n_tp = (mesh.shape[a] for a in ("dp", "roll", "tp"))
    return jax.shard_map(
        build(n_dp, n_roll, n_tp),
        mesh=mesh,
        in_specs=(
            P(("dp", "roll"), "tp"),
            P(("dp", "roll"), "tp"),
            P("tp", None),
            P(None, "tp"),
            P("tp", None),
            P(None, ("dp", "roll"), "tp"),
            P("tp"),
            P(("dp", "roll")),
        ),
        out_specs=(P("tp", None), P(None, "tp"), P(None, ("dp", "roll"), "tp")),
        check_vma=False,
    )
```

```python
import functools

import jax
import jax.numpy as jnp
from jax import lax
from jax.experimental import pallas as pl
from jax.experimental.pallas import tpu as pltpu
from jax.sharding import PartitionSpec as P

D = 4096
HEAD = 128
SCALE = 2.0
LEARN = 3.0
EPS = 1e-05
NORM_EPS = 1e-06
LANES = 128
EXTRA = 32

BF = jnp.bfloat16
F32 = jnp.float32
VMEM = pl.BlockSpec(memory_space=pltpu.VMEM)
SMEM = pl.BlockSpec(memory_space=pltpu.SMEM)
ANY = pl.BlockSpec(memory_space=pl.ANY)
HBM = pl.BlockSpec(memory_space=pltpu.HBM)


def shape(dims, dtype):
    return jax.ShapeDtypeStruct(dims, dtype)


def dot(a, b, dims=((1,), (0,))):
    return lax.dot_general(a, b, (dims, ((), ())), preferred_element_type=F32)


def swap(x, axis, n, k):
    return lax.ppermute(x, axis, [(i, i ^ k) for i in range(n)])


def split_terms(values):
    high = values.astype(BF)
    rest = values - high.astype(F32)
    middle = rest.astype(BF)
    last = (rest - middle.astype(F32)).astype(BF)
    return jnp.concatenate([high, middle, last, jnp.zeros_like(last)], axis=0)


def join_terms(terms):
    x = terms.astype(F32)
    return (x[0:8] + x[8:16]) + x[16:24]


def fetch(sources, targets, sems):
    copies = [pltpu.make_async_copy(s, t, sems.at[i]) for i, (s, t) in enumerate(zip(sources, targets))]
    for copy in copies:
        copy.start()
    return copies


def blocks_of(count):
    return [slice(i, i + LANES) for i in range(0, count, LANES)]


def rank_kernel(x_hbm, v_hbm, a_hbm, b_hbm, out_ref, x_ref, v_ref, a_ref, b_ref, sems):
    copies = fetch((x_hbm, a_hbm, v_hbm, b_hbm), (x_ref, a_ref, v_ref, b_ref), sems)
    count = x_ref.shape[0]
    copies[0].wait()
    copies[1].wait()
    out_ref[:count] = dot(x_ref[...], a_ref[...].astype(BF)).astype(BF)
    copies[2].wait()
    copies[3].wait()
    out_ref[count:] = dot(v_ref[...], b_ref[...].astype(BF), ((1,), (1,))).astype(BF)


def weight_blocks(at, peers, w_hbm, w_ref):
    _, width, cut = w_ref.shape
    sources = []
    for peer in peers:
        for i in range(width // cut):
            start = (at[0] ^ peer) * width + i * cut
            sources.append(w_hbm.at[:, pl.ds(pl.multiple_of(start, cut), cut)])
    return sources, [w_ref.at[i] for i in range(len(sources))]


def prep_kernel(at, h_hbm, gain_hbm, a_hbm, w_hbm, hg_ref, wide_ref, h_ref, gain_ref, a_ref, w_ref, sems):
    count, width = h_ref.shape
    blocks = blocks_of(count)
    sources, targets = weight_blocks(at, (3,), w_hbm, w_ref)
    copies = fetch(
        [gain_hbm] + [h_hbm.at[b] for b in blocks] + [a_hbm] + sources,
        [gain_ref] + [h_ref.at[b] for b in blocks] + [a_ref] + targets,
        sems,
    )
    copies[0].wait()
    rows = []
    for i, b in enumerate(blocks):
        copies[1 + i].wait()
        wide = h_ref[b].astype(F32)
        hg_ref[b] = (wide * gain_ref[...]).astype(BF)
        sums = jnp.sum(wide * wide, axis=-1, keepdims=True)
        rows.append(jnp.broadcast_to(sums, (LANES, LANES)).T[0:1])
    if len(rows) < 8:
        rows.append(jnp.zeros((8 - len(rows), LANES), F32))
    wide_ref[count:, width:] = split_terms(jnp.concatenate(rows, axis=0))
    wide_ref[count:, :width] = jnp.zeros((EXTRA, width), BF)
    copies[1 + len(blocks)].wait()
    wide_ref[:count, width:] = dot(hg_ref[...], a_ref[...].astype(BF)).astype(BF)
    cut = w_ref.shape[2]
    for i in range(width // cut):
        copies[2 + len(blocks) + i].wait()
        wide_ref[:count, i * cut : (i + 1) * cut] = dot(hg_ref[...], w_ref[i]).astype(BF)


def part_kernel(x_ref, got_ref, pass_ref, out_ref, pass_out):
    sum_kernel(x_ref, got_ref, None, out_ref)


def query_kernel(peers, at, hg_ref, w_hbm, after_ref, *rest):
    outs, (w_ref, sems) = rest[:-2], rest[-2:]
    _, width, cut = w_ref.shape
    copies = fetch(*weight_blocks(at, peers, w_hbm, w_ref), sems)
    per = width // cut
    for i, copy in enumerate(copies):
        copy.wait()
        outs[i // per][:, i % per * cut : (i % per + 1) * cut] = dot(hg_ref[...], w_ref[i]).astype(BF)


def far_kernel(mine_ref, diag_ref, got_ref, after_ref, pass_ref, out_ref, pass_out):
    count, width = mine_ref.shape
    out_ref[:count, :width] = (mine_ref[...].astype(F32) + got_ref[:count, :width].astype(F32)).astype(BF)
    out_ref[count:, :width] = jnp.zeros((EXTRA, width), BF)
    out_ref[:count, width:] = (diag_ref[:count, width:].astype(F32) + got_ref[:count, width:].astype(F32)).astype(BF)
    out_ref[count:, width:] = split_terms(join_terms(diag_ref[count:, width:]) + join_terms(got_ref[count:, width:]))


def merge_kernel(a_ref, b_ref, out_ref):
    count = a_ref.shape[0] - EXTRA
    out_ref[:count] = (a_ref[:count].astype(F32) + b_ref[:count].astype(F32)).astype(BF)
    out_ref[count:] = split_terms(join_terms(a_ref[count:]) + join_terms(b_ref[count:]))


def halves(at, axis, bit, size):
    mine = lax.rem(at[axis] // (1 << bit), 2) * size
    other = size - mine
    return pl.ds(pl.multiple_of(mine, size), size), pl.ds(pl.multiple_of(other, size), size)


def halve(at, axis, bit, total_ref, keep_ref, send_ref):
    mine, other = halves(at, axis, bit, keep_ref.shape[0])
    keep_ref[...] = total_ref[mine]
    send_ref[...] = total_ref[other].astype(BF)


def grad_kernel(axes, at, x_ref, v_ref, s_ref, r_ref, pos_ref, keep_a, send_a, keep_b, send_b, pos_out, ga, gb):
    count, width = x_ref.shape
    low = (s_ref[...].astype(F32) + r_ref[...].astype(F32)).astype(BF)
    ga[...] = SCALE * dot(x_ref[...], low[count:], ((0,), (0,)))
    halve(at, *axes[0], ga, keep_a, send_a)
    turned = SCALE * dot(low[:count], v_ref[...], ((0,), (0,)))
    for b in blocks_of(width):
        gb[b] = turned[:, b]
    halve(at, *axes[1], gb, keep_b, send_b)
    pos_out[...] = pos_ref[...].astype(F32)


def halve_kernel(axis, bit, at, keep_ref, got_ref, after_ref, keep_out, send_out, total):
    total[...] = keep_ref[...] + got_ref[...].astype(F32)
    halve(at, axis, bit, total, keep_out, send_out)


def sum_kernel(keep_ref, got_ref, after_ref, out_ref):
    out_ref[...] = (keep_ref[...].astype(F32) + got_ref[...].astype(F32)).astype(BF)


def join_kernel(axis, bit, at, mine_ref, got_ref, out_ref):
    mine, other = halves(at, axis, bit, mine_ref.shape[0])
    out_ref[mine] = mine_ref[...]
    out_ref[other] = got_ref[...]


def square_terms(ref):
    x = ref[...].astype(F32)
    return split_terms(jnp.broadcast_to(jnp.sum(x * x), (8, LANES)))


def low_kernel(axis, bit, at, hg_ref, mine_ref, got_ref, pack_ref, ga_ref):
    join_kernel(axis, bit, at, mine_ref, got_ref, ga_ref)
    count = hg_ref.shape[0]
    pack_ref[:count] = dot(hg_ref[...], ga_ref[...]).astype(BF)
    pack_ref[count:] = square_terms(ga_ref)


def norm_kernel(axis, bit, at, mine_ref, got_ref, gb_ref, out_ref):
    join_kernel(axis, bit, at, mine_ref, got_ref, gb_ref)
    out_ref[...] = square_terms(gb_ref)


def norm_merge_kernel(a_ref, b_ref, out_ref):
    out_ref[...] = split_terms(join_terms(a_ref[...]) + join_terms(b_ref[...]))


def base_kernel(mine_ref, near_ref, far_ref, far_got, after_ref, base_ref, low_ref, scale_ref):
    count, width = mine_ref.shape
    sums = join_terms(far_ref[count:, width:]) + join_terms(far_got[count:, width:])
    scale = lax.rsqrt(sums / D + EPS)
    for i, b in enumerate(blocks_of(count)):
        block = jnp.broadcast_to(scale[i : i + 1], (LANES, LANES)).T
        scale_ref[b] = block
        low_ref[b] = (far_ref[b, width:].astype(F32) + far_got[b, width:].astype(F32)) * block
        for c in blocks_of(width):
            total = mine_ref[b, c].astype(F32) + near_ref[b, c].astype(F32) + far_got[b, c].astype(F32)
            base_ref[b, c] = total * block


def final_kernel(
    base_ref, low_ref, scale_ref, s_ref, r_ref, sn_ref, rn_ref, ga_ref, gb_ref, a_ref, b_ref, cos_ref, sin_ref,
    a_hbm, b_hbm, q_hbm, new_a, new_b, half_b, out, sems,
):
    count, width = base_ref.shape
    total = join_terms(s_ref[count:]) + join_terms(r_ref[count:])
    total = total + (join_terms(sn_ref[...]) + join_terms(rn_ref[...]))
    rate = (LEARN * lax.rsqrt(total + NORM_EPS))[0:1]
    for c in blocks_of(width):
        fresh = b_ref[:, c] - rate * gb_ref[c].astype(F32)
        new_b[:, c] = fresh
        half_b[:, c] = fresh.astype(BF)
    copies = [pltpu.make_async_copy(new_b, b_hbm, sems.at[0])]
    copies[-1].start()
    new_a[...] = a_ref[...] - rate * ga_ref[...].astype(F32)
    copies.append(pltpu.make_async_copy(new_a, a_hbm, sems.at[1]))
    copies[-1].start()
    for i, b in enumerate(blocks_of(count)):
        low = s_ref[b].astype(F32) + r_ref[b].astype(F32)
        mix = (low_ref[b] - rate * (low * scale_ref[b])) * SCALE
        update = dot(mix.astype(BF), half_b[...])
        cos, sin = cos_ref[b], sin_ref[b]
        for c in blocks_of(width):
            query = base_ref[b, c] + update[:, c]
            other = pltpu.roll(query, HEAD // 2, 1)
            out[b, c] = (query * cos + other * sin).astype(BF)
        copies.append(pltpu.make_async_copy(out.at[b], q_hbm.at[b], sems.at[2 + i]))
        copies[-1].start()
    for copy in copies:
        copy.wait()


def keep_hbm(x):
    return pltpu.with_memory_space_constraint(x, pltpu.HBM)


def call(kernel, outs, in_specs, args, name, scratch=(), out_specs=None, limit=16, aliases=None):
    return pl.pallas_call(
        kernel,
        out_shape=outs,
        in_specs=in_specs,
        out_specs=out_specs if out_specs is not None else jax.tree.map(lambda _: VMEM, outs),
        scratch_shapes=list(scratch),
        compiler_params=pltpu.CompilerParams(vmem_limit_bytes=int(limit * 1024 * 1024)),
        input_output_aliases=aliases or {},
        name=name,
    )(*args)


def turn_tables(places, steps):
    half = HEAD // 2
    freq = 10000.0 ** (-jnp.arange(half, dtype=F32) / half)
    cos, sin = [], []
    for step in range(steps):
        angle = (places + float(step))[:, None] * freq[None, :]
        c, s = jnp.cos(angle), jnp.sin(angle)
        cos.append(jnp.concatenate([c, c], axis=-1))
        sin.append(jnp.concatenate([-s, s], axis=-1))
    return jnp.concatenate(cos), jnp.concatenate(sin)


def bits_of(n):
    return [b for b in range(n.bit_length() - 1)]


def build(n_dp, n_roll, n_tp):
    z_bits = [(2, b) for b in bits_of(n_roll)]
    x_bits = [(1, b) for b in bits_of(n_dp)]

    def cross(x, axis, bit):
        name, n = (("dp", n_dp), ("roll", n_roll))[axis - 1]
        return swap(x, name, n, 1 << bit)

    def on_device(
        train_inputs, train_cotangent, factor_a, factor_b, base_weight, incoming, norm_gain, positions
    ):
        steps, rows, width = incoming.shape
        tokens = train_inputs.shape[0]
        rank = factor_a.shape[1]
        count = steps * rows
        at = jnp.stack([lax.axis_index(a) for a in ("tp", "dp", "roll")]).astype(jnp.int32)
        dma = lambda n: pltpu.SemaphoreType.DMA((n,))
        vmem = lambda n, dtype=F32: pltpu.VMEM((n, rank), dtype)

        part = call(
            rank_kernel,
            shape((2 * tokens, rank), BF),
            [HBM] * 4,
            tuple(map(keep_hbm, (train_inputs, train_cotangent, factor_a, factor_b))),
            "rank",
            [pltpu.VMEM(train_inputs.shape, BF), pltpu.VMEM(train_inputs.shape, BF),
             pltpu.VMEM(factor_a.shape, F32), pltpu.VMEM(factor_b.shape, F32), dma(4)],
        )
        part_got = swap(part, "tp", n_tp, 1)
        cut = 512
        wide = shape((count + EXTRA, width + rank), BF)
        tall = shape((count, width), BF)
        gained, diag = call(
            prep_kernel,
            [tall, wide],
            [SMEM] + [HBM] * 4,
            (at, *map(keep_hbm, (incoming.reshape(count, width), norm_gain[None, :], factor_a, base_weight))),
            "prep",
            [pltpu.VMEM((count, width), BF), pltpu.VMEM((1, width), F32), pltpu.VMEM(factor_a.shape, F32),
             pltpu.VMEM((width // cut, width, cut), BF), dma(2 + count // LANES + width // cut)],
        )
        part_sum, diag = call(
            part_kernel,
            [shape(part.shape, BF), wide],
            [VMEM] * 2 + [ANY],
            (part, part_got, diag),
            "part_sum",
            out_specs=[VMEM, ANY],
            aliases={2: 1},
        )
        part_far = swap(part_sum, "tp", n_tp, 2)
        diag_got = swap(diag, "tp", n_tp, 1)

        def query(peers, after, name):
            blocks = len(peers) * width // cut
            return call(
                functools.partial(query_kernel, peers),
                [tall] * len(peers),
                [SMEM, VMEM, HBM, ANY],
                (at, gained, keep_hbm(base_weight), after),
                name,
                [pltpu.VMEM((blocks, width, cut), BF), dma(blocks)],
            )

        distant, beside = query((2, 1), part_sum, "query_first")
        pos = positions.reshape(-1, LANES)
        half = width // 2
        a_axes, b_axes = z_bits, x_bits + z_bits
        keep_a, send_a, keep_b, send_b, places = call(
            functools.partial(grad_kernel, (a_axes[0], b_axes[0])),
            [shape((half, rank), F32), shape((half, rank), BF)] * 2 + [shape(pos.shape, F32)],
            [SMEM] + [VMEM] * 5,
            (at, train_inputs, train_cotangent, part_sum, part_far, pos),
            "grads",
            [vmem(width), vmem(width)],
        )
        far, beside = call(
            far_kernel,
            [wide, tall],
            [VMEM] * 3 + [ANY] * 2,
            (distant, diag, diag_got, send_a, beside),
            "far",
            out_specs=[VMEM, ANY],
            aliases={4: 1},
        )
        far_got = swap(far, "tp", n_tp, 2)
        got_a = cross(send_a, *a_axes[0])
        got_b = cross(send_b, *b_axes[0])
        beside_got = swap(beside, "tp", n_tp, 1)

        def halve_call(keep, got, axis, bit, after, name):
            size = keep.shape[0] // 2
            return call(
                functools.partial(halve_kernel, axis, bit),
                [shape((size, rank), F32), shape((size, rank), BF)],
                [SMEM] + [VMEM] * 2 + [ANY],
                (at, keep, got, after),
                name,
                [vmem(2 * size)],
            )

        def sum_call(keep, got, after, name):
            return call(
                sum_kernel, shape(keep.shape, BF), [VMEM] * 2 + [ANY], (keep, got, after), name
            )

        def join_call(mine, got, axis, bit, name):
            return call(
                functools.partial(join_kernel, axis, bit),
                shape((2 * mine.shape[0], rank), BF),
                [SMEM] + [VMEM] * 2,
                (at, mine, got),
                name,
            )

        (close,) = query((0,), far, "query_close")
        after = close
        for axis, bit in a_axes[1:]:
            keep_a, send_a = halve_call(keep_a, got_a, axis, bit, after, "halve_a")
            got_a = cross(send_a, axis, bit)
        chunk_a = sum_call(keep_a, got_a, after, "chunk_a")
        for axis, bit in x_bits:
            chunk_a = sum_call(chunk_a, cross(chunk_a, axis, bit), after, "cross_a")
        for axis, bit in reversed(a_axes[1:]):
            chunk_a = join_call(chunk_a, cross(chunk_a, axis, bit), axis, bit, "join_a")

        for axis, bit in b_axes[1:]:
            keep_b, send_b = halve_call(keep_b, got_b, axis, bit, send_b, "halve_b")
            got_b = cross(send_b, axis, bit)
        chunk_b = sum_call(keep_b, got_b, send_b, "chunk_b")
        for axis, bit in reversed(b_axes[1:]):
            chunk_b = join_call(chunk_b, cross(chunk_b, axis, bit), axis, bit, "join_b")

        step_pack, grad_a = call(
            functools.partial(low_kernel, *a_axes[0]),
            [shape((count + EXTRA, rank), BF), shape((width, rank), BF)],
            [SMEM] + [VMEM] * 3,
            (at, gained, chunk_a, cross(chunk_a, *a_axes[0])),
            "low_rank",
        )
        step_got = swap(step_pack, "tp", n_tp, 1)
        step_sum = call(merge_kernel, shape((count + EXTRA, rank), BF), [VMEM] * 2, (step_pack, step_got), "merge")
        step_far = swap(step_sum, "tp", n_tp, 2)
        grad_b, norm = call(
            functools.partial(norm_kernel, *b_axes[0]),
            [shape((width, rank), BF), shape((EXTRA, LANES), BF)],
            [SMEM] + [VMEM] * 2,
            (at, chunk_b, cross(chunk_b, *b_axes[0])),
            "norm",
        )
        norm_got = swap(norm, "tp", n_tp, 1)
        norm_sum = call(norm_merge_kernel, shape((EXTRA, LANES), BF), [VMEM] * 2, (norm, norm_got), "norm_merge")
        norm_far = swap(norm_sum, "tp", n_tp, 2)
        base, low, scale = call(
            base_kernel,
            [shape((count, width), F32), shape((count, rank), F32), shape((count, LANES), F32)],
            [VMEM] * 4 + [ANY],
            (close, beside_got, far, far_got, step_sum),
            "base",
        )
        cos, sin = turn_tables(places.reshape(rows), steps)
        new_a, new_b, queries = call(
            final_kernel,
            [shape((width, rank), F32), shape((rank, width), F32), tall],
            [VMEM] * 13,
            (base, low, scale, step_sum, step_far, norm_sum, norm_far, grad_a, grad_b, factor_a, factor_b, cos, sin),
            "final",
            [pltpu.VMEM((width, rank), F32), pltpu.VMEM((rank, width), F32),
             pltpu.VMEM((rank, width), BF), pltpu.VMEM((count, width), BF), dma(2 + count // LANES)],
            [HBM] * 3,
        )
        return new_a, new_b, queries.reshape(steps, rows, width)

    return on_device


def solution(mesh):
    n_dp, n_roll, n_tp = (mesh.shape[a] for a in ("dp", "roll", "tp"))
    return jax.shard_map(
        build(n_dp, n_roll, n_tp),
        mesh=mesh,
        in_specs=(
            P(("dp", "roll"), "tp"),
            P(("dp", "roll"), "tp"),
            P("tp", None),
            P(None, "tp"),
            P("tp", None),
            P(None, ("dp", "roll"), "tp"),
            P("tp"),
            P(("dp", "roll")),
        ),
        out_specs=(P("tp", None), P(None, "tp"), P(None, ("dp", "roll"), "tp")),
        check_vma=False,
    )
```

```python
import functools

import jax
import jax.numpy as jnp
from jax import lax
from jax.experimental import pallas as pl
from jax.experimental.pallas import tpu as pltpu
from jax.sharding import PartitionSpec as P

D = 4096
HEAD = 128
SCALE = 2.0
LEARN = 3.0
EPS = 1e-05
NORM_EPS = 1e-06
LANES = 128
EXTRA = 32

BF = jnp.bfloat16
F32 = jnp.float32
VMEM = pl.BlockSpec(memory_space=pltpu.VMEM)
ANY = pl.BlockSpec(memory_space=pl.ANY)
HBM = pl.BlockSpec(memory_space=pltpu.HBM)


def shape(dims, dtype):
    return jax.ShapeDtypeStruct(dims, dtype)


def dot(a, b, dims=((1,), (0,))):
    return lax.dot_general(a, b, (dims, ((), ())), preferred_element_type=F32)


def swap(x, axis, n, k):
    return lax.ppermute(x, axis, [(i, i ^ k) for i in range(n)])


def split_terms(values):
    high = values.astype(BF)
    rest = values - high.astype(F32)
    middle = rest.astype(BF)
    last = (rest - middle.astype(F32)).astype(BF)
    return jnp.concatenate([high, middle, last, jnp.zeros_like(last)], axis=0)


def join_terms(terms):
    x = terms.astype(F32)
    return (x[0:8] + x[8:16]) + x[16:24]


def fetch(sources, targets, sems):
    copies = [pltpu.make_async_copy(s, t, sems.at[i]) for i, (s, t) in enumerate(zip(sources, targets))]
    for copy in copies:
        copy.start()
    return copies


def blocks_of(count):
    return [slice(i, i + LANES) for i in range(0, count, LANES)]


def rank_kernel(x_hbm, v_hbm, a_hbm, b_hbm, out_ref, x_ref, v_ref, a_ref, b_ref, sems):
    copies = fetch((x_hbm, a_hbm, v_hbm, b_hbm), (x_ref, a_ref, v_ref, b_ref), sems)
    count = x_ref.shape[0]
    copies[0].wait()
    copies[1].wait()
    out_ref[:count] = dot(x_ref[...], a_ref[...].astype(BF)).astype(BF)
    copies[2].wait()
    copies[3].wait()
    out_ref[count:] = dot(v_ref[...], b_ref[...].astype(BF), ((1,), (1,))).astype(BF)


def weight_blocks(peers, w_hbm, w_ref):
    _, width, cut = w_ref.shape
    mine = lax.axis_index("tp")
    sources = []
    for peer in peers:
        for i in range(width // cut):
            start = (mine ^ peer) * width + i * cut
            sources.append(w_hbm.at[:, pl.ds(pl.multiple_of(start, cut), cut)])
    return sources, [w_ref.at[i] for i in range(len(sources))]


def prep_kernel(h_hbm, gain_hbm, a_hbm, w_hbm, hg_ref, wide_ref, h_ref, gain_ref, a_ref, w_ref, sems):
    count, width = h_ref.shape
    blocks = blocks_of(count)
    sources, targets = weight_blocks((3,), w_hbm, w_ref)
    copies = fetch(
        [gain_hbm] + [h_hbm.at[b] for b in blocks] + [a_hbm] + sources,
        [gain_ref] + [h_ref.at[b] for b in blocks] + [a_ref] + targets,
        sems,
    )
    copies[0].wait()
    rows = []
    for i, b in enumerate(blocks):
        copies[1 + i].wait()
        wide = h_ref[b].astype(F32)
        hg_ref[b] = (wide * gain_ref[...]).astype(BF)
        sums = jnp.sum(wide * wide, axis=-1, keepdims=True)
        rows.append(jnp.broadcast_to(sums, (LANES, LANES)).T[0:1])
    if len(rows) < 8:
        rows.append(jnp.zeros((8 - len(rows), LANES), F32))
    wide_ref[count:, width:] = split_terms(jnp.concatenate(rows, axis=0))
    wide_ref[count:, :width] = jnp.zeros((EXTRA, width), BF)
    copies[1 + len(blocks)].wait()
    wide_ref[:count, width:] = dot(hg_ref[...], a_ref[...].astype(BF)).astype(BF)
    cut = w_ref.shape[2]
    for i in range(width // cut):
        copies[2 + len(blocks) + i].wait()
        wide_ref[:count, i * cut : (i + 1) * cut] = dot(hg_ref[...], w_ref[i]).astype(BF)


def part_kernel(x_ref, got_ref, pass_ref, out_ref, pass_out):
    sum_kernel(x_ref, got_ref, out_ref)


def query_kernel(peers, hg_ref, w_hbm, after_ref, *rest):
    outs, (w_ref, sems) = rest[:-2], rest[-2:]
    _, width, cut = w_ref.shape
    copies = fetch(*weight_blocks(peers, w_hbm, w_ref), sems)
    per = width // cut
    for i, copy in enumerate(copies):
        copy.wait()
        outs[i // per][:, i % per * cut : (i % per + 1) * cut] = dot(hg_ref[...], w_ref[i]).astype(BF)


def far_kernel(mine_ref, diag_ref, got_ref, after_ref, pass_ref, out_ref, pass_out):
    count, width = mine_ref.shape
    out_ref[:count, :width] = (mine_ref[...].astype(F32) + got_ref[:count, :width].astype(F32)).astype(BF)
    out_ref[count:, :width] = jnp.zeros((EXTRA, width), BF)
    out_ref[:count, width:] = (diag_ref[:count, width:].astype(F32) + got_ref[:count, width:].astype(F32)).astype(BF)
    out_ref[count:, width:] = split_terms(join_terms(diag_ref[count:, width:]) + join_terms(got_ref[count:, width:]))


def merge_kernel(a_ref, b_ref, out_ref):
    count = a_ref.shape[0] - EXTRA
    out_ref[:count] = (a_ref[:count].astype(F32) + b_ref[:count].astype(F32)).astype(BF)
    out_ref[count:] = split_terms(join_terms(a_ref[count:]) + join_terms(b_ref[count:]))


def halves(axis, bit, size):
    mine = lax.rem(lax.axis_index(axis) // (1 << bit), 2) * size
    return pl.ds(pl.multiple_of(mine, size), size), pl.ds(pl.multiple_of(size - mine, size), size)


def halve(axis, bit, total_ref, keep_ref, send_ref):
    mine, other = halves(axis, bit, keep_ref.shape[0])
    keep_ref[...] = total_ref[mine]
    send_ref[...] = total_ref[other].astype(BF)


def join(axis, bit, mine_ref, got_ref, out_ref):
    mine, other = halves(axis, bit, mine_ref.shape[0])
    out_ref[mine] = mine_ref[...]
    out_ref[other] = got_ref[...]


def grad_kernel(axes, x_ref, v_ref, s_ref, r_ref, pos_ref, keep_a, send_a, keep_b, send_b, pos_out, ga, gb):
    count, width = x_ref.shape
    low = (s_ref[...].astype(F32) + r_ref[...].astype(F32)).astype(BF)
    ga[...] = SCALE * dot(x_ref[...], low[count:], ((0,), (0,)))
    halve(*axes[0], ga, keep_a, send_a)
    turned = SCALE * dot(low[:count], v_ref[...], ((0,), (0,)))
    for b in blocks_of(width):
        gb[b] = turned[:, b]
    halve(*axes[1], gb, keep_b, send_b)
    pos_out[...] = pos_ref[...].astype(F32)


def sum_kernel(keep_ref, got_ref, out_ref):
    out_ref[...] = (keep_ref[...].astype(F32) + got_ref[...].astype(F32)).astype(BF)


def step_kernel(steps, *refs):
    n = len(steps)
    ins, outs = refs[: 2 * n], list(refs[2 * n + 1 :])
    for i, (kind, axis, bit) in enumerate(steps):
        mine, got = ins[2 * i], ins[2 * i + 1]
        if kind == "halve":
            total = outs.pop()
            total[...] = mine[...] + got[...].astype(F32)
            halve(axis, bit, total, outs.pop(0), outs.pop(0))
        elif kind == "sum":
            sum_kernel(mine, got, outs.pop(0))
        else:
            join(axis, bit, mine, got, outs.pop(0))


def square_terms(ref):
    x = ref[...].astype(F32)
    return split_terms(jnp.broadcast_to(jnp.sum(x * x), (8, LANES)))


def low_kernel(axis, bit, hg_ref, mine_a, got_a, mine_b, got_b, pack_ref, ga_ref, gb_ref, norm_ref):
    join(axis, bit, mine_a, got_a, ga_ref)
    count = hg_ref.shape[0]
    pack_ref[:count] = dot(hg_ref[...], ga_ref[...]).astype(BF)
    pack_ref[count:] = square_terms(ga_ref)
    join(axis, bit, mine_b, got_b, gb_ref)
    norm_ref[...] = square_terms(gb_ref)


def norm_merge_kernel(a_ref, b_ref, out_ref):
    out_ref[...] = split_terms(join_terms(a_ref[...]) + join_terms(b_ref[...]))


def base_kernel(mine_ref, near_ref, far_ref, far_got, after_ref, base_ref, low_ref, scale_ref):
    count, width = mine_ref.shape
    sums = join_terms(far_ref[count:, width:]) + join_terms(far_got[count:, width:])
    scale = lax.rsqrt(sums / D + EPS)
    for i, b in enumerate(blocks_of(count)):
        block = jnp.broadcast_to(scale[i : i + 1], (LANES, LANES)).T
        scale_ref[b] = block
        low_ref[b] = (far_ref[b, width:].astype(F32) + far_got[b, width:].astype(F32)) * block
        for c in blocks_of(width):
            total = mine_ref[b, c].astype(F32) + near_ref[b, c].astype(F32) + far_got[b, c].astype(F32)
            base_ref[b, c] = total * block


def final_kernel(
    axis, bit, base_ref, low_ref, scale_ref, s_ref, r_ref, sn_ref, rn_ref, ga_ref, mine_b, got_b, a_ref, b_ref,
    cos_ref, sin_ref, a_hbm, b_hbm, q_hbm, gb_ref, new_a, new_b, half_b, out, sems,
):
    join(axis, bit, mine_b, got_b, gb_ref)
    count, width = base_ref.shape
    total = join_terms(s_ref[count:]) + join_terms(r_ref[count:])
    total = total + (join_terms(sn_ref[...]) + join_terms(rn_ref[...]))
    rate = (LEARN * lax.rsqrt(total + NORM_EPS))[0:1]
    for c in blocks_of(width):
        fresh = b_ref[:, c] - rate * gb_ref[c].astype(F32)
        new_b[:, c] = fresh
        half_b[:, c] = fresh.astype(BF)
    copies = [pltpu.make_async_copy(new_b, b_hbm, sems.at[0])]
    copies[-1].start()
    new_a[...] = a_ref[...] - rate * ga_ref[...].astype(F32)
    copies.append(pltpu.make_async_copy(new_a, a_hbm, sems.at[1]))
    copies[-1].start()
    for i, b in enumerate(blocks_of(count)):
        low = s_ref[b].astype(F32) + r_ref[b].astype(F32)
        mix = (low_ref[b] - rate * (low * scale_ref[b])) * SCALE
        update = dot(mix.astype(BF), half_b[...])
        cos, sin = cos_ref[b], sin_ref[b]
        for c in blocks_of(width):
            query = base_ref[b, c] + update[:, c]
            other = pltpu.roll(query, HEAD // 2, 1)
            out[b, c] = (query * cos + other * sin).astype(BF)
        copies.append(pltpu.make_async_copy(out.at[b], q_hbm.at[b], sems.at[2 + i]))
        copies[-1].start()
    for copy in copies:
        copy.wait()


def keep_hbm(x):
    return pltpu.with_memory_space_constraint(x, pltpu.HBM)


def call(kernel, outs, in_specs, args, name, scratch=(), out_specs=None, limit=16, aliases=None):
    return pl.pallas_call(
        kernel,
        out_shape=outs,
        in_specs=in_specs,
        out_specs=out_specs if out_specs is not None else jax.tree.map(lambda _: VMEM, outs),
        scratch_shapes=list(scratch),
        compiler_params=pltpu.CompilerParams(vmem_limit_bytes=int(limit * 1024 * 1024)),
        input_output_aliases=aliases or {},
        name=name,
    )(*args)


def turn_tables(places, steps):
    half = HEAD // 2
    freq = 10000.0 ** (-jnp.arange(half, dtype=F32) / half)
    cos, sin = [], []
    for step in range(steps):
        angle = (places + float(step))[:, None] * freq[None, :]
        c, s = jnp.cos(angle), jnp.sin(angle)
        cos.append(jnp.concatenate([c, c], axis=-1))
        sin.append(jnp.concatenate([-s, s], axis=-1))
    return jnp.concatenate(cos), jnp.concatenate(sin)


def bits_of(n):
    return [b for b in range(n.bit_length() - 1)]


def build(n_dp, n_roll, n_tp):
    z_bits = [("roll", b) for b in bits_of(n_roll)]
    x_bits = [("dp", b) for b in bits_of(n_dp)]
    sizes = {"dp": n_dp, "roll": n_roll}

    def cross(x, axis, bit):
        return swap(x, axis, sizes[axis], 1 << bit)

    def path(down, across):
        ways = down + across + down[::-1]
        after = [("halve",) + way for way in down[1:]] + [("sum", None, None)] * (1 + len(across))
        return list(zip(ways, after + [("join",) + way for way in down[::-1]]))

    path_a, path_b = path(z_bits, x_bits), path(x_bits + z_bits, [])

    def on_device(
        train_inputs, train_cotangent, factor_a, factor_b, base_weight, incoming, norm_gain, positions
    ):
        steps, rows, width = incoming.shape
        tokens = train_inputs.shape[0]
        rank = factor_a.shape[1]
        count = steps * rows
        dma = lambda n: pltpu.SemaphoreType.DMA((n,))
        vmem = lambda n, dtype=F32: pltpu.VMEM((n, rank), dtype)

        part = call(
            rank_kernel,
            shape((2 * tokens, rank), BF),
            [HBM] * 4,
            tuple(map(keep_hbm, (train_inputs, train_cotangent, factor_a, factor_b))),
            "rank",
            [pltpu.VMEM(train_inputs.shape, BF), pltpu.VMEM(train_inputs.shape, BF),
             pltpu.VMEM(factor_a.shape, F32), pltpu.VMEM(factor_b.shape, F32), dma(4)],
        )
        part_got = swap(part, "tp", n_tp, 1)
        cut = 512
        wide = shape((count + EXTRA, width + rank), BF)
        tall = shape((count, width), BF)
        gained, diag = call(
            prep_kernel,
            [tall, wide],
            [HBM] * 4,
            tuple(map(keep_hbm, (incoming.reshape(count, width), norm_gain[None, :], factor_a, base_weight))),
            "prep",
            [pltpu.VMEM((count, width), BF), pltpu.VMEM((1, width), F32), pltpu.VMEM(factor_a.shape, F32),
             pltpu.VMEM((width // cut, width, cut), BF), dma(2 + count // LANES + width // cut)],
        )
        part_sum, diag = call(
            part_kernel,
            [shape(part.shape, BF), wide],
            [VMEM] * 2 + [ANY],
            (part, part_got, diag),
            "part_sum",
            out_specs=[VMEM, ANY],
            aliases={2: 1},
        )
        part_far = swap(part_sum, "tp", n_tp, 2)
        diag_got = swap(diag, "tp", n_tp, 1)

        def query(peers, after, name):
            blocks = len(peers) * width // cut
            return call(
                functools.partial(query_kernel, peers),
                [tall] * len(peers),
                [VMEM, HBM, ANY],
                (gained, keep_hbm(base_weight), after),
                name,
                [pltpu.VMEM((blocks, width, cut), BF), dma(blocks)],
            )

        distant, beside = query((2, 1), part_sum, "query_first")
        pos = positions.reshape(-1, LANES)
        half = width // 2
        keep_a, send_a, keep_b, send_b, places = call(
            functools.partial(grad_kernel, (path_a[0][0], path_b[0][0])),
            [shape((half, rank), F32), shape((half, rank), BF)] * 2 + [shape(pos.shape, F32)],
            [VMEM] * 5,
            (train_inputs, train_cotangent, part_sum, part_far, pos),
            "grads",
            [vmem(width), vmem(width)],
        )
        far, beside = call(
            far_kernel,
            [wide, tall],
            [VMEM] * 3 + [ANY] * 2,
            (distant, diag, diag_got, send_a, beside),
            "far",
            out_specs=[VMEM, ANY],
            aliases={4: 1},
        )
        far_got = swap(far, "tp", n_tp, 2)
        beside_got = swap(beside, "tp", n_tp, 1)
        (close,) = query((0,), far, "query_close")
        cos, sin = turn_tables(places.reshape(rows), steps)

        def step_call(steps, after, name):
            ins, outs, scratch = [], [], []
            for (kind, _, _), mine, got in steps:
                size = mine.shape[0]
                ins += [mine, got]
                if kind == "halve":
                    outs += [shape((size // 2, rank), F32), shape((size // 2, rank), BF)]
                    scratch.append(vmem(size))
                else:
                    outs.append(shape((2 * size if kind == "join" else size, rank), BF))
            made = call(
                functools.partial(step_kernel, [step[0] for step in steps]),
                outs,
                [VMEM] * len(ins) + [ANY],
                (*ins, after),
                name,
                scratch,
            )
            made, states = list(made), []
            for (kind, _, _), _, _ in steps:
                states.append((made.pop(0), made.pop(0)) if kind == "halve" else (made[0], made.pop(0)))
            return states

        state_a, state_b = (keep_a, send_a), (keep_b, send_b)
        for i, ((way_a, step_a), (way_b, step_b)) in enumerate(zip(path_a[:-1], path_b)):
            got_a, got_b = cross(state_a[1], *way_a), cross(state_b[1], *way_b)
            after = close if i == 0 else cos if i == 1 else sin
            state_a, state_b = step_call(
                [(step_a, state_a[0], got_a), (step_b, state_b[0], got_b)], after, f"step_{i}"
            )
        way = path_a[-1][0]
        mine_a, mine_b = state_a[1], state_b[1]
        got_a, got_b = cross(mine_a, *way), cross(mine_b, *way)
        step_pack, grad_a, mine_b, norm = call(
            functools.partial(low_kernel, *way),
            [shape((count + EXTRA, rank), BF), shape((width, rank), BF), shape((2 * mine_b.shape[0], rank), BF),
             shape((EXTRA, LANES), BF)],
            [VMEM] * 5,
            (gained, mine_a, got_a, mine_b, got_b),
            "low_rank",
        )
        step_got = swap(step_pack, "tp", n_tp, 1)
        step_sum = call(merge_kernel, shape((count + EXTRA, rank), BF), [VMEM] * 2, (step_pack, step_got), "merge")
        step_far = swap(step_sum, "tp", n_tp, 2)

        for (axis, bit), step in path_b[len(path_a) : -1]:
            ((_, mine_b),) = step_call([(step, mine_b, cross(mine_b, axis, bit))], step_pack, "join_b")
        got_b = cross(mine_b, *path_b[-1][0])

        def norm_add(x, y):
            return call(norm_merge_kernel, shape((EXTRA, LANES), BF), [VMEM] * 2, (x, y), "norm_merge")

        for way in x_bits:
            norm = norm_add(norm, cross(norm, *way))
        norm = norm_add(norm, swap(norm, "tp", n_tp, 1))
        norm_far = swap(norm, "tp", n_tp, 2)
        base, low, scale = call(
            base_kernel,
            [shape((count, width), F32), shape((count, rank), F32), shape((count, LANES), F32)],
            [VMEM] * 4 + [ANY],
            (close, beside_got, far, far_got, step_sum),
            "base",
        )
        new_a, new_b, queries = call(
            functools.partial(final_kernel, *path_b[-1][0]),
            [shape((width, rank), F32), shape((rank, width), F32), tall],
            [VMEM] * 14,
            (base, low, scale, step_sum, step_far, norm, norm_far, grad_a, mine_b, got_b, factor_a, factor_b, cos, sin),
            "final",
            [vmem(width, BF), pltpu.VMEM((width, rank), F32), pltpu.VMEM((rank, width), F32),
             pltpu.VMEM((rank, width), BF), pltpu.VMEM((count, width), BF), dma(2 + count // LANES)],
            [HBM] * 3,
        )
        return new_a, new_b, queries.reshape(steps, rows, width)

    return on_device


def solution(mesh):
    n_dp, n_roll, n_tp = (mesh.shape[a] for a in ("dp", "roll", "tp"))
    return jax.shard_map(
        build(n_dp, n_roll, n_tp),
        mesh=mesh,
        in_specs=(
            P(("dp", "roll"), "tp"),
            P(("dp", "roll"), "tp"),
            P("tp", None),
            P(None, "tp"),
            P("tp", None),
            P(None, ("dp", "roll"), "tp"),
            P("tp"),
            P(("dp", "roll")),
        ),
        out_specs=(P("tp", None), P(None, "tp"), P(None, ("dp", "roll"), "tp")),
        check_vma=False,
    )
```

```python
import functools

import jax
import jax.numpy as jnp
from jax import lax
from jax.experimental import pallas as pl
from jax.experimental.pallas import tpu as pltpu
from jax.sharding import PartitionSpec as P

D = 4096
HEAD = 128
SCALE = 2.0
LEARN = 3.0
EPS = 1e-05
NORM_EPS = 1e-06
LANES = 128
EXTRA = 32

BF = jnp.bfloat16
F32 = jnp.float32
VMEM = pl.BlockSpec(memory_space=pltpu.VMEM)
ANY = pl.BlockSpec(memory_space=pl.ANY)
HBM = pl.BlockSpec(memory_space=pltpu.HBM)


def shape(dims, dtype):
    return jax.ShapeDtypeStruct(dims, dtype)


def dot(a, b, dims=((1,), (0,))):
    return lax.dot_general(a, b, (dims, ((), ())), preferred_element_type=F32)


def swap(x, axis, n, k):
    return lax.ppermute(x, axis, [(i, i ^ k) for i in range(n)])


def split_terms(values):
    high = values.astype(BF)
    rest = values - high.astype(F32)
    middle = rest.astype(BF)
    last = (rest - middle.astype(F32)).astype(BF)
    return jnp.concatenate([high, middle, last, jnp.zeros_like(last)], axis=0)


def join_terms(terms):
    x = terms.astype(F32)
    return (x[0:8] + x[8:16]) + x[16:24]


def fetch(sources, targets, sems):
    copies = [pltpu.make_async_copy(s, t, sems.at[i]) for i, (s, t) in enumerate(zip(sources, targets))]
    for copy in copies:
        copy.start()
    return copies


def blocks_of(count):
    return [slice(i, i + LANES) for i in range(0, count, LANES)]


def rank_kernel(x_hbm, v_hbm, a_hbm, b_hbm, out_ref, x_ref, v_ref, a_ref, b_ref, sems):
    copies = fetch((x_hbm, a_hbm, v_hbm, b_hbm), (x_ref, a_ref, v_ref, b_ref), sems)
    count = x_ref.shape[0]
    copies[0].wait()
    copies[1].wait()
    out_ref[:count] = dot(x_ref[...], a_ref[...].astype(BF)).astype(BF)
    copies[2].wait()
    copies[3].wait()
    out_ref[count:] = dot(v_ref[...], b_ref[...].astype(BF), ((1,), (1,))).astype(BF)


def weight_blocks(peers, w_hbm, w_ref):
    _, width, cut = w_ref.shape
    mine = lax.axis_index("tp")
    sources = []
    for peer in peers:
        for i in range(width // cut):
            start = (mine ^ peer) * width + i * cut
            sources.append(w_hbm.at[:, pl.ds(pl.multiple_of(start, cut), cut)])
    return sources, [w_ref.at[i] for i in range(len(sources))]


def prep_kernel(h_hbm, gain_hbm, a_hbm, hg_ref, pack_ref, h_ref, gain_ref, a_ref, sems):
    count, width = h_ref.shape
    blocks = blocks_of(count)
    copies = fetch(
        [gain_hbm] + [h_hbm.at[b] for b in blocks] + [a_hbm],
        [gain_ref] + [h_ref.at[b] for b in blocks] + [a_ref],
        sems,
    )
    copies[0].wait()
    rows = []
    for i, b in enumerate(blocks):
        copies[1 + i].wait()
        wide = h_ref[b].astype(F32)
        hg_ref[b] = (wide * gain_ref[...]).astype(BF)
        sums = jnp.sum(wide * wide, axis=-1, keepdims=True)
        rows.append(jnp.broadcast_to(sums, (LANES, LANES)).T[0:1])
    if len(rows) < 8:
        rows.append(jnp.zeros((8 - len(rows), LANES), F32))
    pack_ref[count:] = split_terms(jnp.concatenate(rows, axis=0))
    copies[-1].wait()
    pack_ref[:count] = dot(hg_ref[...], a_ref[...].astype(BF)).astype(BF)


def part_kernel(x_ref, got_ref, after_ref, out_ref):
    sum_kernel(x_ref, got_ref, out_ref)


def query_kernel(peers, hg_ref, w_hbm, pack_ref, after_ref, *rest):
    outs, (w_ref, sems) = rest[:-2], rest[-2:]
    _, width, cut = w_ref.shape
    copies = fetch(*weight_blocks(peers, w_hbm, w_ref), sems)
    count = hg_ref.shape[0]
    if outs[0].shape[0] > count:
        outs[0][count:, :width] = jnp.zeros((EXTRA, width), BF)
        outs[0][:, width:] = pack_ref[...]
    per = width // cut
    for i, copy in enumerate(copies):
        copy.wait()
        block = dot(hg_ref[...], w_ref[i]).astype(BF)
        outs[i // per][:count, i % per * cut : (i % per + 1) * cut] = block


def far_kernel(mine_ref, diag_ref, got_ref, after_ref, pass_ref, out_ref, pass_out):
    count, width = mine_ref.shape
    out_ref[:count, :width] = (mine_ref[...].astype(F32) + got_ref[:count, :width].astype(F32)).astype(BF)
    out_ref[count:, :width] = jnp.zeros((EXTRA, width), BF)
    out_ref[:count, width:] = (diag_ref[:count, width:].astype(F32) + got_ref[:count, width:].astype(F32)).astype(BF)
    out_ref[count:, width:] = split_terms(join_terms(diag_ref[count:, width:]) + join_terms(got_ref[count:, width:]))


def merge_kernel(a_ref, b_ref, out_ref):
    count = a_ref.shape[0] - EXTRA
    out_ref[:count] = (a_ref[:count].astype(F32) + b_ref[:count].astype(F32)).astype(BF)
    out_ref[count:] = split_terms(join_terms(a_ref[count:]) + join_terms(b_ref[count:]))


def halves(axis, bit, size):
    mine = lax.rem(lax.axis_index(axis) // (1 << bit), 2) * size
    return pl.ds(pl.multiple_of(mine, size), size), pl.ds(pl.multiple_of(size - mine, size), size)


def halve(axis, bit, total_ref, keep_ref, send_ref):
    mine, other = halves(axis, bit, keep_ref.shape[0])
    keep_ref[...] = total_ref[mine]
    send_ref[...] = total_ref[other].astype(BF)


def join(axis, bit, mine_ref, got_ref, out_ref):
    mine, other = halves(axis, bit, mine_ref.shape[0])
    out_ref[mine] = mine_ref[...]
    out_ref[other] = got_ref[...]


def join_some(axis, bit, mine_ref, got_ref, out_ref):
    size = mine_ref.shape[0] - EXTRA
    mine, other = halves(axis, bit, size)
    out_ref[mine] = mine_ref[:size]
    out_ref[other] = got_ref[:size]


def grad_kernel(axes, x_ref, v_ref, s_ref, r_ref, pass_ref, keep_a, send_a, keep_b, send_b, pass_out, ga, gb):
    count, width = x_ref.shape
    low = (s_ref[...].astype(F32) + r_ref[...].astype(F32)).astype(BF)
    ga[...] = SCALE * dot(x_ref[...], low[count:], ((0,), (0,)))
    halve(*axes[0], ga, keep_a, send_a)
    turned = SCALE * dot(low[:count], v_ref[...], ((0,), (0,)))
    for b in blocks_of(width):
        gb[b] = turned[:, b]
    halve(*axes[1], gb, keep_b, send_b)


def sum_kernel(keep_ref, got_ref, out_ref):
    out_ref[...] = (keep_ref[...].astype(F32) + got_ref[...].astype(F32)).astype(BF)


def tree_sum(values):
    while len(values) > 1:
        values = [a + b for a, b in zip(values[::2], values[1::2])]
    return values[0]


def step_kernel(plan, *refs):
    ins, refs = refs[: sum(n for _, n in plan)], refs[sum(n for _, n in plan) + 1 :]
    ins, outs = list(ins), list(refs)
    for (kind, axis, bit), n in plan:
        mine, got, terms = ins[0], ins[1], ins[2:n]
        ins = ins[n:]
        if kind == "halve":
            total = outs.pop()
            total[...] = mine[...] + got[...].astype(F32)
            halve(axis, bit, total, outs.pop(0), outs.pop(0))
        elif kind == "sum":
            sum_kernel(mine, got, outs.pop(0))
        elif kind == "norm":
            size = mine.shape[0]
            total = mine[...] + got[...].astype(F32)
            out, sums = outs.pop(0), outs.pop(0)
            out[:size] = total.astype(BF)
            sums[...] = split_terms(jnp.broadcast_to(jnp.sum(total * total), (8, LANES)))
            out[size:] = sums[...]
        elif kind == "join":
            join(axis, bit, mine, got, outs.pop(0))
        else:
            out = outs.pop(0)
            join_some(axis, bit, mine, got, out)
            half = len(terms) // 2
            near = tree_sum([join_terms(mine[-EXTRA:])] + [join_terms(t[...]) for t in terms[:half]])
            far = tree_sum([join_terms(got[-EXTRA:])] + [join_terms(t[...]) for t in terms[half:]])
            out[-EXTRA:] = split_terms(near + far)


def place_kernel(pos_ref, after_ref, out_ref):
    out_ref[...] = pos_ref[...].astype(F32)


def square_sum(ref):
    x = ref[...].astype(F32)
    return jnp.broadcast_to(jnp.sum(x * x), (8, LANES))


def low_kernel(axis, bit, hg_ref, mine_a, got_a, mine_b, got_b, pack_ref, ga_ref, gb_ref):
    join(axis, bit, mine_a, got_a, ga_ref)
    count = hg_ref.shape[0]
    pack_ref[:count] = dot(hg_ref[...], ga_ref[...]).astype(BF)
    join_some(axis, bit, mine_b, got_b, gb_ref)
    total = square_sum(ga_ref) + (join_terms(mine_b[-EXTRA:]) + join_terms(got_b[-EXTRA:]))
    pack_ref[count:] = split_terms(total)


def base_kernel(mine_ref, near_ref, far_ref, far_got, after_ref, base_ref, low_ref, scale_ref):
    count, width = mine_ref.shape
    sums = join_terms(far_ref[count:, width:]) + join_terms(far_got[count:, width:])
    scale = lax.rsqrt(sums / D + EPS)
    for i, b in enumerate(blocks_of(count)):
        block = jnp.broadcast_to(scale[i : i + 1], (LANES, LANES)).T
        scale_ref[b] = block
        low_ref[b] = (far_ref[b, width:].astype(F32) + far_got[b, width:].astype(F32)) * block
        for c in blocks_of(width):
            total = mine_ref[b, c].astype(F32) + near_ref[b, c].astype(F32) + far_got[b, c].astype(F32)
            base_ref[b, c] = total * block


def final_kernel(
    axis, bit, base_ref, low_ref, scale_ref, s_ref, r_ref, ga_ref, mine_b, got_b, a_ref, b_ref,
    cos_ref, sin_ref, a_hbm, b_hbm, q_hbm, gb_ref, new_a, new_b, half_b, out, sems,
):
    join(axis, bit, mine_b, got_b, gb_ref)
    count, width = base_ref.shape
    total = join_terms(s_ref[count:]) + join_terms(r_ref[count:])
    rate = (LEARN * lax.rsqrt(total + NORM_EPS))[0:1]
    for c in blocks_of(width):
        fresh = b_ref[:, c] - rate * gb_ref[c].astype(F32)
        new_b[:, c] = fresh
        half_b[:, c] = fresh.astype(BF)
    copies = [pltpu.make_async_copy(new_b, b_hbm, sems.at[0])]
    copies[-1].start()
    new_a[...] = a_ref[...] - rate * ga_ref[...].astype(F32)
    copies.append(pltpu.make_async_copy(new_a, a_hbm, sems.at[1]))
    copies[-1].start()
    for i, b in enumerate(blocks_of(count)):
        low = s_ref[b].astype(F32) + r_ref[b].astype(F32)
        mix = (low_ref[b] - rate * (low * scale_ref[b])) * SCALE
        update = dot(mix.astype(BF), half_b[...])
        cos, sin = cos_ref[b], sin_ref[b]
        for c in blocks_of(width):
            query = base_ref[b, c] + update[:, c]
            other = pltpu.roll(query, HEAD // 2, 1)
            out[b, c] = (query * cos + other * sin).astype(BF)
        copies.append(pltpu.make_async_copy(out.at[b], q_hbm.at[b], sems.at[2 + i]))
        copies[-1].start()
    for copy in copies:
        copy.wait()


def keep_hbm(x):
    return pltpu.with_memory_space_constraint(x, pltpu.HBM)


def call(kernel, outs, in_specs, args, name, scratch=(), out_specs=None, limit=16, aliases=None):
    return pl.pallas_call(
        kernel,
        out_shape=outs,
        in_specs=in_specs,
        out_specs=out_specs if out_specs is not None else jax.tree.map(lambda _: VMEM, outs),
        scratch_shapes=list(scratch),
        compiler_params=pltpu.CompilerParams(vmem_limit_bytes=int(limit * 1024 * 1024)),
        input_output_aliases=aliases or {},
        name=name,
    )(*args)


def turn_tables(places, steps):
    half = HEAD // 2
    freq = 10000.0 ** (-jnp.arange(half, dtype=F32) / half)
    cos, sin = [], []
    for step in range(steps):
        angle = (places + float(step))[:, None] * freq[None, :]
        c, s = jnp.cos(angle), jnp.sin(angle)
        cos.append(jnp.concatenate([c, c], axis=-1))
        sin.append(jnp.concatenate([-s, s], axis=-1))
    return jnp.concatenate(cos), jnp.concatenate(sin)


def bits_of(n):
    return [b for b in range(n.bit_length() - 1)]


def build(n_dp, n_roll, n_tp):
    z_bits = [("roll", b) for b in bits_of(n_roll)]
    x_bits = [("dp", b) for b in bits_of(n_dp)]
    sizes = {"dp": n_dp, "roll": n_roll}

    def cross(x, axis, bit):
        return swap(x, axis, sizes[axis], 1 << bit)

    def path(down, across):
        ways = down + across + down[::-1]
        after = [("halve",) + way for way in down[1:]] + [("sum", None, None)] * (1 + len(across))
        return list(zip(ways, after + [("join",) + way for way in down[::-1]]))

    path_a, path_b = path(z_bits, x_bits), path(x_bits + z_bits, [])
    whole_b = len(x_bits + z_bits) - 1
    path_b = [
        (way, ("norm", None, None) if i == whole_b else ("join_norm",) + step[1:] if whole_b < i < len(path_a) else step)
        for i, (way, step) in enumerate(path_b)
    ]

    def others(x, axis, bit):
        pairs = lambda kx, kz: [
            (i, ((i // n_roll) ^ kx) * n_roll + ((i % n_roll) ^ kz)) for i in range(n_dp * n_roll)
        ]
        return [lax.ppermute(x, ("dp", "roll"), pairs(kx, kz)) for kz in (0, 1 << bit) for kx in range(1, n_dp)]

    def on_device(
        train_inputs, train_cotangent, factor_a, factor_b, base_weight, incoming, norm_gain, positions
    ):
        steps, rows, width = incoming.shape
        tokens = train_inputs.shape[0]
        rank = factor_a.shape[1]
        count = steps * rows
        dma = lambda n: pltpu.SemaphoreType.DMA((n,))
        vmem = lambda n, dtype=F32: pltpu.VMEM((n, rank), dtype)

        part = call(
            rank_kernel,
            shape((2 * tokens, rank), BF),
            [HBM] * 4,
            tuple(map(keep_hbm, (train_inputs, train_cotangent, factor_a, factor_b))),
            "rank",
            [pltpu.VMEM(train_inputs.shape, BF), pltpu.VMEM(train_inputs.shape, BF),
             pltpu.VMEM(factor_a.shape, F32), pltpu.VMEM(factor_b.shape, F32), dma(4)],
        )
        part_got = swap(part, "tp", n_tp, 1)
        cut = 512
        wide = shape((count + EXTRA, width + rank), BF)
        tall = shape((count, width), BF)
        gained, pack = call(
            prep_kernel,
            [tall, shape((count + EXTRA, rank), BF)],
            [HBM] * 3,
            tuple(map(keep_hbm, (incoming.reshape(count, width), norm_gain[None, :], factor_a))),
            "prep",
            [pltpu.VMEM((count, width), BF), pltpu.VMEM((1, width), F32), pltpu.VMEM(factor_a.shape, F32),
             dma(2 + count // LANES)],
        )
        part_sum = call(part_kernel, shape(part.shape, BF), [VMEM] * 2 + [ANY], (part, part_got, pack), "part_sum")
        part_far = swap(part_sum, "tp", n_tp, 2)

        def query(peers, outs, after, name):
            blocks = len(peers) * width // cut
            return call(
                functools.partial(query_kernel, peers),
                outs,
                [VMEM, HBM, VMEM, ANY],
                (gained, keep_hbm(base_weight), pack, after),
                name,
                [pltpu.VMEM((blocks, width, cut), BF), dma(blocks)],
            )

        diag, distant = query((3, 2), [wide, tall], part_sum, "query_far")
        half = width // 2
        keep_a, send_a, keep_b, send_b, diag = call(
            functools.partial(grad_kernel, (path_a[0][0], path_b[0][0])),
            [shape((half, rank), F32), shape((half, rank), BF)] * 2 + [wide],
            [VMEM] * 4 + [ANY],
            (train_inputs, train_cotangent, part_sum, part_far, diag),
            "grads",
            [vmem(width), vmem(width)],
            out_specs=[VMEM] * 4 + [ANY],
            aliases={4: 4},
        )
        diag_got = swap(diag, "tp", n_tp, 1)
        (beside,) = query((1,), [tall], send_a, "query_beside")
        far, beside = call(
            far_kernel,
            [wide, tall],
            [VMEM] * 3 + [ANY] * 2,
            (distant, diag, diag_got, send_a, beside),
            "far",
            out_specs=[VMEM, ANY],
            aliases={4: 1},
        )
        far_got = swap(far, "tp", n_tp, 2)
        beside_got = swap(beside, "tp", n_tp, 1)
        def step_call(parts, after, name):
            ins, outs, scratch = [], [], []
            for (kind, _, _), arrays in parts:
                size = arrays[0].shape[0]
                ins += arrays
                if kind == "halve":
                    outs += [shape((size // 2, rank), F32), shape((size // 2, rank), BF)]
                    scratch.append(vmem(size))
                elif kind == "norm":
                    outs += [shape((size + EXTRA, rank), BF), shape((EXTRA, rank), BF)]
                else:
                    size = {"sum": size, "join": 2 * size, "join_norm": 2 * size - EXTRA}[kind]
                    outs.append(shape((size, rank), BF))
            made = list(
                call(
                    functools.partial(step_kernel, [(step, len(arrays)) for step, arrays in parts]),
                    outs,
                    [VMEM] * len(ins) + [ANY],
                    (*ins, after),
                    name,
                    scratch,
                )
            )
            return [[made.pop(0) for _ in range(1 + (step[0] in ("halve", "norm")))] for step, _ in parts]

        state_a, state_b, sums = [keep_a, send_a], [keep_b, send_b], []
        for i, ((way_a, step_a), (way_b, step_b)) in enumerate(zip(path_a[:-1], path_b)):
            arrays_a = [state_a[0], cross(state_a[-1], *way_a)]
            arrays_b = [state_b[0], cross(state_b[-1], *way_b)] + sums
            after = far if i == 0 else close if i == 1 else sin if i == 2 else far
            state_a, state_b = step_call([(step_a, arrays_a), (step_b, arrays_b)], after, f"step_{i}")
            sums = []
            if step_b[0] == "norm":
                sums = others(state_b.pop(), *path_b[i + 1][0])
            if i == 0:
                (close,) = query((0,), [tall], state_a[-1], "query_close")
            if i == 1:
                pos = positions.reshape(-1, LANES)
                places = call(place_kernel, shape(pos.shape, F32), [VMEM, ANY], (pos, state_a[-1]), "places")
                cos, sin = turn_tables(places.reshape(rows), steps)
        way = path_a[-1][0]
        mine_a, mine_b = state_a[-1], state_b[-1]
        got_a, got_b = cross(mine_a, *way), cross(mine_b, *way)
        step_pack, grad_a, mine_b = call(
            functools.partial(low_kernel, *way),
            [shape((count + EXTRA, rank), BF), shape((width, rank), BF), shape((2 * (mine_b.shape[0] - EXTRA), rank), BF)],
            [VMEM] * 5,
            (gained, mine_a, got_a, mine_b, got_b),
            "low_rank",
        )
        step_got = swap(step_pack, "tp", n_tp, 1)
        step_sum = call(merge_kernel, shape((count + EXTRA, rank), BF), [VMEM] * 2, (step_pack, step_got), "merge")
        step_far = swap(step_sum, "tp", n_tp, 2)

        for (axis, bit), step in path_b[len(path_a) : -1]:
            ((mine_b,),) = step_call([(step, [mine_b, cross(mine_b, axis, bit)])], step_pack, "join_b")
        got_b = cross(mine_b, *path_b[-1][0])

        base, low, scale = call(
            base_kernel,
            [shape((count, width), F32), shape((count, rank), F32), shape((count, LANES), F32)],
            [VMEM] * 4 + [ANY],
            (close, beside_got, far, far_got, step_sum),
            "base",
        )
        new_a, new_b, queries = call(
            functools.partial(final_kernel, *path_b[-1][0]),
            [shape((width, rank), F32), shape((rank, width), F32), tall],
            [VMEM] * 12,
            (base, low, scale, step_sum, step_far, grad_a, mine_b, got_b, factor_a, factor_b, cos, sin),
            "final",
            [vmem(width, BF), pltpu.VMEM((width, rank), F32), pltpu.VMEM((rank, width), F32),
             pltpu.VMEM((rank, width), BF), pltpu.VMEM((count, width), BF), dma(2 + count // LANES)],
            [HBM] * 3,
        )
        return new_a, new_b, queries.reshape(steps, rows, width)

    return on_device


def solution(mesh):
    n_dp, n_roll, n_tp = (mesh.shape[a] for a in ("dp", "roll", "tp"))
    return jax.shard_map(
        build(n_dp, n_roll, n_tp),
        mesh=mesh,
        in_specs=(
            P(("dp", "roll"), "tp"),
            P(("dp", "roll"), "tp"),
            P("tp", None),
            P(None, "tp"),
            P("tp", None),
            P(None, ("dp", "roll"), "tp"),
            P("tp"),
            P(("dp", "roll")),
        ),
        out_specs=(P("tp", None), P(None, "tp"), P(None, ("dp", "roll"), "tp")),
        check_vma=False,
    )
```

```python
import functools

import jax
import jax.numpy as jnp
from jax import lax
from jax.experimental import pallas as pl
from jax.experimental.pallas import tpu as pltpu
from jax.sharding import PartitionSpec as P

D = 4096
HEAD = 128
SCALE = 2.0
LEARN = 3.0
EPS = 1e-05
NORM_EPS = 1e-06
LANES = 128
EXTRA = 32

BF = jnp.bfloat16
F32 = jnp.float32
VMEM = pl.BlockSpec(memory_space=pltpu.VMEM)
ANY = pl.BlockSpec(memory_space=pl.ANY)
HBM = pl.BlockSpec(memory_space=pltpu.HBM)


def shape(dims, dtype):
    return jax.ShapeDtypeStruct(dims, dtype)


def dot(a, b, dims=((1,), (0,))):
    return lax.dot_general(a, b, (dims, ((), ())), preferred_element_type=F32)


def swap(x, axis, n, k):
    return lax.ppermute(x, axis, [(i, i ^ k) for i in range(n)])


def split_terms(values):
    high = values.astype(BF)
    rest = values - high.astype(F32)
    middle = rest.astype(BF)
    last = (rest - middle.astype(F32)).astype(BF)
    return jnp.concatenate([high, middle, last, jnp.zeros_like(last)], axis=0)


def join_terms(terms):
    x = terms.astype(F32)
    return (x[0:8] + x[8:16]) + x[16:24]


def fetch(sources, targets, sems):
    copies = [pltpu.make_async_copy(s, t, sems.at[i]) for i, (s, t) in enumerate(zip(sources, targets))]
    for copy in copies:
        copy.start()
    return copies


def blocks_of(count):
    return [slice(i, i + LANES) for i in range(0, count, LANES)]


def rank_kernel(x_hbm, v_hbm, a_hbm, b_hbm, out_ref, x_ref, v_ref, a_ref, b_ref, sems):
    copies = fetch((x_hbm, a_hbm, v_hbm, b_hbm), (x_ref, a_ref, v_ref, b_ref), sems)
    count = x_ref.shape[0]
    copies[0].wait()
    copies[1].wait()
    out_ref[:count] = dot(x_ref[...], a_ref[...].astype(BF)).astype(BF)
    copies[2].wait()
    copies[3].wait()
    out_ref[count:] = dot(v_ref[...], b_ref[...].astype(BF), ((1,), (1,))).astype(BF)


def weight_blocks(peers, w_hbm, w_ref):
    _, width, cut = w_ref.shape
    mine = lax.axis_index("tp")
    sources = []
    for peer in peers:
        for i in range(width // cut):
            start = (mine ^ peer) * width + i * cut
            sources.append(w_hbm.at[:, pl.ds(pl.multiple_of(start, cut), cut)])
    return sources, [w_ref.at[i] for i in range(len(sources))]


def prep_kernel(h_hbm, gain_hbm, a_hbm, hg_ref, pack_ref, h_ref, gain_ref, a_ref, sems):
    count, width = h_ref.shape
    blocks = blocks_of(count)
    copies = fetch(
        [gain_hbm] + [h_hbm.at[b] for b in blocks] + [a_hbm],
        [gain_ref] + [h_ref.at[b] for b in blocks] + [a_ref],
        sems,
    )
    copies[0].wait()
    rows = []
    for i, b in enumerate(blocks):
        copies[1 + i].wait()
        wide = h_ref[b].astype(F32)
        hg_ref[b] = (wide * gain_ref[...]).astype(BF)
        sums = jnp.sum(wide * wide, axis=-1, keepdims=True)
        rows.append(jnp.broadcast_to(sums, (LANES, LANES)).T[0:1])
    if len(rows) < 8:
        rows.append(jnp.zeros((8 - len(rows), LANES), F32))
    pack_ref[count:] = split_terms(jnp.concatenate(rows, axis=0))
    copies[-1].wait()
    pack_ref[:count] = dot(hg_ref[...], a_ref[...].astype(BF)).astype(BF)


def part_kernel(x_ref, got_ref, after_ref, out_ref):
    sum_kernel(x_ref, got_ref, out_ref)


def query_kernel(peers, hg_ref, w_hbm, pack_ref, after_ref, *rest):
    outs, (w_ref, sems) = rest[:-2], rest[-2:]
    _, width, cut = w_ref.shape
    copies = fetch(*weight_blocks(peers, w_hbm, w_ref), sems)
    count = hg_ref.shape[0]
    if outs[0].shape[0] > count:
        outs[0][count:, :width] = jnp.zeros((EXTRA, width), BF)
        outs[0][:, width:] = pack_ref[...]
    per = width // cut
    for i, copy in enumerate(copies):
        copy.wait()
        block = dot(hg_ref[...], w_ref[i]).astype(BF)
        outs[i // per][:count, i % per * cut : (i % per + 1) * cut] = block


def far_kernel(mine_ref, diag_ref, got_ref, after_ref, out_ref):
    count, width = mine_ref.shape
    out_ref[:count, :width] = (mine_ref[...].astype(F32) + got_ref[:count, :width].astype(F32)).astype(BF)
    out_ref[count:, :width] = jnp.zeros((EXTRA, width), BF)
    out_ref[:count, width:] = (diag_ref[:count, width:].astype(F32) + got_ref[:count, width:].astype(F32)).astype(BF)
    out_ref[count:, width:] = split_terms(join_terms(diag_ref[count:, width:]) + join_terms(got_ref[count:, width:]))


def merge_kernel(a_ref, b_ref, out_ref):
    count = a_ref.shape[0] - EXTRA
    out_ref[:count] = (a_ref[:count].astype(F32) + b_ref[:count].astype(F32)).astype(BF)
    out_ref[count:] = split_terms(join_terms(a_ref[count:]) + join_terms(b_ref[count:]))


def halves(axis, bit, size):
    mine = lax.rem(lax.axis_index(axis) // (1 << bit), 2) * size
    return pl.ds(pl.multiple_of(mine, size), size), pl.ds(pl.multiple_of(size - mine, size), size)


def halve(axis, bit, total_ref, keep_ref, send_ref):
    mine, other = halves(axis, bit, keep_ref.shape[0])
    keep_ref[...] = total_ref[mine]
    send_ref[...] = total_ref[other].astype(BF)


def join(axis, bit, mine_ref, got_ref, out_ref):
    mine, other = halves(axis, bit, mine_ref.shape[0])
    out_ref[mine] = mine_ref[...]
    out_ref[other] = got_ref[...]


def grad_kernel(axes, x_ref, v_ref, s_ref, r_ref, pass_ref, keep_a, send_a, keep_b, send_b, pass_out, ga, gb):
    count, width = x_ref.shape
    low = (s_ref[...].astype(F32) + r_ref[...].astype(F32)).astype(BF)
    ga[...] = SCALE * dot(x_ref[...], low[count:], ((0,), (0,)))
    halve(*axes[0], ga, keep_a, send_a)
    turned = SCALE * dot(low[:count], v_ref[...], ((0,), (0,)))
    for b in blocks_of(width):
        gb[b] = turned[:, b]
    halve(*axes[1], gb, keep_b, send_b)


def sum_kernel(keep_ref, got_ref, out_ref):
    out_ref[...] = (keep_ref[...].astype(F32) + got_ref[...].astype(F32)).astype(BF)


def halved(plan):
    return sum(step[0] == "halve" for step in plan)


def step_kernel(plan, *refs):
    ins, outs = list(refs[: 2 * len(plan)]), list(refs[2 * len(plan) :])
    waits, passed = plan[0][3]
    outs = outs[waits + passed :]
    outs = outs[: len(outs) - passed - halved(plan)] + outs[len(outs) - halved(plan) :]
    for kind, axis, bit, _ in plan:
        mine, got = ins.pop(0), ins.pop(0)
        if kind == "halve":
            total = outs.pop()
            total[...] = mine[...] + got[...].astype(F32)
            halve(axis, bit, total, outs.pop(0), outs.pop(0))
        elif kind == "sum":
            sum_kernel(mine, got, outs.pop(0))
        else:
            join(axis, bit, mine, got, outs.pop(0))


def place_kernel(pos_ref, after_ref, out_ref):
    out_ref[...] = pos_ref[...].astype(F32)


def square_sum(ref):
    x = ref[...].astype(F32)
    return jnp.broadcast_to(jnp.sum(x * x), (8, LANES))


def low_kernel(axis, bit, hg_ref, mine_a, got_a, mine_b, got_b, pack_ref, ga_ref, gb_ref):
    join(axis, bit, mine_a, got_a, ga_ref)
    count = hg_ref.shape[0]
    pack_ref[:count] = dot(hg_ref[...], ga_ref[...]).astype(BF)
    pack_ref[count:] = split_terms(square_sum(ga_ref))
    join(axis, bit, mine_b, got_b, gb_ref)


def norm_kernel(axis, bit, mine_b, got_b, gb_ref, norm_ref):
    join(axis, bit, mine_b, got_b, gb_ref)
    norm_ref[...] = split_terms(square_sum(gb_ref))


def norm_merge_kernel(a_ref, b_ref, out_ref):
    out_ref[...] = split_terms(join_terms(a_ref[...]) + join_terms(b_ref[...]))


def base_kernel(mine_ref, near_ref, far_ref, far_got, after_ref, base_ref, low_ref, scale_ref):
    count, width = mine_ref.shape
    sums = join_terms(far_ref[count:, width:]) + join_terms(far_got[count:, width:])
    scale = lax.rsqrt(sums / D + EPS)
    for i, b in enumerate(blocks_of(count)):
        block = jnp.broadcast_to(scale[i : i + 1], (LANES, LANES)).T
        scale_ref[b] = block
        low_ref[b] = (far_ref[b, width:].astype(F32) + far_got[b, width:].astype(F32)) * block
        for c in blocks_of(width):
            total = mine_ref[b, c].astype(F32) + near_ref[b, c].astype(F32) + far_got[b, c].astype(F32)
            base_ref[b, c] = total * block


def final_kernel(
    base_ref, low_ref, scale_ref, s_ref, r_ref, sn_ref, rn_ref, ga_ref, gb_ref, a_ref, b_ref, cos_ref, sin_ref,
    a_hbm, b_hbm, q_hbm, new_a, new_b, half_b, out, sems,
):
    count, width = base_ref.shape
    total = join_terms(s_ref[count:]) + join_terms(r_ref[count:])
    total = total + (join_terms(sn_ref[...]) + join_terms(rn_ref[...]))
    rate = (LEARN * lax.rsqrt(total + NORM_EPS))[0:1]
    for c in blocks_of(width):
        fresh = b_ref[:, c] - rate * gb_ref[c].astype(F32)
        new_b[:, c] = fresh
        half_b[:, c] = fresh.astype(BF)
    copies = [pltpu.make_async_copy(new_b, b_hbm, sems.at[0])]
    copies[-1].start()
    new_a[...] = a_ref[...] - rate * ga_ref[...].astype(F32)
    copies.append(pltpu.make_async_copy(new_a, a_hbm, sems.at[1]))
    copies[-1].start()
    for i, b in enumerate(blocks_of(count)):
        low = s_ref[b].astype(F32) + r_ref[b].astype(F32)
        mix = (low_ref[b] - rate * (low * scale_ref[b])) * SCALE
        update = dot(mix.astype(BF), half_b[...])
        cos, sin = cos_ref[b], sin_ref[b]
        for c in blocks_of(width):
            query = base_ref[b, c] + update[:, c]
            other = pltpu.roll(query, HEAD // 2, 1)
            out[b, c] = (query * cos + other * sin).astype(BF)
        copies.append(pltpu.make_async_copy(out.at[b], q_hbm.at[b], sems.at[2 + i]))
        copies[-1].start()
    for copy in copies:
        copy.wait()


def keep_hbm(x):
    return pltpu.with_memory_space_constraint(x, pltpu.HBM)


def call(kernel, outs, in_specs, args, name, scratch=(), out_specs=None, limit=16, aliases=None):
    return pl.pallas_call(
        kernel,
        out_shape=outs,
        in_specs=in_specs,
        out_specs=out_specs if out_specs is not None else jax.tree.map(lambda _: VMEM, outs),
        scratch_shapes=list(scratch),
        compiler_params=pltpu.CompilerParams(vmem_limit_bytes=int(limit * 1024 * 1024)),
        input_output_aliases=aliases or {},
        name=name,
    )(*args)


def turn_tables(places, steps):
    half = HEAD // 2
    freq = 10000.0 ** (-jnp.arange(half, dtype=F32) / half)
    cos, sin = [], []
    for step in range(steps):
        angle = (places + float(step))[:, None] * freq[None, :]
        c, s = jnp.cos(angle), jnp.sin(angle)
        cos.append(jnp.concatenate([c, c], axis=-1))
        sin.append(jnp.concatenate([-s, s], axis=-1))
    return jnp.concatenate(cos), jnp.concatenate(sin)


def bits_of(n):
    return [b for b in range(n.bit_length() - 1)]


def build(n_dp, n_roll, n_tp):
    z_bits = [("roll", b) for b in bits_of(n_roll)]
    x_bits = [("dp", b) for b in bits_of(n_dp)]
    sizes = {"dp": n_dp, "roll": n_roll}

    def cross(x, axis, bit):
        return swap(x, axis, sizes[axis], 1 << bit)

    def path(down, across):
        ways = down + across + down[::-1]
        after = [("halve",) + way for way in down[1:]] + [("sum", None, None)] * (1 + len(across))
        return list(zip(ways, after + [("join",) + way for way in down[::-1]]))

    path_a, path_b = path(z_bits, x_bits), path(x_bits + z_bits, [])

    def on_device(
        train_inputs, train_cotangent, factor_a, factor_b, base_weight, incoming, norm_gain, positions
    ):
        steps, rows, width = incoming.shape
        tokens = train_inputs.shape[0]
        rank = factor_a.shape[1]
        count = steps * rows
        dma = lambda n: pltpu.SemaphoreType.DMA((n,))
        vmem = lambda n, dtype=F32: pltpu.VMEM((n, rank), dtype)

        part = call(
            rank_kernel,
            shape((2 * tokens, rank), BF),
            [HBM] * 4,
            tuple(map(keep_hbm, (train_inputs, train_cotangent, factor_a, factor_b))),
            "rank",
            [pltpu.VMEM(train_inputs.shape, BF), pltpu.VMEM(train_inputs.shape, BF),
             pltpu.VMEM(factor_a.shape, F32), pltpu.VMEM(factor_b.shape, F32), dma(4)],
        )
        part_got = swap(part, "tp", n_tp, 1)
        cut = 512
        wide = shape((count + EXTRA, width + rank), BF)
        tall = shape((count, width), BF)
        gained, pack = call(
            prep_kernel,
            [tall, shape((count + EXTRA, rank), BF)],
            [HBM] * 3,
            tuple(map(keep_hbm, (incoming.reshape(count, width), norm_gain[None, :], factor_a))),
            "prep",
            [pltpu.VMEM((count, width), BF), pltpu.VMEM((1, width), F32), pltpu.VMEM(factor_a.shape, F32),
             dma(2 + count // LANES)],
        )
        part_sum = call(part_kernel, shape(part.shape, BF), [VMEM] * 2 + [ANY], (part, part_got, pack), "part_sum")
        part_far = swap(part_sum, "tp", n_tp, 2)

        def query(peers, outs, after, name):
            blocks = len(peers) * width // cut
            return call(
                functools.partial(query_kernel, peers),
                outs,
                [VMEM, HBM, VMEM, ANY],
                (gained, keep_hbm(base_weight), pack, after),
                name,
                [pltpu.VMEM((blocks, width, cut), BF), dma(blocks)],
            )

        diag, distant = query((3, 2), [wide, tall], part_sum, "query_far")
        half = width // 2
        keep_a, send_a, keep_b, send_b, diag = call(
            functools.partial(grad_kernel, (path_a[0][0], path_b[0][0])),
            [shape((half, rank), F32), shape((half, rank), BF)] * 2 + [wide],
            [VMEM] * 4 + [ANY],
            (train_inputs, train_cotangent, part_sum, part_far, diag),
            "grads",
            [vmem(width), vmem(width)],
            out_specs=[VMEM] * 4 + [ANY],
            aliases={4: 4},
        )
        diag_got = swap(diag, "tp", n_tp, 1)
        far = call(far_kernel, wide, [VMEM] * 3 + [ANY], (distant, diag, diag_got, send_a), "far")
        far_got = swap(far, "tp", n_tp, 2)

        def step_call(parts, after, name, passed=()):
            ins, outs, scratch = [], [], []
            for step, (mine, got) in parts:
                size = mine.shape[0]
                ins += [mine, got]
                if step[0] == "halve":
                    outs += [shape((size // 2, rank), F32), shape((size // 2, rank), BF)]
                    scratch.append(vmem(size))
                else:
                    outs.append(shape((2 * size if step[0] == "join" else size, rank), BF))
            first = len(ins) + len(after)
            made = call(
                functools.partial(step_kernel, [step + ((len(after), len(passed)),) for step, _ in parts]),
                outs + [shape(x.shape, x.dtype) for x in passed],
                [VMEM] * len(ins) + [ANY] * (len(after) + len(passed)),
                (*ins, *after, *passed),
                name,
                scratch,
                [VMEM] * len(outs) + [ANY] * len(passed),
                aliases={first + i: len(outs) + i for i in range(len(passed))},
            )
            made = list(made)
            return [[made.pop(0) for _ in range(1 + (step[0] == "halve"))] for step, _ in parts] + made

        state_a, state_b, after, passed = [keep_a, send_a], [keep_b, send_b], [far], []
        for i, ((way_a, step_a), (way_b, step_b)) in enumerate(zip(path_a[:-1], path_b)):
            got_a, got_b = cross(state_a[-1], *way_a), cross(state_b[-1], *way_b)
            state_a, state_b, *made = step_call(
                [(step_a, (state_a[0], got_a)), (step_b, (state_b[0], got_b))], after, f"step_{i}", passed
            )
            after, passed = [], []
            if made:
                beside_got = swap(made[0], "tp", n_tp, 1)
            if i == 0:
                after = query((0,), [tall], state_a[-1], "query_close")
                (close,) = after
            if i == 1:
                pos = positions.reshape(-1, LANES)
                places = call(place_kernel, shape(pos.shape, F32), [VMEM, ANY], (pos, state_a[-1]), "places")
                after = list(turn_tables(places.reshape(rows), steps))
                cos, sin = after
            if i == 2:
                passed = query((1,), [tall], state_a[-1], "query_beside")
        way = path_a[-1][0]
        mine_a, mine_b = state_a[-1], state_b[-1]
        step_pack, grad_a, mine_b = call(
            functools.partial(low_kernel, *way),
            [shape((count + EXTRA, rank), BF), shape((width, rank), BF), shape((2 * mine_b.shape[0], rank), BF)],
            [VMEM] * 5,
            (gained, mine_a, cross(mine_a, *way), mine_b, cross(mine_b, *way)),
            "low_rank",
        )
        step_got = swap(step_pack, "tp", n_tp, 1)
        step_sum = call(merge_kernel, shape((count + EXTRA, rank), BF), [VMEM] * 2, (step_pack, step_got), "merge")
        step_far = swap(step_sum, "tp", n_tp, 2)

        for way_b, step_b in path_b[len(path_a) : -1]:
            ((mine_b,),) = step_call([(step_b, (mine_b, cross(mine_b, *way_b)))], [], "join_b")
        way = path_b[-1][0]
        grad_b, norm = call(
            functools.partial(norm_kernel, *way),
            [shape((width, rank), BF), shape((EXTRA, LANES), BF)],
            [VMEM] * 2,
            (mine_b, cross(mine_b, *way)),
            "norm",
        )
        norm = call(
            norm_merge_kernel, shape((EXTRA, LANES), BF), [VMEM] * 2, (norm, swap(norm, "tp", n_tp, 1)), "norm_merge"
        )
        norm_far = swap(norm, "tp", n_tp, 2)
        base, low, scale = call(
            base_kernel,
            [shape((count, width), F32), shape((count, rank), F32), shape((count, LANES), F32)],
            [VMEM] * 4 + [ANY],
            (close, beside_got, far, far_got, step_sum),
            "base",
        )
        new_a, new_b, queries = call(
            final_kernel,
            [shape((width, rank), F32), shape((rank, width), F32), tall],
            [VMEM] * 13,
            (base, low, scale, step_sum, step_far, norm, norm_far, grad_a, grad_b, factor_a, factor_b, cos, sin),
            "final",
            [pltpu.VMEM((width, rank), F32), pltpu.VMEM((rank, width), F32),
             pltpu.VMEM((rank, width), BF), pltpu.VMEM((count, width), BF), dma(2 + count // LANES)],
            [HBM] * 3,
        )
        return new_a, new_b, queries.reshape(steps, rows, width)

    return on_device


def solution(mesh):
    n_dp, n_roll, n_tp = (mesh.shape[a] for a in ("dp", "roll", "tp"))
    return jax.shard_map(
        build(n_dp, n_roll, n_tp),
        mesh=mesh,
        in_specs=(
            P(("dp", "roll"), "tp"),
            P(("dp", "roll"), "tp"),
            P("tp", None),
            P(None, "tp"),
            P("tp", None),
            P(None, ("dp", "roll"), "tp"),
            P("tp"),
            P(("dp", "roll")),
        ),
        out_specs=(P("tp", None), P(None, "tp"), P(None, ("dp", "roll"), "tp")),
        check_vma=False,
    )
```

```python
import functools

import jax
import jax.numpy as jnp
from jax import lax
from jax.experimental import pallas as pl
from jax.experimental.pallas import tpu as pltpu
from jax.sharding import PartitionSpec as P

D = 4096
HEAD = 128
SCALE = 2.0
LEARN = 3.0
EPS = 1e-05
NORM_EPS = 1e-06
LANES = 128
EXTRA = 32

BF = jnp.bfloat16
F32 = jnp.float32
VMEM = pl.BlockSpec(memory_space=pltpu.VMEM)
ANY = pl.BlockSpec(memory_space=pl.ANY)
HBM = pl.BlockSpec(memory_space=pltpu.HBM)


def shape(dims, dtype):
    return jax.ShapeDtypeStruct(dims, dtype)


def dot(a, b, dims=((1,), (0,))):
    return lax.dot_general(a, b, (dims, ((), ())), preferred_element_type=F32)


def swap(x, axis, n, k):
    return lax.ppermute(x, axis, [(i, i ^ k) for i in range(n)])


def split_terms(values):
    high = values.astype(BF)
    rest = values - high.astype(F32)
    middle = rest.astype(BF)
    last = (rest - middle.astype(F32)).astype(BF)
    return jnp.concatenate([high, middle, last, jnp.zeros_like(last)], axis=0)


def join_terms(terms):
    x = terms.astype(F32)
    return (x[0:8] + x[8:16]) + x[16:24]


def fetch(sources, targets, sems):
    copies = [pltpu.make_async_copy(s, t, sems.at[i]) for i, (s, t) in enumerate(zip(sources, targets))]
    for copy in copies:
        copy.start()
    return copies


def blocks_of(count):
    return [slice(i, i + LANES) for i in range(0, count, LANES)]


def rank_kernel(x_hbm, v_hbm, a_hbm, b_hbm, out_ref, x_ref, v_ref, a_ref, b_ref, sems):
    copies = fetch((x_hbm, a_hbm, v_hbm, b_hbm), (x_ref, a_ref, v_ref, b_ref), sems)
    count = x_ref.shape[0]
    copies[0].wait()
    copies[1].wait()
    out_ref[:count] = dot(x_ref[...], a_ref[...].astype(BF)).astype(BF)
    copies[2].wait()
    copies[3].wait()
    out_ref[count:] = dot(v_ref[...], b_ref[...].astype(BF), ((1,), (1,))).astype(BF)


def weight_blocks(peers, w_hbm, w_ref):
    _, width, cut = w_ref.shape
    mine = lax.axis_index("tp")
    sources = []
    for peer in peers:
        for i in range(width // cut):
            start = (mine ^ peer) * width + i * cut
            sources.append(w_hbm.at[:, pl.ds(pl.multiple_of(start, cut), cut)])
    return sources, [w_ref.at[i] for i in range(len(sources))]


def prep_kernel(h_hbm, gain_hbm, a_hbm, hg_ref, pack_ref, h_ref, gain_ref, a_ref, sems):
    count, width = h_ref.shape
    blocks = blocks_of(count)
    copies = fetch(
        [gain_hbm] + [h_hbm.at[b] for b in blocks] + [a_hbm],
        [gain_ref] + [h_ref.at[b] for b in blocks] + [a_ref],
        sems,
    )
    copies[0].wait()
    rows = []
    for i, b in enumerate(blocks):
        copies[1 + i].wait()
        wide = h_ref[b].astype(F32)
        hg_ref[b] = (wide * gain_ref[...]).astype(BF)
        sums = jnp.sum(wide * wide, axis=-1, keepdims=True)
        rows.append(jnp.broadcast_to(sums, (LANES, LANES)).T[0:1])
    if len(rows) < 8:
        rows.append(jnp.zeros((8 - len(rows), LANES), F32))
    pack_ref[count:] = split_terms(jnp.concatenate(rows, axis=0))
    copies[-1].wait()
    pack_ref[:count] = dot(hg_ref[...], a_ref[...].astype(BF)).astype(BF)


def part_kernel(x_ref, got_ref, after_ref, out_ref):
    sum_kernel(x_ref, got_ref, out_ref)


def query_kernel(peers, hg_ref, w_hbm, pack_ref, after_ref, *rest):
    outs, (w_ref, sems) = rest[:-2], rest[-2:]
    _, width, cut = w_ref.shape
    copies = fetch(*weight_blocks(peers, w_hbm, w_ref), sems)
    count = hg_ref.shape[0]
    if outs[0].shape[0] > count:
        outs[0][count:, :width] = jnp.zeros((EXTRA, width), BF)
        outs[0][:, width:] = pack_ref[...]
    per = width // cut
    for i, copy in enumerate(copies):
        copy.wait()
        block = dot(hg_ref[...], w_ref[i]).astype(BF)
        outs[i // per][:count, i % per * cut : (i % per + 1) * cut] = block


def far_kernel(mine_ref, diag_ref, got_ref, after_ref, out_ref):
    count, width = mine_ref.shape
    out_ref[:count, :width] = (mine_ref[...].astype(F32) + got_ref[:count, :width].astype(F32)).astype(BF)
    out_ref[count:, :width] = jnp.zeros((EXTRA, width), BF)
    out_ref[:count, width:] = (diag_ref[:count, width:].astype(F32) + got_ref[:count, width:].astype(F32)).astype(BF)
    out_ref[count:, width:] = split_terms(join_terms(diag_ref[count:, width:]) + join_terms(got_ref[count:, width:]))


def merge_kernel(a_ref, b_ref, out_ref):
    count = a_ref.shape[0] - EXTRA
    out_ref[:count] = (a_ref[:count].astype(F32) + b_ref[:count].astype(F32)).astype(BF)
    out_ref[count:] = split_terms(join_terms(a_ref[count:]) + join_terms(b_ref[count:]))


def halves(axis, bit, size):
    mine = lax.rem(lax.axis_index(axis) // (1 << bit), 2) * size
    return pl.ds(pl.multiple_of(mine, size), size), pl.ds(pl.multiple_of(size - mine, size), size)


def halve(axis, bit, total_ref, keep_ref, send_ref):
    mine, other = halves(axis, bit, keep_ref.shape[0])
    keep_ref[...] = total_ref[mine]
    send_ref[...] = total_ref[other].astype(BF)


def join(axis, bit, mine_ref, got_ref, out_ref):
    mine, other = halves(axis, bit, mine_ref.shape[0])
    out_ref[mine] = mine_ref[...]
    out_ref[other] = got_ref[...]


def grad_kernel(axes, x_ref, v_ref, s_ref, r_ref, pass_ref, keep_a, send_a, keep_b, send_b, pass_out, ga, gb):
    count, width = x_ref.shape
    low = (s_ref[...].astype(F32) + r_ref[...].astype(F32)).astype(BF)
    ga[...] = SCALE * dot(x_ref[...], low[count:], ((0,), (0,)))
    halve(*axes[0], ga, keep_a, send_a)
    turned = SCALE * dot(low[:count], v_ref[...], ((0,), (0,)))
    for b in blocks_of(width):
        gb[b] = turned[:, b]
    halve(*axes[1], gb, keep_b, send_b)


def sum_kernel(keep_ref, got_ref, out_ref):
    out_ref[...] = (keep_ref[...].astype(F32) + got_ref[...].astype(F32)).astype(BF)


def step_kernel(waits, mine_a, got_a, mine_b, got_b, *refs):
    sum_a, sum_b = refs[waits : waits + 2]
    sum_kernel(mine_a, got_a, sum_a)
    sum_kernel(mine_b, got_b, sum_b)


def place_kernel(pos_ref, after_ref, out_ref):
    out_ref[...] = pos_ref[...].astype(F32)


def square_sum(ref):
    x = ref[...].astype(F32)
    return jnp.broadcast_to(jnp.sum(x * x), (8, LANES))


def low_kernel(way_a, way_b, hg_ref, mine_a, got_a, mine_b, got_b, pack_ref, ga_ref, gb_ref):
    join(*way_a, mine_a, got_a, ga_ref)
    count = hg_ref.shape[0]
    pack_ref[:count] = dot(hg_ref[...], ga_ref[...]).astype(BF)
    join(*way_b, mine_b, got_b, gb_ref)
    pack_ref[count:] = split_terms(square_sum(ga_ref) + square_sum(gb_ref))


def base_kernel(mine_ref, near_ref, far_ref, far_got, after_ref, base_ref, low_ref, scale_ref):
    count, width = mine_ref.shape
    sums = join_terms(far_ref[count:, width:]) + join_terms(far_got[count:, width:])
    scale = lax.rsqrt(sums / D + EPS)
    for i, b in enumerate(blocks_of(count)):
        block = jnp.broadcast_to(scale[i : i + 1], (LANES, LANES)).T
        scale_ref[b] = block
        low_ref[b] = (far_ref[b, width:].astype(F32) + far_got[b, width:].astype(F32)) * block
        for c in blocks_of(width):
            total = mine_ref[b, c].astype(F32) + near_ref[b, c].astype(F32) + far_got[b, c].astype(F32)
            base_ref[b, c] = total * block


def final_kernel(
    base_ref, low_ref, scale_ref, s_ref, r_ref, ga_ref, gb_ref, a_ref, b_ref, cos_ref, sin_ref,
    a_hbm, b_hbm, q_hbm, new_a, new_b, half_b, out, sems,
):
    count, width = base_ref.shape
    total = join_terms(s_ref[count:]) + join_terms(r_ref[count:])
    rate = (LEARN * lax.rsqrt(total + NORM_EPS))[0:1]
    for c in blocks_of(width):
        fresh = b_ref[:, c] - rate * gb_ref[c].astype(F32)
        new_b[:, c] = fresh
        half_b[:, c] = fresh.astype(BF)
    copies = [pltpu.make_async_copy(new_b, b_hbm, sems.at[0])]
    copies[-1].start()
    new_a[...] = a_ref[...] - rate * ga_ref[...].astype(F32)
    copies.append(pltpu.make_async_copy(new_a, a_hbm, sems.at[1]))
    copies[-1].start()
    for i, b in enumerate(blocks_of(count)):
        low = s_ref[b].astype(F32) + r_ref[b].astype(F32)
        mix = (low_ref[b] - rate * (low * scale_ref[b])) * SCALE
        update = dot(mix.astype(BF), half_b[...])
        cos, sin = cos_ref[b], sin_ref[b]
        for c in blocks_of(width):
            query = base_ref[b, c] + update[:, c]
            other = pltpu.roll(query, HEAD // 2, 1)
            out[b, c] = (query * cos + other * sin).astype(BF)
        copies.append(pltpu.make_async_copy(out.at[b], q_hbm.at[b], sems.at[2 + i]))
        copies[-1].start()
    for copy in copies:
        copy.wait()


def keep_hbm(x):
    return pltpu.with_memory_space_constraint(x, pltpu.HBM)


def call(kernel, outs, in_specs, args, name, scratch=(), out_specs=None, limit=16, aliases=None):
    return pl.pallas_call(
        kernel,
        out_shape=outs,
        in_specs=in_specs,
        out_specs=out_specs if out_specs is not None else jax.tree.map(lambda _: VMEM, outs),
        scratch_shapes=list(scratch),
        compiler_params=pltpu.CompilerParams(vmem_limit_bytes=int(limit * 1024 * 1024)),
        input_output_aliases=aliases or {},
        name=name,
    )(*args)


def turn_tables(places, steps):
    half = HEAD // 2
    freq = 10000.0 ** (-jnp.arange(half, dtype=F32) / half)
    cos, sin = [], []
    for step in range(steps):
        angle = (places + float(step))[:, None] * freq[None, :]
        c, s = jnp.cos(angle), jnp.sin(angle)
        cos.append(jnp.concatenate([c, c], axis=-1))
        sin.append(jnp.concatenate([-s, s], axis=-1))
    return jnp.concatenate(cos), jnp.concatenate(sin)


def bits_of(n):
    return [b for b in range(n.bit_length() - 1)]


def build(n_dp, n_roll, n_tp):
    z_bits = [("roll", b) for b in bits_of(n_roll)]
    x_bits = [("dp", b) for b in bits_of(n_dp)]
    sizes = {"dp": n_dp, "roll": n_roll}

    def cross(x, axis, bit):
        return swap(x, axis, sizes[axis], 1 << bit)

    path_a, path_b = z_bits + x_bits + z_bits[:1], x_bits[:1] + z_bits + x_bits[1:] + x_bits[:1]

    def on_device(
        train_inputs, train_cotangent, factor_a, factor_b, base_weight, incoming, norm_gain, positions
    ):
        steps, rows, width = incoming.shape
        tokens = train_inputs.shape[0]
        rank = factor_a.shape[1]
        count = steps * rows
        dma = lambda n: pltpu.SemaphoreType.DMA((n,))
        vmem = lambda n, dtype=F32: pltpu.VMEM((n, rank), dtype)

        part = call(
            rank_kernel,
            shape((2 * tokens, rank), BF),
            [HBM] * 4,
            tuple(map(keep_hbm, (train_inputs, train_cotangent, factor_a, factor_b))),
            "rank",
            [pltpu.VMEM(train_inputs.shape, BF), pltpu.VMEM(train_inputs.shape, BF),
             pltpu.VMEM(factor_a.shape, F32), pltpu.VMEM(factor_b.shape, F32), dma(4)],
        )
        part_got = swap(part, "tp", n_tp, 1)
        cut = 512
        wide = shape((count + EXTRA, width + rank), BF)
        tall = shape((count, width), BF)
        gained, pack = call(
            prep_kernel,
            [tall, shape((count + EXTRA, rank), BF)],
            [HBM] * 3,
            tuple(map(keep_hbm, (incoming.reshape(count, width), norm_gain[None, :], factor_a))),
            "prep",
            [pltpu.VMEM((count, width), BF), pltpu.VMEM((1, width), F32), pltpu.VMEM(factor_a.shape, F32),
             dma(2 + count // LANES)],
        )
        part_sum = call(part_kernel, shape(part.shape, BF), [VMEM] * 2 + [ANY], (part, part_got, pack), "part_sum")
        part_far = swap(part_sum, "tp", n_tp, 2)

        def query(peers, outs, after, name):
            blocks = len(peers) * width // cut
            return call(
                functools.partial(query_kernel, peers),
                outs,
                [VMEM, HBM, VMEM, ANY],
                (gained, keep_hbm(base_weight), pack, after),
                name,
                [pltpu.VMEM((blocks, width, cut), BF), dma(blocks)],
            )

        diag, distant = query((3, 2), [wide, tall], part_sum, "query_far")
        half = width // 2
        keep_a, send_a, keep_b, send_b, diag = call(
            functools.partial(grad_kernel, (path_a[0], path_b[0])),
            [shape((half, rank), F32), shape((half, rank), BF)] * 2 + [wide],
            [VMEM] * 4 + [ANY],
            (train_inputs, train_cotangent, part_sum, part_far, diag),
            "grads",
            [vmem(width), vmem(width)],
            out_specs=[VMEM] * 4 + [ANY],
            aliases={4: 4},
        )
        diag_got = swap(diag, "tp", n_tp, 1)
        far = call(far_kernel, wide, [VMEM] * 3 + [ANY], (distant, diag, diag_got, send_a), "far")
        far_got = swap(far, "tp", n_tp, 2)

        (close,) = query((0,), [tall], far, "query_close")
        mine_a, mine_b, after, passed = keep_a, keep_b, [close], []
        for i, (way_a, way_b) in enumerate(zip(path_a[:-1], path_b[:-1])):
            got_a, got_b = cross(send_a, *way_a), cross(send_b, *way_b)
            mine_a, mine_b, *made = call(
                functools.partial(step_kernel, len(after) + len(passed)),
                [shape((half, rank), BF)] * 2 + [shape(x.shape, x.dtype) for x in passed],
                [VMEM] * 4 + [ANY] * (len(after) + len(passed)),
                (mine_a, got_a, mine_b, got_b, *after, *passed),
                f"step_{i}",
                out_specs=[VMEM] * 2 + [ANY] * len(passed),
                aliases={4 + len(after) + k: 2 + k for k in range(len(passed))},
            )
            send_a, send_b = mine_a, mine_b
            after, passed = [], []
            if made:
                beside_got = swap(made[0], "tp", n_tp, 1)
            if i == 0:
                passed = query((1,), [tall], mine_a, "query_beside")
                pos = positions.reshape(-1, LANES)
                places = call(place_kernel, shape(pos.shape, F32), [VMEM, ANY], (pos, mine_a), "places")
                cos, sin = turn_tables(places.reshape(rows), steps)
                after = [cos, sin]
        step_pack, grad_a, grad_b = call(
            functools.partial(low_kernel, path_a[-1], path_b[-1]),
            [shape((count + EXTRA, rank), BF), shape((width, rank), BF), shape((width, rank), BF)],
            [VMEM] * 5,
            (gained, mine_a, cross(mine_a, *path_a[-1]), mine_b, cross(mine_b, *path_b[-1])),
            "low_rank",
        )
        step_got = swap(step_pack, "tp", n_tp, 1)
        step_sum = call(merge_kernel, shape((count + EXTRA, rank), BF), [VMEM] * 2, (step_pack, step_got), "merge")
        step_far = swap(step_sum, "tp", n_tp, 2)

        base, low, scale = call(
            base_kernel,
            [shape((count, width), F32), shape((count, rank), F32), shape((count, LANES), F32)],
            [VMEM] * 4 + [ANY],
            (close, beside_got, far, far_got, step_sum),
            "base",
        )
        new_a, new_b, queries = call(
            final_kernel,
            [shape((width, rank), F32), shape((rank, width), F32), tall],
            [VMEM] * 11,
            (base, low, scale, step_sum, step_far, grad_a, grad_b, factor_a, factor_b, cos, sin),
            "final",
            [pltpu.VMEM((width, rank), F32), pltpu.VMEM((rank, width), F32),
             pltpu.VMEM((rank, width), BF), pltpu.VMEM((count, width), BF), dma(2 + count // LANES)],
            [HBM] * 3,
        )
        return new_a, new_b, queries.reshape(steps, rows, width)

    return on_device


def solution(mesh):
    n_dp, n_roll, n_tp = (mesh.shape[a] for a in ("dp", "roll", "tp"))
    return jax.shard_map(
        build(n_dp, n_roll, n_tp),
        mesh=mesh,
        in_specs=(
            P(("dp", "roll"), "tp"),
            P(("dp", "roll"), "tp"),
            P("tp", None),
            P(None, "tp"),
            P("tp", None),
            P(None, ("dp", "roll"), "tp"),
            P("tp"),
            P(("dp", "roll")),
        ),
        out_specs=(P("tp", None), P(None, "tp"), P(None, ("dp", "roll"), "tp")),
        check_vma=False,
    )
```

```python
import functools

import jax
import jax.numpy as jnp
from jax import lax
from jax.experimental import pallas as pl
from jax.experimental.pallas import tpu as pltpu
from jax.sharding import PartitionSpec as P

D = 4096
HEAD = 128
SCALE = 2.0
LEARN = 3.0
EPS = 1e-05
NORM_EPS = 1e-06
LANES = 128
EXTRA = 32

BF = jnp.bfloat16
F32 = jnp.float32
VMEM = pl.BlockSpec(memory_space=pltpu.VMEM)
ANY = pl.BlockSpec(memory_space=pl.ANY)
HBM = pl.BlockSpec(memory_space=pltpu.HBM)


def shape(dims, dtype):
    return jax.ShapeDtypeStruct(dims, dtype)


def dot(a, b, dims=((1,), (0,))):
    return lax.dot_general(a, b, (dims, ((), ())), preferred_element_type=F32)


def swap(x, axis, n, k):
    return lax.ppermute(x, axis, [(i, i ^ k) for i in range(n)])


def split_terms(values):
    high = values.astype(BF)
    rest = values - high.astype(F32)
    middle = rest.astype(BF)
    last = (rest - middle.astype(F32)).astype(BF)
    return jnp.concatenate([high, middle, last, jnp.zeros_like(last)], axis=0)


def join_terms(terms):
    x = terms.astype(F32)
    return (x[0:8] + x[8:16]) + x[16:24]


def fetch(sources, targets, sems):
    copies = [pltpu.make_async_copy(s, t, sems.at[i]) for i, (s, t) in enumerate(zip(sources, targets))]
    for copy in copies:
        copy.start()
    return copies


def blocks_of(count):
    return [slice(i, i + LANES) for i in range(0, count, LANES)]


def rank_kernel(x_hbm, v_hbm, a_hbm, b_hbm, h_hbm, out_ref, a16_ref, h_ref, x_ref, v_ref, a_ref, b_ref, sems):
    copies = fetch((x_hbm, a_hbm, v_hbm, b_hbm, h_hbm), (x_ref, a_ref, v_ref, b_ref, h_ref), sems)
    count = x_ref.shape[0]
    copies[1].wait()
    a16_ref[...] = a_ref[...].astype(BF)
    copies[0].wait()
    out_ref[:count] = dot(x_ref[...], a16_ref[...]).astype(BF)
    copies[3].wait()
    b16 = b_ref[...].astype(BF)
    copies[2].wait()
    out_ref[count:] = dot(v_ref[...], b16, ((1,), (1,))).astype(BF)
    copies[4].wait()


def weight_blocks(peers, w_hbm, w_ref):
    _, width, cut = w_ref.shape
    mine = lax.axis_index("tp")
    sources = []
    for peer in peers:
        for i in range(width // cut):
            start = (mine ^ peer) * width + i * cut
            sources.append(w_hbm.at[:, pl.ds(pl.multiple_of(start, cut), cut)])
    return sources, [w_ref.at[i] for i in range(len(sources))]


def prep_kernel(h_ref, gain_ref, a16_ref, hg_ref, pack_ref):
    count, width = h_ref.shape
    rows = []
    for b in blocks_of(count):
        wide = h_ref[b].astype(F32)
        hg_ref[b] = (wide * gain_ref[...]).astype(BF)
        sums = jnp.sum(wide * wide, axis=-1, keepdims=True)
        rows.append(jnp.broadcast_to(sums, (LANES, LANES)).T[0:1])
    if len(rows) < 8:
        rows.append(jnp.zeros((8 - len(rows), LANES), F32))
    pack_ref[count:] = split_terms(jnp.concatenate(rows, axis=0))
    pack_ref[:count] = dot(hg_ref[...], a16_ref[...]).astype(BF)


def part_kernel(x_ref, got_ref, after_ref, out_ref):
    sum_kernel(x_ref, got_ref, out_ref)


def query_kernel(peers, hg_ref, w_hbm, pack_ref, after_ref, *rest):
    outs, (w_ref, sems) = rest[:-2], rest[-2:]
    _, width, cut = w_ref.shape
    copies = fetch(*weight_blocks(peers, w_hbm, w_ref), sems)
    count = hg_ref.shape[0]
    if outs[0].shape[0] > count:
        outs[0][count:, :width] = jnp.zeros((EXTRA, width), BF)
        outs[0][:, width:] = pack_ref[...]
    per = width // cut
    for i, copy in enumerate(copies):
        copy.wait()
        block = dot(hg_ref[...], w_ref[i]).astype(BF)
        outs[i // per][:count, i % per * cut : (i % per + 1) * cut] = block


def far_kernel(mine_ref, diag_ref, got_ref, after_ref, pass_ref, out_ref, pass_out):
    count, width = mine_ref.shape
    out_ref[:count, :width] = (mine_ref[...].astype(F32) + got_ref[:count, :width].astype(F32)).astype(BF)
    out_ref[count:, :width] = jnp.zeros((EXTRA, width), BF)
    out_ref[:count, width:] = (diag_ref[:count, width:].astype(F32) + got_ref[:count, width:].astype(F32)).astype(BF)
    out_ref[count:, width:] = split_terms(join_terms(diag_ref[count:, width:]) + join_terms(got_ref[count:, width:]))


def merge_kernel(a_ref, b_ref, out_ref):
    count = a_ref.shape[0] - EXTRA
    out_ref[:count] = (a_ref[:count].astype(F32) + b_ref[:count].astype(F32)).astype(BF)
    out_ref[count:] = split_terms(join_terms(a_ref[count:]) + join_terms(b_ref[count:]))


def halves(axis, bit, size):
    mine = lax.rem(lax.axis_index(axis) // (1 << bit), 2) * size
    return pl.ds(pl.multiple_of(mine, size), size), pl.ds(pl.multiple_of(size - mine, size), size)


def halve(axis, bit, total_ref, keep_ref, send_ref):
    mine, other = halves(axis, bit, keep_ref.shape[0])
    keep_ref[...] = total_ref[mine]
    send_ref[...] = total_ref[other].astype(BF)


def join(axis, bit, mine_ref, got_ref, out_ref):
    mine, other = halves(axis, bit, mine_ref.shape[0])
    out_ref[mine] = mine_ref[...]
    out_ref[other] = got_ref[...]


def grad_kernel(axes, x_ref, v_ref, s_ref, r_ref, pass_ref, keep_a, send_a, keep_b, send_b, pass_out, ga, gb):
    count, width = x_ref.shape
    low = (s_ref[...].astype(F32) + r_ref[...].astype(F32)).astype(BF)
    ga[...] = SCALE * dot(x_ref[...], low[count:], ((0,), (0,)))
    halve(*axes[0], ga, keep_a, send_a)
    turned = SCALE * dot(low[:count], v_ref[...], ((0,), (0,)))
    for b in blocks_of(width):
        gb[b] = turned[:, b]
    halve(*axes[1], gb, keep_b, send_b)


def sum_kernel(keep_ref, got_ref, out_ref):
    out_ref[...] = (keep_ref[...].astype(F32) + got_ref[...].astype(F32)).astype(BF)


def step_kernel(waits, mine_a, got_a, mine_b, got_b, *refs):
    sum_a, sum_b = refs[waits : waits + 2]
    sum_kernel(mine_a, got_a, sum_a)
    sum_kernel(mine_b, got_b, sum_b)


def place_kernel(pos_ref, after_ref, out_ref):
    out_ref[...] = pos_ref[...].astype(F32)


def square_sum(ref):
    x = ref[...].astype(F32)
    return jnp.broadcast_to(jnp.sum(x * x), (8, LANES))


def low_kernel(way_a, way_b, hg_ref, mine_a, got_a, mine_b, got_b, pack_ref, ga_ref, gb_ref):
    join(*way_a, mine_a, got_a, ga_ref)
    count = hg_ref.shape[0]
    pack_ref[:count] = dot(hg_ref[...], ga_ref[...]).astype(BF)
    join(*way_b, mine_b, got_b, gb_ref)
    pack_ref[count:] = split_terms(square_sum(ga_ref) + square_sum(gb_ref))


def base_kernel(mine_ref, near_ref, far_ref, far_got, after_ref, base_ref, low_ref, scale_ref):
    count, width = mine_ref.shape
    sums = join_terms(far_ref[count:, width:]) + join_terms(far_got[count:, width:])
    scale = lax.rsqrt(sums / D + EPS)
    for i, b in enumerate(blocks_of(count)):
        block = jnp.broadcast_to(scale[i : i + 1], (LANES, LANES)).T
        scale_ref[b] = block
        low_ref[b] = (far_ref[b, width:].astype(F32) + far_got[b, width:].astype(F32)) * block
        for c in blocks_of(width):
            total = mine_ref[b, c].astype(F32) + near_ref[b, c].astype(F32) + far_got[b, c].astype(F32)
            base_ref[b, c] = total * block


def final_kernel(
    base_ref, low_ref, scale_ref, s_ref, r_ref, ga_ref, gb_ref, a_ref, b_ref, cos_ref, sin_ref,
    a_hbm, b_hbm, q_hbm, new_a, new_b, half_b, out, sems,
):
    count, width = base_ref.shape
    total = join_terms(s_ref[count:]) + join_terms(r_ref[count:])
    rate = (LEARN * lax.rsqrt(total + NORM_EPS))[0:1]
    for c in blocks_of(width):
        fresh = b_ref[:, c] - rate * gb_ref[c].astype(F32)
        new_b[:, c] = fresh
        half_b[:, c] = fresh.astype(BF)
    copies = [pltpu.make_async_copy(new_b, b_hbm, sems.at[0])]
    copies[-1].start()
    new_a[...] = a_ref[...] - rate * ga_ref[...].astype(F32)
    copies.append(pltpu.make_async_copy(new_a, a_hbm, sems.at[1]))
    copies[-1].start()
    for i, b in enumerate(blocks_of(count)):
        low = s_ref[b].astype(F32) + r_ref[b].astype(F32)
        mix = (low_ref[b] - rate * (low * scale_ref[b])) * SCALE
        update = dot(mix.astype(BF), half_b[...])
        cos, sin = cos_ref[b], sin_ref[b]
        for c in blocks_of(width):
            query = base_ref[b, c] + update[:, c]
            other = pltpu.roll(query, HEAD // 2, 1)
            out[b, c] = (query * cos + other * sin).astype(BF)
        copies.append(pltpu.make_async_copy(out.at[b], q_hbm.at[b], sems.at[2 + i]))
        copies[-1].start()
    for copy in copies:
        copy.wait()


def keep_hbm(x):
    return pltpu.with_memory_space_constraint(x, pltpu.HBM)


def call(kernel, outs, in_specs, args, name, scratch=(), out_specs=None, limit=16, aliases=None):
    return pl.pallas_call(
        kernel,
        out_shape=outs,
        in_specs=in_specs,
        out_specs=out_specs if out_specs is not None else jax.tree.map(lambda _: VMEM, outs),
        scratch_shapes=list(scratch),
        compiler_params=pltpu.CompilerParams(vmem_limit_bytes=int(limit * 1024 * 1024)),
        input_output_aliases=aliases or {},
        name=name,
    )(*args)


def turn_tables(places, steps):
    half = HEAD // 2
    freq = 10000.0 ** (-jnp.arange(half, dtype=F32) / half)
    cos, sin = [], []
    for step in range(steps):
        angle = (places + float(step))[:, None] * freq[None, :]
        c, s = jnp.cos(angle), jnp.sin(angle)
        cos.append(jnp.concatenate([c, c], axis=-1))
        sin.append(jnp.concatenate([-s, s], axis=-1))
    return jnp.concatenate(cos), jnp.concatenate(sin)


def bits_of(n):
    return [b for b in range(n.bit_length() - 1)]


def build(n_dp, n_roll, n_tp):
    z_bits = [("roll", b) for b in bits_of(n_roll)]
    x_bits = [("dp", b) for b in bits_of(n_dp)]
    sizes = {"dp": n_dp, "roll": n_roll}

    def cross(x, axis, bit):
        return swap(x, axis, sizes[axis], 1 << bit)

    path_a, path_b = z_bits + x_bits + z_bits[:1], x_bits[:1] + z_bits + x_bits[1:] + x_bits[:1]

    def on_device(
        train_inputs, train_cotangent, factor_a, factor_b, base_weight, incoming, norm_gain, positions
    ):
        steps, rows, width = incoming.shape
        tokens = train_inputs.shape[0]
        rank = factor_a.shape[1]
        count = steps * rows
        dma = lambda n: pltpu.SemaphoreType.DMA((n,))
        vmem = lambda n, dtype=F32: pltpu.VMEM((n, rank), dtype)

        tall = shape((count, width), BF)
        part, half_a, hidden = call(
            rank_kernel,
            [shape((2 * tokens, rank), BF), shape(factor_a.shape, BF), tall],
            [HBM] * 5,
            tuple(
                map(keep_hbm, (train_inputs, train_cotangent, factor_a, factor_b, incoming.reshape(count, width)))
            ),
            "rank",
            [pltpu.VMEM(train_inputs.shape, BF), pltpu.VMEM(train_inputs.shape, BF),
             pltpu.VMEM(factor_a.shape, F32), pltpu.VMEM(factor_b.shape, F32), dma(5)],
        )
        part_got = swap(part, "tp", n_tp, 1)
        cut = 512
        wide = shape((count + EXTRA, width + rank), BF)
        gained, pack = call(
            prep_kernel,
            [tall, shape((count + EXTRA, rank), BF)],
            [VMEM] * 3,
            (hidden, norm_gain[None, :], half_a),
            "prep",
        )
        part_sum = call(part_kernel, shape(part.shape, BF), [VMEM] * 2 + [ANY], (part, part_got, pack), "part_sum")
        part_far = swap(part_sum, "tp", n_tp, 2)

        def query(peers, outs, after, name):
            blocks = len(peers) * width // cut
            return call(
                functools.partial(query_kernel, peers),
                outs,
                [VMEM, HBM, VMEM, ANY],
                (gained, keep_hbm(base_weight), pack, after),
                name,
                [pltpu.VMEM((blocks, width, cut), BF), dma(blocks)],
            )

        diag, distant, beside = query((3, 2, 1), [wide, tall, tall], part_sum, "query_far")
        half = width // 2
        keep_a, send_a, keep_b, send_b, diag = call(
            functools.partial(grad_kernel, (path_a[0], path_b[0])),
            [shape((half, rank), F32), shape((half, rank), BF)] * 2 + [wide],
            [VMEM] * 4 + [ANY],
            (train_inputs, train_cotangent, part_sum, part_far, diag),
            "grads",
            [vmem(width), vmem(width)],
            out_specs=[VMEM] * 4 + [ANY],
            aliases={4: 4},
        )
        diag_got = swap(diag, "tp", n_tp, 1)
        far, beside = call(
            far_kernel,
            [wide, tall],
            [VMEM] * 3 + [ANY] * 2,
            (distant, diag, diag_got, send_a, beside),
            "far",
            out_specs=[VMEM, ANY],
            aliases={4: 1},
        )
        far_got = swap(far, "tp", n_tp, 2)
        beside_got = swap(beside, "tp", n_tp, 1)

        mine_a, mine_b, after = keep_a, keep_b, [far]
        for i, (way_a, way_b) in enumerate(zip(path_a[:-1], path_b[:-1])):
            got_a, got_b = cross(send_a, *way_a), cross(send_b, *way_b)
            mine_a, mine_b = call(
                functools.partial(step_kernel, len(after)),
                [shape((half, rank), BF)] * 2,
                [VMEM] * 4 + [ANY] * len(after),
                (mine_a, got_a, mine_b, got_b, *after),
                f"step_{i}",
            )
            send_a, send_b, after = mine_a, mine_b, []
            if i == 0:
                pos = positions.reshape(-1, LANES)
                places = call(place_kernel, shape(pos.shape, F32), [VMEM, ANY], (pos, mine_a), "places")
                cos, sin = after = turn_tables(places.reshape(rows), steps)
            if i == 1:
                (close,) = after = query((0,), [tall], mine_a, "query_close")
        step_pack, grad_a, grad_b = call(
            functools.partial(low_kernel, path_a[-1], path_b[-1]),
            [shape((count + EXTRA, rank), BF), shape((width, rank), BF), shape((width, rank), BF)],
            [VMEM] * 5,
            (gained, mine_a, cross(mine_a, *path_a[-1]), mine_b, cross(mine_b, *path_b[-1])),
            "low_rank",
        )
        step_got = swap(step_pack, "tp", n_tp, 1)
        step_sum = call(merge_kernel, shape((count + EXTRA, rank), BF), [VMEM] * 2, (step_pack, step_got), "merge")
        step_far = swap(step_sum, "tp", n_tp, 2)

        base, low, scale = call(
            base_kernel,
            [shape((count, width), F32), shape((count, rank), F32), shape((count, LANES), F32)],
            [VMEM] * 4 + [ANY],
            (close, beside_got, far, far_got, step_sum),
            "base",
        )
        new_a, new_b, queries = call(
            final_kernel,
            [shape((width, rank), F32), shape((rank, width), F32), tall],
            [VMEM] * 11,
            (base, low, scale, step_sum, step_far, grad_a, grad_b, factor_a, factor_b, cos, sin),
            "final",
            [pltpu.VMEM((width, rank), F32), pltpu.VMEM((rank, width), F32),
             pltpu.VMEM((rank, width), BF), pltpu.VMEM((count, width), BF), dma(2 + count // LANES)],
            [HBM] * 3,
        )
        return new_a, new_b, queries.reshape(steps, rows, width)

    return on_device


def solution(mesh):
    n_dp, n_roll, n_tp = (mesh.shape[a] for a in ("dp", "roll", "tp"))
    return jax.shard_map(
        build(n_dp, n_roll, n_tp),
        mesh=mesh,
        in_specs=(
            P(("dp", "roll"), "tp"),
            P(("dp", "roll"), "tp"),
            P("tp", None),
            P(None, "tp"),
            P("tp", None),
            P(None, ("dp", "roll"), "tp"),
            P("tp"),
            P(("dp", "roll")),
        ),
        out_specs=(P("tp", None), P(None, "tp"), P(None, ("dp", "roll"), "tp")),
        check_vma=False,
    )
```

```python
import functools

import jax
import jax.numpy as jnp
from jax import lax
from jax.experimental import pallas as pl
from jax.experimental.pallas import tpu as pltpu
from jax.sharding import PartitionSpec as P

D = 4096
HEAD = 128
SCALE = 2.0
LEARN = 3.0
EPS = 1e-05
NORM_EPS = 1e-06
LANES = 128
EXTRA = 32

BF = jnp.bfloat16
F32 = jnp.float32
VMEM = pl.BlockSpec(memory_space=pltpu.VMEM)
ANY = pl.BlockSpec(memory_space=pl.ANY)
HBM = pl.BlockSpec(memory_space=pltpu.HBM)


def shape(dims, dtype):
    return jax.ShapeDtypeStruct(dims, dtype)


def dot(a, b, dims=((1,), (0,))):
    return lax.dot_general(a, b, (dims, ((), ())), preferred_element_type=F32)


def swap(x, axis, n, k):
    return lax.ppermute(x, axis, [(i, i ^ k) for i in range(n)])


def split_terms(values):
    high = values.astype(BF)
    rest = values - high.astype(F32)
    middle = rest.astype(BF)
    last = (rest - middle.astype(F32)).astype(BF)
    return jnp.concatenate([high, middle, last, jnp.zeros_like(last)], axis=0)


def join_terms(terms):
    x = terms.astype(F32)
    return (x[0:8] + x[8:16]) + x[16:24]


def fetch(sources, targets, sems):
    copies = [pltpu.make_async_copy(s, t, sems.at[i]) for i, (s, t) in enumerate(zip(sources, targets))]
    for copy in copies:
        copy.start()
    return copies


def blocks_of(count):
    return [slice(i, i + LANES) for i in range(0, count, LANES)]


def rank_kernel(x_hbm, v_hbm, a_hbm, b_hbm, h_hbm, out_ref, a16_ref, h_ref, x_ref, v_ref, a_ref, b_ref, sems):
    copies = fetch((x_hbm, a_hbm, v_hbm, b_hbm, h_hbm), (x_ref, a_ref, v_ref, b_ref, h_ref), sems)
    count = x_ref.shape[0]
    copies[1].wait()
    a16_ref[...] = a_ref[...].astype(BF)
    copies[0].wait()
    out_ref[:count] = dot(x_ref[...], a16_ref[...]).astype(BF)
    copies[3].wait()
    b16 = b_ref[...].astype(BF)
    copies[2].wait()
    out_ref[count:] = dot(v_ref[...], b16, ((1,), (1,))).astype(BF)
    copies[4].wait()


def weight_blocks(peers, w_hbm, w_ref):
    _, width, cut = w_ref.shape
    mine = lax.axis_index("tp")
    sources = []
    for peer in peers:
        for i in range(width // cut):
            start = (mine ^ peer) * width + i * cut
            sources.append(w_hbm.at[:, pl.ds(pl.multiple_of(start, cut), cut)])
    return sources, [w_ref.at[i] for i in range(len(sources))]


def prep_kernel(h_ref, gain_ref, a16_ref, hg_ref, low_ref, sums_ref):
    count, width = h_ref.shape
    rows = []
    for b in blocks_of(count):
        wide = h_ref[b].astype(F32)
        hg_ref[b] = (wide * gain_ref[...]).astype(BF)
        sums = jnp.sum(wide * wide, axis=-1, keepdims=True)
        rows.append(jnp.broadcast_to(sums, (LANES, LANES)).T[0:1])
    if len(rows) < 8:
        rows.append(jnp.zeros((8 - len(rows), LANES), F32))
    sums_ref[...] = jnp.concatenate(rows, axis=0)
    low_ref[...] = dot(hg_ref[...], a16_ref[...]).astype(BF)


def part_kernel(x_ref, got_ref, after_ref, out_ref):
    sum_kernel(x_ref, got_ref, out_ref)


def query_kernel(peers, hg_ref, w_hbm, low_ref, after_ref, *rest):
    outs, (w_ref, sems) = rest[:-2], rest[-2:]
    _, width, cut = w_ref.shape
    copies = fetch(*weight_blocks(peers, w_hbm, w_ref), sems)
    if outs[0].shape[1] > width:
        outs[0][:, width:] = low_ref[...]
    per = width // cut
    for i, copy in enumerate(copies):
        copy.wait()
        outs[i // per][:, i % per * cut : (i % per + 1) * cut] = dot(hg_ref[...], w_ref[i]).astype(BF)


def far_kernel(mine_ref, diag_ref, got_ref, after_ref, out_ref):
    width = mine_ref.shape[1]
    sum_kernel(mine_ref, got_ref.at[:, :width], out_ref.at[:, :width])
    sum_kernel(diag_ref.at[:, width:], got_ref.at[:, width:], out_ref.at[:, width:])


def merge_kernel(a_ref, b_ref, out_ref):
    count = a_ref.shape[0] - EXTRA
    out_ref[:count] = (a_ref[:count].astype(F32) + b_ref[:count].astype(F32)).astype(BF)
    out_ref[count:] = split_terms(join_terms(a_ref[count:]) + join_terms(b_ref[count:]))


def halves(axis, bit, size):
    mine = lax.rem(lax.axis_index(axis) // (1 << bit), 2) * size
    return pl.ds(pl.multiple_of(mine, size), size), pl.ds(pl.multiple_of(size - mine, size), size)


def halve(axis, bit, total_ref, keep_ref, send_ref):
    mine, other = halves(axis, bit, keep_ref.shape[0])
    keep_ref[...] = total_ref[mine]
    send_ref[...] = total_ref[other].astype(BF)


def join(axis, bit, mine_ref, got_ref, out_ref):
    mine, other = halves(axis, bit, mine_ref.shape[0])
    out_ref[mine] = mine_ref[...]
    out_ref[other] = got_ref[...]


def grad_kernel(axes, x_ref, v_ref, s_ref, r_ref, after_ref, keep_a, send_a, keep_b, send_b, ga, gb):
    count, width = x_ref.shape
    low = (s_ref[...].astype(F32) + r_ref[...].astype(F32)).astype(BF)
    ga[...] = SCALE * dot(x_ref[...], low[count:], ((0,), (0,)))
    halve(*axes[0], ga, keep_a, send_a)
    turned = SCALE * dot(low[:count], v_ref[...], ((0,), (0,)))
    for b in blocks_of(width):
        gb[b] = turned[:, b]
    halve(*axes[1], gb, keep_b, send_b)


def sum_kernel(keep_ref, got_ref, out_ref):
    out_ref[...] = (keep_ref[...].astype(F32) + got_ref[...].astype(F32)).astype(BF)


def step_kernel(mine_ref, got_ref, *rest):
    sum_kernel(mine_ref, got_ref, rest[len(rest) // 2])


def place_kernel(pos_ref, after_ref, out_ref):
    out_ref[...] = pos_ref[...].astype(F32)


def square_sum(ref):
    x = ref[...].astype(F32)
    return jnp.broadcast_to(jnp.sum(x * x), (8, LANES))


def low_kernel(way_a, way_b, hg_ref, sums_ref, mine_a, got_a, mine_b, got_b, pack_ref, ga_ref, gb_ref):
    join(*way_a, mine_a, got_a, ga_ref)
    count = hg_ref.shape[0]
    pack_ref[:count] = dot(hg_ref[...], ga_ref[...]).astype(BF)
    join(*way_b, mine_b, got_b, gb_ref)
    row = lax.broadcasted_iota(jnp.int32, (8, LANES), 0)
    pack_ref[count:] = split_terms(jnp.where(row == 7, square_sum(ga_ref) + square_sum(gb_ref), sums_ref[...]))


def base_kernel(mine_ref, near_ref, far_ref, far_got, after_ref, base_ref, low_ref):
    width = mine_ref.shape[1]
    low_ref[...] = far_ref[:, width:].astype(F32) + far_got[:, width:].astype(F32)
    for c in blocks_of(width):
        base_ref[:, c] = mine_ref[:, c].astype(F32) + near_ref[:, c].astype(F32) + far_got[:, c].astype(F32)


def final_kernel(
    base_ref, low_ref, s_ref, r_ref, ga_ref, gb_ref, a_ref, b_ref, cos_ref, sin_ref,
    a_hbm, b_hbm, q_hbm, new_a, new_b, half_b, out, sems,
):
    count, width = base_ref.shape
    total = join_terms(s_ref[count:]) + join_terms(r_ref[count:])
    rate = (LEARN * lax.rsqrt(total + NORM_EPS))[7:8]
    scales = lax.rsqrt(total / D + EPS)
    for c in blocks_of(width):
        fresh = b_ref[:, c] - rate * gb_ref[c].astype(F32)
        new_b[:, c] = fresh
        half_b[:, c] = fresh.astype(BF)
    copies = [pltpu.make_async_copy(new_b, b_hbm, sems.at[0])]
    copies[-1].start()
    new_a[...] = a_ref[...] - rate * ga_ref[...].astype(F32)
    copies.append(pltpu.make_async_copy(new_a, a_hbm, sems.at[1]))
    copies[-1].start()
    for i, b in enumerate(blocks_of(count)):
        low = s_ref[b].astype(F32) + r_ref[b].astype(F32)
        scale = jnp.broadcast_to(scales[i : i + 1], (LANES, LANES)).T
        mix = (low_ref[b] - rate * low) * scale * SCALE
        update = dot(mix.astype(BF), half_b[...])
        cos, sin = cos_ref[b], sin_ref[b]
        for c in blocks_of(width):
            query = base_ref[b, c] * scale + update[:, c]
            other = pltpu.roll(query, HEAD // 2, 1)
            out[b, c] = (query * cos + other * sin).astype(BF)
        copies.append(pltpu.make_async_copy(out.at[b], q_hbm.at[b], sems.at[2 + i]))
        copies[-1].start()
    for copy in copies:
        copy.wait()


def keep_hbm(x):
    return pltpu.with_memory_space_constraint(x, pltpu.HBM)


WEIGHTS = {
    "rank": 2.4, "prep": 0.6, "query_diag": 40.0, "query_distant": 0.01, "query_beside": 1.0, "query_close": 0.5, "grads": 40.0,
    "final": 1.8,
}
FLOPS_PER_WEIGHT = 1_150_000_000


def call(kernel, outs, in_specs, args, name, scratch=(), out_specs=None, limit=16, aliases=None):
    return pl.pallas_call(
        kernel,
        out_shape=outs,
        in_specs=in_specs,
        out_specs=out_specs if out_specs is not None else jax.tree.map(lambda _: VMEM, outs),
        scratch_shapes=list(scratch),
        compiler_params=pltpu.CompilerParams(vmem_limit_bytes=int(limit * 1024 * 1024)),
        input_output_aliases=aliases or {},
        cost_estimate=pl.CostEstimate(
            flops=int(WEIGHTS.get(name, 0.01) * FLOPS_PER_WEIGHT), bytes_accessed=0, transcendentals=0
        ),
        name=name,
    )(*args)


def turn_tables(places, steps):
    half = HEAD // 2
    freq = 10000.0 ** (-jnp.arange(half, dtype=F32) / half)
    cos, sin = [], []
    for step in range(steps):
        angle = (places + float(step))[:, None] * freq[None, :]
        c, s = jnp.cos(angle), jnp.sin(angle)
        cos.append(jnp.concatenate([c, c], axis=-1))
        sin.append(jnp.concatenate([-s, s], axis=-1))
    return jnp.concatenate(cos), jnp.concatenate(sin)


def bits_of(n):
    return [b for b in range(n.bit_length() - 1)]


def build(n_dp, n_roll, n_tp):
    z_bits = [("roll", b) for b in bits_of(n_roll)]
    x_bits = [("dp", b) for b in bits_of(n_dp)]
    sizes = {"dp": n_dp, "roll": n_roll}

    def cross(x, axis, bit):
        return swap(x, axis, sizes[axis], 1 << bit)

    path_a, path_b = z_bits + x_bits + z_bits[:1], x_bits[:1] + z_bits + x_bits[1:] + x_bits[:1]

    def on_device(
        train_inputs, train_cotangent, factor_a, factor_b, base_weight, incoming, norm_gain, positions
    ):
        steps, rows, width = incoming.shape
        tokens = train_inputs.shape[0]
        rank = factor_a.shape[1]
        count = steps * rows
        dma = lambda n: pltpu.SemaphoreType.DMA((n,))
        vmem = lambda n, dtype=F32: pltpu.VMEM((n, rank), dtype)

        tall = shape((count, width), BF)
        part, half_a, hidden = call(
            rank_kernel,
            [shape((2 * tokens, rank), BF), shape(factor_a.shape, BF), tall],
            [HBM] * 5,
            tuple(
                map(keep_hbm, (train_inputs, train_cotangent, factor_a, factor_b, incoming.reshape(count, width)))
            ),
            "rank",
            [pltpu.VMEM(train_inputs.shape, BF), pltpu.VMEM(train_inputs.shape, BF),
             pltpu.VMEM(factor_a.shape, F32), pltpu.VMEM(factor_b.shape, F32), dma(5)],
        )
        part_got = swap(part, "tp", n_tp, 1)
        cut = 512
        wide = shape((count, width + rank), BF)
        gained, low, sums = call(
            prep_kernel,
            [tall, shape((count, rank), BF), shape((8, LANES), F32)],
            [VMEM] * 3,
            (hidden, norm_gain[None, :], half_a),
            "prep",
        )
        part_sum = call(part_kernel, shape(part.shape, BF), [VMEM] * 2 + [ANY], (part, part_got, low), "part_sum")
        part_far = swap(part_sum, "tp", n_tp, 2)

        def query(peers, outs, after, name):
            blocks = len(peers) * width // cut
            return call(
                functools.partial(query_kernel, peers),
                outs,
                [VMEM, HBM, VMEM, ANY],
                (gained, keep_hbm(base_weight), low, after),
                "query_" + name,
                [pltpu.VMEM((blocks, width, cut), BF), dma(blocks)],
            )

        (diag,) = query((3,), [wide], part_sum, "diag")
        diag_got = swap(diag, "tp", n_tp, 1)
        (distant,) = query((2,), [tall], diag, "distant")

        half = width // 2
        keep_a, send_a, keep_b, send_b = call(
            functools.partial(grad_kernel, (path_a[0], path_b[0])),
            [shape((half, rank), F32), shape((half, rank), BF)] * 2,
            [VMEM] * 4 + [ANY],
            (train_inputs, train_cotangent, part_sum, part_far, distant),
            "grads",
            [vmem(width), vmem(width)],
        )
        far = call(far_kernel, wide, [VMEM] * 3 + [ANY], (distant, diag, diag_got, send_a), "far")
        far_got = swap(far, "tp", n_tp, 2)

        def step(mine, send, way, after, passed, name):
            return call(
                step_kernel,
                [shape((half, rank), BF)] + [shape(x.shape, x.dtype) for x in passed],
                [VMEM] * 2 + [ANY] * (1 + len(passed)),
                (mine, cross(send, *way), after, *passed),
                name,
                out_specs=[VMEM] + [ANY] * len(passed),
                aliases={3 + k: 1 + k for k in range(len(passed))},
            )

        mine_a, mine_b, after, passed = keep_a, keep_b, far, []
        order = ["a", "b", "n", "b", "a", "c", "t", "a", "b"] if n_dp * n_roll == 8 else ["a", "b", "n", "b", "t", "a", "c"] + ["a", "b"] * (len(path_a) - 3)
        steps_a, steps_b = iter(path_a[:-1]), iter(path_b[:-1])
        for i, which in enumerate(order):
            if which == "a":
                mine_a = send_a = after = step(mine_a, send_a, next(steps_a), after, [], f"step_a{i}")[0]
            elif which == "b":
                mine_b, *made = step(mine_b, send_b, next(steps_b), after, passed, f"step_b{i}")
                send_b = after = mine_b
                if made:
                    beside_got, passed = swap(made[0], "tp", n_tp, 1), []
            elif which == "t":
                pos = positions.reshape(-1, LANES)
                places = call(place_kernel, shape(pos.shape, F32), [VMEM, ANY], (pos, after), "places")
                cos, sin = turn_tables(places.reshape(rows), steps)
                after = sin
            elif which == "n":
                passed = query((1,), [tall], after, "beside")
            else:
                (close,) = query((0,), [tall], after, "close")
                after = close
        step_pack, grad_a, grad_b = call(
            functools.partial(low_kernel, path_a[-1], path_b[-1]),
            [shape((count + EXTRA, rank), BF), shape((width, rank), BF), shape((width, rank), BF)],
            [VMEM] * 6,
            (gained, sums, mine_a, cross(mine_a, *path_a[-1]), mine_b, cross(mine_b, *path_b[-1])),
            "low_rank",
        )
        step_got = swap(step_pack, "tp", n_tp, 1)
        step_sum = call(merge_kernel, shape((count + EXTRA, rank), BF), [VMEM] * 2, (step_pack, step_got), "merge")
        step_far = swap(step_sum, "tp", n_tp, 2)

        base, low_all = call(
            base_kernel,
            [shape((count, width), F32), shape((count, rank), F32)],
            [VMEM] * 4 + [ANY],
            (close, beside_got, far, far_got, step_sum),
            "base",
        )
        new_a, new_b, queries = call(
            final_kernel,
            [shape((width, rank), F32), shape((rank, width), F32), tall],
            [VMEM] * 10,
            (base, low_all, step_sum, step_far, grad_a, grad_b, factor_a, factor_b, cos, sin),
            "final",
            [pltpu.VMEM((width, rank), F32), pltpu.VMEM((rank, width), F32),
             pltpu.VMEM((rank, width), BF), pltpu.VMEM((count, width), BF), dma(2 + count // LANES)],
            [HBM] * 3,
        )
        return new_a, new_b, queries.reshape(steps, rows, width)

    return on_device


def solution(mesh):
    n_dp, n_roll, n_tp = (mesh.shape[a] for a in ("dp", "roll", "tp"))
    return jax.shard_map(
        build(n_dp, n_roll, n_tp),
        mesh=mesh,
        in_specs=(
            P(("dp", "roll"), "tp"),
            P(("dp", "roll"), "tp"),
            P("tp", None),
            P(None, "tp"),
            P("tp", None),
            P(None, ("dp", "roll"), "tp"),
            P("tp"),
            P(("dp", "roll")),
        ),
        out_specs=(P("tp", None), P(None, "tp"), P(None, ("dp", "roll"), "tp")),
        check_vma=False,
    )
```

```python
import functools

import jax
import jax.numpy as jnp
from jax import lax
from jax.experimental import pallas as pl
from jax.experimental.pallas import tpu as pltpu
from jax.sharding import PartitionSpec as P

D = 4096
HEAD = 128
SCALE = 2.0
LEARN = 3.0
EPS = 1e-05
NORM_EPS = 1e-06
LANES = 128
EXTRA = 32

BF = jnp.bfloat16
F32 = jnp.float32
VMEM = pl.BlockSpec(memory_space=pltpu.VMEM)
ANY = pl.BlockSpec(memory_space=pl.ANY)
HBM = pl.BlockSpec(memory_space=pltpu.HBM)


def shape(dims, dtype):
    return jax.ShapeDtypeStruct(dims, dtype)


def dot(a, b, dims=((1,), (0,))):
    return lax.dot_general(a, b, (dims, ((), ())), preferred_element_type=F32)


def swap(x, axis, n, k):
    return lax.ppermute(x, axis, [(i, i ^ k) for i in range(n)])


def split_terms(values):
    high = values.astype(BF)
    rest = values - high.astype(F32)
    middle = rest.astype(BF)
    last = (rest - middle.astype(F32)).astype(BF)
    return jnp.concatenate([high, middle, last, jnp.zeros_like(last)], axis=0)


def join_terms(terms):
    x = terms.astype(F32)
    return (x[0:8] + x[8:16]) + x[16:24]


def fetch(sources, targets, sems):
    copies = [pltpu.make_async_copy(s, t, sems.at[i]) for i, (s, t) in enumerate(zip(sources, targets))]
    for copy in copies:
        copy.start()
    return copies


def blocks_of(count):
    return [slice(i, i + LANES) for i in range(0, count, LANES)]


def rank_kernel(x_hbm, v_hbm, a_hbm, b_hbm, h_hbm, out_ref, a16_ref, h_ref, x_ref, v_ref, a_ref, b_ref, sems):
    count = x_ref.shape[0]
    half = count // 2
    copies = fetch(
        (a_hbm, x_hbm, b_hbm, v_hbm.at[:half], v_hbm.at[half:], h_hbm),
        (a_ref, x_ref, b_ref, v_ref.at[:half], v_ref.at[half:], h_ref),
        sems,
    )
    copies[0].wait()
    a16_ref[...] = a_ref[...].astype(BF)
    copies[1].wait()
    out_ref[:count] = dot(x_ref[...], a16_ref[...]).astype(BF)
    copies[2].wait()
    b16 = b_ref[...].astype(BF)
    copies[3].wait()
    out_ref[count : count + half] = dot(v_ref[:half], b16, ((1,), (1,))).astype(BF)
    copies[4].wait()
    out_ref[count + half :] = dot(v_ref[half:], b16, ((1,), (1,))).astype(BF)
    copies[5].wait()


def weight_blocks(peers, w_hbm, w_ref):
    _, width, cut = w_ref.shape
    mine = lax.axis_index("tp")
    sources = []
    for peer in peers:
        for i in range(width // cut):
            start = (mine ^ peer) * width + i * cut
            sources.append(w_hbm.at[:, pl.ds(pl.multiple_of(start, cut), cut)])
    return sources, [w_ref.at[i] for i in range(len(sources))]


def prep_kernel(h_ref, gain_ref, a16_ref, hg_ref, low_ref, sums_ref):
    count, width = h_ref.shape
    rows = []
    for b in blocks_of(count):
        wide = h_ref[b].astype(F32)
        hg_ref[b] = (wide * gain_ref[...]).astype(BF)
        sums = jnp.sum(wide * wide, axis=-1, keepdims=True)
        rows.append(jnp.broadcast_to(sums, (LANES, LANES)).T[0:1])
    if len(rows) < 8:
        rows.append(jnp.zeros((8 - len(rows), LANES), F32))
    sums_ref[...] = jnp.concatenate(rows, axis=0)
    low_ref[...] = dot(hg_ref[...], a16_ref[...]).astype(BF)


def part_kernel(x_ref, got_ref, after_ref, out_ref):
    sum_kernel(x_ref, got_ref, out_ref)


def query_kernel(peers, hg_ref, w_hbm, after_ref, *rest):
    outs, (w_ref, sems) = rest[:-2], rest[-2:]
    _, width, cut = w_ref.shape
    copies = fetch(*weight_blocks(peers, w_hbm, w_ref), sems)
    per = width // cut
    for i, copy in enumerate(copies):
        copy.wait()
        outs[i // per][:, i % per * cut : (i % per + 1) * cut] = dot(hg_ref[...], w_ref[i]).astype(BF)


def diag_kernel(hg_ref, w_hbm, low_ref, after_ref, out_ref, next_ref, w_ref, sems):
    _, width, cut = w_ref.shape
    per = width // cut
    mine, targets = weight_blocks((3,), w_hbm, w_ref)
    later, next_targets = weight_blocks((2,), w_hbm, next_ref)
    copies = fetch(mine + later, targets + next_targets, sems)
    out_ref[:, width:] = low_ref[...]
    for i in range(per):
        copies[i].wait()
        out_ref[:, i * cut : (i + 1) * cut] = dot(hg_ref[...], w_ref[i]).astype(BF)
    for copy in copies[per:]:
        copy.wait()


def distant_kernel(hg_ref, w_ref, after_ref, out_ref):
    per, _, cut = w_ref.shape
    for i in range(per):
        out_ref[:, i * cut : (i + 1) * cut] = dot(hg_ref[...], w_ref[i]).astype(BF)


def far_kernel(mine_ref, diag_ref, got_ref, after_ref, out_ref):
    width = mine_ref.shape[1]
    sum_kernel(mine_ref, got_ref.at[:, :width], out_ref.at[:, :width])
    sum_kernel(diag_ref.at[:, width:], got_ref.at[:, width:], out_ref.at[:, width:])


def merge_kernel(a_ref, b_ref, out_ref):
    count = a_ref.shape[0] - EXTRA
    out_ref[:count] = (a_ref[:count].astype(F32) + b_ref[:count].astype(F32)).astype(BF)
    out_ref[count:] = split_terms(join_terms(a_ref[count:]) + join_terms(b_ref[count:]))


def halves(axis, bit, size):
    mine = lax.rem(lax.axis_index(axis) // (1 << bit), 2) * size
    return pl.ds(pl.multiple_of(mine, size), size), pl.ds(pl.multiple_of(size - mine, size), size)


def join(axis, bit, mine_ref, got_ref, out_ref):
    mine, other = halves(axis, bit, mine_ref.shape[0])
    out_ref[mine] = mine_ref[...]
    out_ref[other] = got_ref[...]


def grad_kernel(axes, x_ref, v_ref, s_ref, r_ref, after_ref, keep_a, send_a, keep_b, send_b):
    count, width = x_ref.shape
    low = (s_ref[...].astype(F32) + r_ref[...].astype(F32)).astype(BF)
    mine, other = halves(*axes[0], width // 2)
    send_a[...] = (SCALE * dot(x_ref[:, other], low[count:], ((0,), (0,)))).astype(BF)
    keep_a[...] = SCALE * dot(x_ref[:, mine], low[count:], ((0,), (0,)))
    mine, other = halves(*axes[1], width // 2)
    sent = (SCALE * dot(low[:count], v_ref[:, other], ((0,), (0,)))).astype(BF)
    kept = SCALE * dot(low[:count], v_ref[:, mine], ((0,), (0,)))
    for b in blocks_of(width // 2):
        send_b[b] = sent[:, b]
        keep_b[b] = kept[:, b]


def sum_kernel(keep_ref, got_ref, out_ref):
    out_ref[...] = (keep_ref[...].astype(F32) + got_ref[...].astype(F32)).astype(BF)


def step_kernel(mine_ref, got_ref, *rest):
    sum_kernel(mine_ref, got_ref, rest[len(rest) // 2])


def place_kernel(pos_ref, after_ref, out_ref):
    out_ref[...] = pos_ref[...].astype(F32)


def square_sum(ref):
    x = ref[...].astype(F32)
    return jnp.broadcast_to(jnp.sum(x * x), (8, LANES))


def own_kernel(way, hg_ref, sums_ref, mine_a, mine_b, after_ref, low_ref, sums_out):
    mine, _ = halves(*way, mine_a.shape[0])
    low_ref[...] = dot(hg_ref[:, mine], mine_a[...])
    sums_out[0] = sums_ref[...]
    sums_out[1] = square_sum(mine_a)
    sums_out[2] = square_sum(mine_b)


def low_kernel(way_a, way_b, hg_ref, low_ref, sums_ref, mine_a, got_a, mine_b, got_b, pack_ref, ga_ref, gb_ref):
    join(*way_a, mine_a, got_a, ga_ref)
    count = hg_ref.shape[0]
    _, other = halves(*way_a, mine_a.shape[0])
    pack_ref[:count] = (low_ref[...] + dot(hg_ref[:, other], got_a[...])).astype(BF)
    join(*way_b, mine_b, got_b, gb_ref)
    squares = (sums_ref[1] + square_sum(got_a)) + (sums_ref[2] + square_sum(got_b))
    row = lax.broadcasted_iota(jnp.int32, (8, LANES), 0)
    pack_ref[count:] = split_terms(jnp.where(row == 7, squares, sums_ref[0]))


def base_kernel(mine_ref, near_ref, far_ref, far_got, after_ref, base_ref, low_ref):
    width = mine_ref.shape[1]
    low_ref[...] = far_ref[:, width:].astype(F32) + far_got[:, width:].astype(F32)
    for c in blocks_of(width):
        base_ref[:, c] = mine_ref[:, c].astype(F32) + near_ref[:, c].astype(F32) + far_got[:, c].astype(F32)


def final_kernel(
    base_ref, low_ref, s_ref, r_ref, ga_ref, gb_ref, a_ref, b_ref, cos_ref, sin_ref,
    a_hbm, b_hbm, q_hbm, new_a, new_b, half_b, out, sems,
):
    count, width = base_ref.shape
    total = join_terms(s_ref[count:]) + join_terms(r_ref[count:])
    rate = (LEARN * lax.rsqrt(total + NORM_EPS))[7:8]
    scales = lax.rsqrt(total / D + EPS)
    for c in blocks_of(width):
        fresh = b_ref[:, c] - rate * gb_ref[c].astype(F32)
        new_b[:, c] = fresh
        half_b[:, c] = fresh.astype(BF)
    copies = [pltpu.make_async_copy(new_b, b_hbm, sems.at[0])]
    copies[-1].start()
    new_a[...] = a_ref[...] - rate * ga_ref[...].astype(F32)
    copies.append(pltpu.make_async_copy(new_a, a_hbm, sems.at[1]))
    copies[-1].start()
    for i, b in enumerate(blocks_of(count)):
        low = s_ref[b].astype(F32) + r_ref[b].astype(F32)
        scale = jnp.broadcast_to(scales[i : i + 1], (LANES, LANES)).T
        mix = (low_ref[b] - rate * low) * scale * SCALE
        update = dot(mix.astype(BF), half_b[...])
        cos, sin = cos_ref[b], sin_ref[b]
        for c in blocks_of(width):
            query = base_ref[b, c] * scale + update[:, c]
            other = pltpu.roll(query, HEAD // 2, 1)
            out[b, c] = (query * cos + other * sin).astype(BF)
        copies.append(pltpu.make_async_copy(out.at[b], q_hbm.at[b], sems.at[2 + i]))
        copies[-1].start()
    for copy in copies:
        copy.wait()


def keep_hbm(x):
    return pltpu.with_memory_space_constraint(x, pltpu.HBM)


WEIGHTS = {"rank": 2.4, "prep": 0.6, "query_diag": 40.0, "query_distant": 0.01, "query_beside": 1.0, "query_close": 0.5, "grads": 40.0, "final": 1.8}
FLOPS_PER_WEIGHT = 1_150_000_000


def call(kernel, outs, in_specs, args, name, scratch=(), out_specs=None, limit=16, aliases=None):
    return pl.pallas_call(
        kernel,
        out_shape=outs,
        in_specs=in_specs,
        out_specs=out_specs if out_specs is not None else jax.tree.map(lambda _: VMEM, outs),
        scratch_shapes=list(scratch),
        compiler_params=pltpu.CompilerParams(vmem_limit_bytes=int(limit * 1024 * 1024)),
        input_output_aliases=aliases or {},
        cost_estimate=pl.CostEstimate(
            flops=int(WEIGHTS.get(name, 0.01) * FLOPS_PER_WEIGHT), bytes_accessed=0, transcendentals=0
        ),
        name=name,
    )(*args)


def turn_tables(places, steps):
    half = HEAD // 2
    freq = 10000.0 ** (-jnp.arange(half, dtype=F32) / half)
    cos, sin = [], []
    for step in range(steps):
        angle = (places + float(step))[:, None] * freq[None, :]
        c, s = jnp.cos(angle), jnp.sin(angle)
        cos.append(jnp.concatenate([c, c], axis=-1))
        sin.append(jnp.concatenate([-s, s], axis=-1))
    return jnp.concatenate(cos), jnp.concatenate(sin)


def bits_of(n):
    return [b for b in range(n.bit_length() - 1)]


def build(n_dp, n_roll, n_tp):
    z_bits = [("roll", b) for b in bits_of(n_roll)]
    x_bits = [("dp", b) for b in bits_of(n_dp)]
    sizes = {"dp": n_dp, "roll": n_roll}

    def cross(x, axis, bit):
        return swap(x, axis, sizes[axis], 1 << bit)

    path_a, path_b = z_bits + x_bits + z_bits[:1], x_bits[:1] + z_bits + x_bits[1:] + x_bits[:1]

    def on_device(
        train_inputs, train_cotangent, factor_a, factor_b, base_weight, incoming, norm_gain, positions
    ):
        steps, rows, width = incoming.shape
        tokens = train_inputs.shape[0]
        rank = factor_a.shape[1]
        count = steps * rows
        dma = lambda n: pltpu.SemaphoreType.DMA((n,))
        vmem = lambda n, dtype=F32: pltpu.VMEM((n, rank), dtype)

        tall = shape((count, width), BF)
        part, half_a, hidden = call(
            rank_kernel,
            [shape((2 * tokens, rank), BF), shape(factor_a.shape, BF), tall],
            [HBM] * 5,
            tuple(
                map(keep_hbm, (train_inputs, train_cotangent, factor_a, factor_b, incoming.reshape(count, width)))
            ),
            "rank",
            [pltpu.VMEM(train_inputs.shape, BF), pltpu.VMEM(train_inputs.shape, BF),
             pltpu.VMEM(factor_a.shape, F32), pltpu.VMEM(factor_b.shape, F32), dma(6)],
        )
        part_got = swap(part, "tp", n_tp, 1)
        cut = 512
        wide = shape((count, width + rank), BF)
        gained, low, sums = call(
            prep_kernel,
            [tall, shape((count, rank), BF), shape((8, LANES), F32)],
            [VMEM] * 3,
            (hidden, norm_gain[None, :], half_a),
            "prep",
        )
        part_sum = call(part_kernel, shape(part.shape, BF), [VMEM] * 2 + [ANY], (part, part_got, low), "part_sum")
        part_far = swap(part_sum, "tp", n_tp, 2)

        def query(peers, outs, after, name):
            blocks = len(peers) * width // cut
            return call(
                functools.partial(query_kernel, peers),
                outs,
                [VMEM, HBM, ANY],
                (gained, keep_hbm(base_weight), after),
                "query_" + name,
                [pltpu.VMEM((blocks, width, cut), BF), dma(blocks)],
            )

        per = width // cut
        diag, columns = call(
            diag_kernel,
            [wide, shape((per, width, cut), BF)],
            [VMEM, HBM, VMEM, ANY],
            (gained, keep_hbm(base_weight), low, part_sum),
            "query_diag",
            [pltpu.VMEM((per, width, cut), BF), dma(2 * per)],
        )
        diag_got = swap(diag, "tp", n_tp, 1)
        distant = call(distant_kernel, tall, [VMEM, VMEM, ANY], (gained, columns, diag), "query_distant")

        half = width // 2
        keep_a, send_a, keep_b, send_b = call(
            functools.partial(grad_kernel, (path_a[0], path_b[0])),
            [shape((half, rank), F32), shape((half, rank), BF)] * 2,
            [VMEM] * 4 + [ANY],
            (train_inputs, train_cotangent, part_sum, part_far, distant),
            "grads",
        )
        far = call(far_kernel, wide, [VMEM] * 3 + [ANY], (distant, diag, diag_got, send_a), "far")
        far_got = swap(far, "tp", n_tp, 2)

        def step(mine, send, way, after, passed, name):
            return call(
                step_kernel,
                [shape((half, rank), BF)] + [shape(x.shape, x.dtype) for x in passed],
                [VMEM] * 2 + [ANY] * (1 + len(passed)),
                (mine, cross(send, *way), after, *passed),
                name,
                out_specs=[VMEM] + [ANY] * len(passed),
                aliases={3 + k: 1 + k for k in range(len(passed))},
            )

        mine_a, mine_b, after, passed = keep_a, keep_b, far, []
        order = ["a", "b", "n", "b", "a", "c", "t", "a", "b"] if n_dp * n_roll == 8 else ["a", "b", "n", "b", "t", "a", "c"] + ["a", "b"] * (len(path_a) - 3)
        steps_a, steps_b = iter(path_a[:-1]), iter(path_b[:-1])
        for i, which in enumerate(order):
            if which == "a":
                mine_a = send_a = after = step(mine_a, send_a, next(steps_a), after, [], f"step_a{i}")[0]
            elif which == "b":
                mine_b, *made = step(mine_b, send_b, next(steps_b), after, passed, f"step_b{i}")
                send_b = after = mine_b
                if made:
                    beside_got, passed = swap(made[0], "tp", n_tp, 1), []
            elif which == "t":
                pos = positions.reshape(-1, LANES)
                places = call(place_kernel, shape(pos.shape, F32), [VMEM, ANY], (pos, after), "places")
                cos, sin = turn_tables(places.reshape(rows), steps)
                after = sin
            elif which == "n":
                passed = query((1,), [tall], after, "beside")
            else:
                (close,) = query((0,), [tall], after, "close")
                after = close
        own_low, own_sums = call(
            functools.partial(own_kernel, path_a[-1]),
            [shape((count, rank), F32), shape((3, 8, LANES), F32)],
            [VMEM] * 4 + [ANY],
            (gained, sums, mine_a, mine_b, after),
            "own_half",
        )
        step_pack, grad_a, grad_b = call(
            functools.partial(low_kernel, path_a[-1], path_b[-1]),
            [shape((count + EXTRA, rank), BF), shape((width, rank), BF), shape((width, rank), BF)],
            [VMEM] * 7,
            (gained, own_low, own_sums, mine_a, cross(mine_a, *path_a[-1]), mine_b, cross(mine_b, *path_b[-1])),
            "low_rank",
        )
        step_got = swap(step_pack, "tp", n_tp, 1)
        step_sum = call(merge_kernel, shape((count + EXTRA, rank), BF), [VMEM] * 2, (step_pack, step_got), "merge")
        step_far = swap(step_sum, "tp", n_tp, 2)

        base, low_all = call(
            base_kernel,
            [shape((count, width), F32), shape((count, rank), F32)],
            [VMEM] * 4 + [ANY],
            (close, beside_got, far, far_got, step_sum),
            "base",
        )
        new_a, new_b, queries = call(
            final_kernel,
            [shape((width, rank), F32), shape((rank, width), F32), tall],
            [VMEM] * 10,
            (base, low_all, step_sum, step_far, grad_a, grad_b, factor_a, factor_b, cos, sin),
            "final",
            [pltpu.VMEM((width, rank), F32), pltpu.VMEM((rank, width), F32),
             pltpu.VMEM((rank, width), BF), pltpu.VMEM((count, width), BF), dma(2 + count // LANES)],
            [HBM] * 3,
        )
        return new_a, new_b, queries.reshape(steps, rows, width)

    return on_device


def solution(mesh):
    n_dp, n_roll, n_tp = (mesh.shape[a] for a in ("dp", "roll", "tp"))
    return jax.shard_map(
        build(n_dp, n_roll, n_tp),
        mesh=mesh,
        in_specs=(
            P(("dp", "roll"), "tp"),
            P(("dp", "roll"), "tp"),
            P("tp", None),
            P(None, "tp"),
            P("tp", None),
            P(None, ("dp", "roll"), "tp"),
            P("tp"),
            P(("dp", "roll")),
        ),
        out_specs=(P("tp", None), P(None, "tp"), P(None, ("dp", "roll"), "tp")),
        check_vma=False,
    )
```

```python
import functools

import jax
import jax.numpy as jnp
from jax import lax
from jax.experimental import pallas as pl
from jax.experimental.pallas import tpu as pltpu
from jax.sharding import PartitionSpec as P

D = 4096
HEAD = 128
SCALE = 2.0
LEARN = 3.0
EPS = 1e-05
NORM_EPS = 1e-06
LANES = 128
EXTRA = 32

BF = jnp.bfloat16
F32 = jnp.float32
VMEM = pl.BlockSpec(memory_space=pltpu.VMEM)
ANY = pl.BlockSpec(memory_space=pl.ANY)
HBM = pl.BlockSpec(memory_space=pltpu.HBM)


def shape(dims, dtype):
    return jax.ShapeDtypeStruct(dims, dtype)


def dot(a, b, dims=((1,), (0,))):
    return lax.dot_general(a, b, (dims, ((), ())), preferred_element_type=F32)


def swap(x, axis, n, k):
    return lax.ppermute(x, axis, [(i, i ^ k) for i in range(n)])


def split_terms(values):
    high = values.astype(BF)
    rest = values - high.astype(F32)
    middle = rest.astype(BF)
    last = (rest - middle.astype(F32)).astype(BF)
    return jnp.concatenate([high, middle, last, jnp.zeros_like(last)], axis=0)


def join_terms(terms):
    x = terms.astype(F32)
    return (x[0:8] + x[8:16]) + x[16:24]


def fetch(sources, targets, sems):
    copies = [pltpu.make_async_copy(s, t, sems.at[i]) for i, (s, t) in enumerate(zip(sources, targets))]
    for copy in copies:
        copy.start()
    return copies


def blocks_of(count):
    return [slice(i, i + LANES) for i in range(0, count, LANES)]


def rank_v_kernel(x_hbm, v_hbm, a_hbm, b_hbm, h_hbm, out_ref, x_ref, v_ref, a16_ref, h_ref, a_ref, b_ref, sems):
    copies = fetch((v_hbm, b_hbm, x_hbm, a_hbm, h_hbm), (v_ref, b_ref, x_ref, a_ref, h_ref), sems)
    copies[1].wait()
    b16 = b_ref[...].astype(BF)
    copies[0].wait()
    out_ref[...] = dot(v_ref[...], b16, ((1,), (1,))).astype(BF)
    copies[3].wait()
    a16_ref[...] = a_ref[...].astype(BF)
    copies[2].wait()
    copies[4].wait()


def rank_u_kernel(x_ref, a16_ref, out_ref):
    out_ref[...] = dot(x_ref[...], a16_ref[...]).astype(BF)


def weight_blocks(peers, w_hbm, w_ref):
    _, width, cut = w_ref.shape
    mine = lax.axis_index("tp")
    sources = []
    for peer in peers:
        for i in range(width // cut):
            start = (mine ^ peer) * width + i * cut
            sources.append(w_hbm.at[:, pl.ds(pl.multiple_of(start, cut), cut)])
    return sources, [w_ref.at[i] for i in range(len(sources))]


def prep_kernel(h_ref, gain_ref, a16_ref, hg_ref, low_ref, sums_ref):
    count, width = h_ref.shape
    rows = []
    for b in blocks_of(count):
        wide = h_ref[b].astype(F32)
        hg_ref[b] = (wide * gain_ref[...]).astype(BF)
        sums = jnp.sum(wide * wide, axis=-1, keepdims=True)
        rows.append(jnp.broadcast_to(sums, (LANES, LANES)).T[0:1])
    if len(rows) < 8:
        rows.append(jnp.zeros((8 - len(rows), LANES), F32))
    sums_ref[...] = jnp.concatenate(rows, axis=0)
    low_ref[...] = dot(hg_ref[...], a16_ref[...]).astype(BF)


def part_kernel(x_ref, got_ref, after_ref, out_ref):
    sum_kernel(x_ref, got_ref, out_ref)


def query_kernel(peers, hg_ref, w_hbm, after_ref, *rest):
    outs, (w_ref, sems) = rest[:-2], rest[-2:]
    _, width, cut = w_ref.shape
    copies = fetch(*weight_blocks(peers, w_hbm, w_ref), sems)
    per = width // cut
    for i, copy in enumerate(copies):
        copy.wait()
        outs[i // per][:, i % per * cut : (i % per + 1) * cut] = dot(hg_ref[...], w_ref[i]).astype(BF)


def diag_kernel(hg_ref, w_hbm, low_ref, after_ref, out_ref, next_ref, w_ref, sems):
    _, width, cut = w_ref.shape
    per = width // cut
    mine, targets = weight_blocks((3,), w_hbm, w_ref)
    later, next_targets = weight_blocks((2,), w_hbm, next_ref)
    copies = fetch(mine + later, targets + next_targets, sems)
    out_ref[:, width:] = low_ref[...]
    for i in range(per):
        copies[i].wait()
        out_ref[:, i * cut : (i + 1) * cut] = dot(hg_ref[...], w_ref[i]).astype(BF)
    for copy in copies[per:]:
        copy.wait()


def distant_kernel(hg_ref, w_ref, after_ref, out_ref):
    per, _, cut = w_ref.shape
    for i in range(per):
        out_ref[:, i * cut : (i + 1) * cut] = dot(hg_ref[...], w_ref[i]).astype(BF)


def far_kernel(mine_ref, diag_ref, got_ref, after_ref, out_ref):
    width = mine_ref.shape[1]
    sum_kernel(mine_ref, got_ref.at[:, :width], out_ref.at[:, :width])
    sum_kernel(diag_ref.at[:, width:], got_ref.at[:, width:], out_ref.at[:, width:])


def merge_kernel(a_ref, b_ref, out_ref):
    count = a_ref.shape[0] - EXTRA
    out_ref[:count] = (a_ref[:count].astype(F32) + b_ref[:count].astype(F32)).astype(BF)
    out_ref[count:] = split_terms(join_terms(a_ref[count:]) + join_terms(b_ref[count:]))


def halves(axis, bit, size):
    mine = lax.rem(lax.axis_index(axis) // (1 << bit), 2) * size
    return pl.ds(pl.multiple_of(mine, size), size), pl.ds(pl.multiple_of(size - mine, size), size)


def join(axis, bit, mine_ref, got_ref, out_ref):
    mine, other = halves(axis, bit, mine_ref.shape[0])
    out_ref[mine] = mine_ref[...]
    out_ref[other] = got_ref[...]


def grad_a_kernel(way, x_ref, s_ref, r_ref, after_ref, keep_ref, send_ref):
    low = (s_ref[...].astype(F32) + r_ref[...].astype(F32)).astype(BF)
    mine, other = halves(*way, x_ref.shape[1] // 2)
    send_ref[...] = (SCALE * dot(x_ref[:, other], low, ((0,), (0,)))).astype(BF)
    keep_ref[...] = SCALE * dot(x_ref[:, mine], low, ((0,), (0,)))


def grad_b_kernel(way, v_ref, s_ref, r_ref, after_ref, keep_ref, send_ref):
    low = (s_ref[...].astype(F32) + r_ref[...].astype(F32)).astype(BF)
    mine, other = halves(*way, v_ref.shape[1] // 2)
    sent = (SCALE * dot(low, v_ref[:, other], ((0,), (0,)))).astype(BF)
    kept = SCALE * dot(low, v_ref[:, mine], ((0,), (0,)))
    for b in blocks_of(v_ref.shape[1] // 2):
        send_ref[b] = sent[:, b]
        keep_ref[b] = kept[:, b]


def sum_kernel(keep_ref, got_ref, out_ref):
    out_ref[...] = (keep_ref[...].astype(F32) + got_ref[...].astype(F32)).astype(BF)


def step_kernel(mine_ref, got_ref, *rest):
    sum_kernel(mine_ref, got_ref, rest[len(rest) // 2])


def place_kernel(pos_ref, after_ref, out_ref):
    out_ref[...] = pos_ref[...].astype(F32)


def square_sum(ref):
    x = ref[...].astype(F32)
    return jnp.broadcast_to(jnp.sum(x * x), (8, LANES))


def update_kernel(way, hg_ref, mine_a, got_a, mine_b, low_ref, ga_ref, squares_ref):
    join(*way, mine_a, got_a, ga_ref)
    low_ref[...] = dot(hg_ref[...], ga_ref[...]).astype(BF)
    squares_ref[0] = square_sum(mine_a) + square_sum(got_a)
    squares_ref[1] = square_sum(mine_b)


def pack_kernel(way, low_ref, sums_ref, squares_ref, mine_b, got_b, pack_ref, gb_ref):
    count = low_ref.shape[0]
    pack_ref[:count] = low_ref[...]
    row = lax.broadcasted_iota(jnp.int32, (8, LANES), 0)
    squares = squares_ref[0] + (squares_ref[1] + square_sum(got_b))
    pack_ref[count:] = split_terms(jnp.where(row == 7, squares, sums_ref[...]))
    join(*way, mine_b, got_b, gb_ref)


def base_kernel(mine_ref, near_ref, far_ref, far_got, after_ref, base_ref, low_ref):
    width = mine_ref.shape[1]
    low_ref[...] = far_ref[:, width:].astype(F32) + far_got[:, width:].astype(F32)
    for c in blocks_of(width):
        base_ref[:, c] = mine_ref[:, c].astype(F32) + near_ref[:, c].astype(F32) + far_got[:, c].astype(F32)


def final_kernel(
    base_ref, low_ref, s_ref, r_ref, ga_ref, gb_ref, a_ref, b_ref, cos_ref, sin_ref,
    a_hbm, b_hbm, q_hbm, new_a, new_b, half_b, out, sems,
):
    count, width = base_ref.shape
    total = join_terms(s_ref[count:]) + join_terms(r_ref[count:])
    rate = (LEARN * lax.rsqrt(total + NORM_EPS))[7:8]
    scales = lax.rsqrt(total / D + EPS)
    for c in blocks_of(width):
        fresh = b_ref[:, c] - rate * gb_ref[c].astype(F32)
        new_b[:, c] = fresh
        half_b[:, c] = fresh.astype(BF)
    copies = [pltpu.make_async_copy(new_b, b_hbm, sems.at[0])]
    copies[-1].start()
    new_a[...] = a_ref[...] - rate * ga_ref[...].astype(F32)
    copies.append(pltpu.make_async_copy(new_a, a_hbm, sems.at[1]))
    copies[-1].start()
    for i, b in enumerate(blocks_of(count)):
        low = s_ref[b].astype(F32) + r_ref[b].astype(F32)
        scale = jnp.broadcast_to(scales[i : i + 1], (LANES, LANES)).T
        mix = (low_ref[b] - rate * low) * scale * SCALE
        update = dot(mix.astype(BF), half_b[...])
        cos, sin = cos_ref[b], sin_ref[b]
        for c in blocks_of(width):
            query = base_ref[b, c] * scale + update[:, c]
            other = pltpu.roll(query, HEAD // 2, 1)
            out[b, c] = (query * cos + other * sin).astype(BF)
        copies.append(pltpu.make_async_copy(out.at[b], q_hbm.at[b], sems.at[2 + i]))
        copies[-1].start()
    for copy in copies:
        copy.wait()


def keep_hbm(x):
    return pltpu.with_memory_space_constraint(x, pltpu.HBM)


WEIGHTS = {
    "rank_v": 2.4, "prep": 0.6, "query_diag": 40.0, "query_beside": 1.0, "query_close": 0.5, "grad_b": 40.0, "final": 1.8,
}
FLOPS_PER_WEIGHT = 1_150_000_000


def call(kernel, outs, in_specs, args, name, scratch=(), out_specs=None, limit=16, aliases=None):
    return pl.pallas_call(
        kernel,
        out_shape=outs,
        in_specs=in_specs,
        out_specs=out_specs if out_specs is not None else jax.tree.map(lambda _: VMEM, outs),
        scratch_shapes=list(scratch),
        compiler_params=pltpu.CompilerParams(vmem_limit_bytes=int(limit * 1024 * 1024)),
        input_output_aliases=aliases or {},
        cost_estimate=pl.CostEstimate(
            flops=int(WEIGHTS.get(name, 0.01) * FLOPS_PER_WEIGHT), bytes_accessed=0, transcendentals=0
        ),
        name=name,
    )(*args)


def turn_tables(places, steps):
    half = HEAD // 2
    freq = 10000.0 ** (-jnp.arange(half, dtype=F32) / half)
    cos, sin = [], []
    for step in range(steps):
        angle = (places + float(step))[:, None] * freq[None, :]
        c, s = jnp.cos(angle), jnp.sin(angle)
        cos.append(jnp.concatenate([c, c], axis=-1))
        sin.append(jnp.concatenate([-s, s], axis=-1))
    return jnp.concatenate(cos), jnp.concatenate(sin)


def bits_of(n):
    return [b for b in range(n.bit_length() - 1)]


def build(n_dp, n_roll, n_tp):
    z_bits = [("roll", b) for b in bits_of(n_roll)]
    x_bits = [("dp", b) for b in bits_of(n_dp)]
    sizes = {"dp": n_dp, "roll": n_roll}

    def cross(x, axis, bit):
        return swap(x, axis, sizes[axis], 1 << bit)

    path_a, path_b = z_bits + x_bits + z_bits[:1], x_bits[:1] + z_bits + x_bits[1:] + x_bits[:1]

    def on_device(
        train_inputs, train_cotangent, factor_a, factor_b, base_weight, incoming, norm_gain, positions
    ):
        steps, rows, width = incoming.shape
        tokens = train_inputs.shape[0]
        rank = factor_a.shape[1]
        count = steps * rows
        dma = lambda n: pltpu.SemaphoreType.DMA((n,))
        vmem = lambda n, dtype=F32: pltpu.VMEM((n, rank), dtype)

        tall = shape((count, width), BF)
        low_shape = shape((tokens, rank), BF)
        part_v, inputs, cotangent, half_a, hidden = call(
            rank_v_kernel,
            [low_shape, shape(train_inputs.shape, BF), shape(train_inputs.shape, BF), shape(factor_a.shape, BF), tall],
            [HBM] * 5,
            tuple(
                map(keep_hbm, (train_inputs, train_cotangent, factor_a, factor_b, incoming.reshape(count, width)))
            ),
            "rank_v",
            [pltpu.VMEM(factor_a.shape, F32), pltpu.VMEM(factor_b.shape, F32), dma(5)],
        )
        got_v = swap(part_v, "tp", n_tp, 1)
        part_u = call(rank_u_kernel, low_shape, [VMEM] * 2, (inputs, half_a), "rank_u")
        got_u = swap(part_u, "tp", n_tp, 1)
        cut = 512
        wide = shape((count, width + rank), BF)
        gained, low, sums = call(
            prep_kernel,
            [tall, shape((count, rank), BF), shape((8, LANES), F32)],
            [VMEM] * 3,
            (hidden, norm_gain[None, :], half_a),
            "prep",
        )
        low_v = call(part_kernel, low_shape, [VMEM] * 2 + [ANY], (part_v, got_v, low), "low_v")
        far_v = swap(low_v, "tp", n_tp, 2)
        low_u = call(part_kernel, low_shape, [VMEM] * 2 + [ANY], (part_u, got_u, low_v), "low_u")
        far_u = swap(low_u, "tp", n_tp, 2)

        def query(peers, outs, after, name):
            blocks = len(peers) * width // cut
            return call(
                functools.partial(query_kernel, peers),
                outs,
                [VMEM, HBM, ANY],
                (gained, keep_hbm(base_weight), after),
                "query_" + name,
                [pltpu.VMEM((blocks, width, cut), BF), dma(blocks)],
            )

        per = width // cut
        diag, columns = call(
            diag_kernel,
            [wide, shape((per, width, cut), BF)],
            [VMEM, HBM, VMEM, ANY],
            (gained, keep_hbm(base_weight), low, low_u),
            "query_diag",
            [pltpu.VMEM((per, width, cut), BF), dma(2 * per)],
        )
        diag_got = swap(diag, "tp", n_tp, 1)

        half = width // 2
        keep_a, send_a = call(
            functools.partial(grad_a_kernel, path_a[0]),
            [shape((half, rank), F32), shape((half, rank), BF)],
            [VMEM] * 3 + [ANY],
            (inputs, low_v, far_v, diag),
            "grad_a",
        )
        keep_b, send_b = call(
            functools.partial(grad_b_kernel, path_b[0]),
            [shape((half, rank), F32), shape((half, rank), BF)],
            [VMEM] * 3 + [ANY],
            (cotangent, low_u, far_u, send_a),
            "grad_b",
        )
        distant = call(distant_kernel, tall, [VMEM, VMEM, ANY], (gained, columns, send_b), "query_distant")
        far = call(far_kernel, wide, [VMEM] * 3 + [ANY], (distant, diag, diag_got, send_b), "far")
        far_got = swap(far, "tp", n_tp, 2)

        def step(mine, send, way, after, passed, name):
            return call(
                step_kernel,
                [shape((half, rank), BF)] + [shape(x.shape, x.dtype) for x in passed],
                [VMEM] * 2 + [ANY] * (1 + len(passed)),
                (mine, cross(send, *way), after, *passed),
                name,
                out_specs=[VMEM] + [ANY] * len(passed),
                aliases={3 + k: 1 + k for k in range(len(passed))},
            )

        mine_a, mine_b, after, passed = keep_a, keep_b, far, []
        order = ["a", "b", "n", "b", "a", "c", "t", "a", "b"] if n_dp * n_roll == 8 else ["a", "b", "n", "b", "t", "a", "c"] + ["a", "b"] * (len(path_a) - 3)
        steps_a, steps_b = iter(path_a[:-1]), iter(path_b[:-1])
        for i, which in enumerate(order):
            if which == "a":
                mine_a = send_a = after = step(mine_a, send_a, next(steps_a), after, [], f"step_a{i}")[0]
            elif which == "b":
                mine_b, *made = step(mine_b, send_b, next(steps_b), after, passed, f"step_b{i}")
                send_b = after = mine_b
                if made:
                    beside_got, passed = swap(made[0], "tp", n_tp, 1), []
            elif which == "t":
                pos = positions.reshape(-1, LANES)
                places = call(place_kernel, shape(pos.shape, F32), [VMEM, ANY], (pos, after), "places")
                cos, sin = turn_tables(places.reshape(rows), steps)
                after = sin
            elif which == "n":
                passed = query((1,), [tall], after, "beside")
            else:
                (close,) = query((0,), [tall], after, "close")
                after = close
        step_low, grad_a, squares = call(
            functools.partial(update_kernel, path_a[-1]),
            [shape((count, rank), BF), shape((width, rank), BF), shape((2, 8, LANES), F32)],
            [VMEM] * 4,
            (gained, mine_a, cross(mine_a, *path_a[-1]), mine_b),
            "update",
        )
        step_pack, grad_b = call(
            functools.partial(pack_kernel, path_b[-1]),
            [shape((count + EXTRA, rank), BF), shape((width, rank), BF)],
            [VMEM] * 5,
            (step_low, sums, squares, mine_b, cross(mine_b, *path_b[-1])),
            "pack",
        )
        step_got = swap(step_pack, "tp", n_tp, 1)
        step_sum = call(merge_kernel, shape((count + EXTRA, rank), BF), [VMEM] * 2, (step_pack, step_got), "merge")
        step_far = swap(step_sum, "tp", n_tp, 2)

        base, low_all = call(
            base_kernel,
            [shape((count, width), F32), shape((count, rank), F32)],
            [VMEM] * 4 + [ANY],
            (close, beside_got, far, far_got, step_sum),
            "base",
        )
        new_a, new_b, queries = call(
            final_kernel,
            [shape((width, rank), F32), shape((rank, width), F32), tall],
            [VMEM] * 10,
            (base, low_all, step_sum, step_far, grad_a, grad_b, factor_a, factor_b, cos, sin),
            "final",
            [pltpu.VMEM((width, rank), F32), pltpu.VMEM((rank, width), F32),
             pltpu.VMEM((rank, width), BF), pltpu.VMEM((count, width), BF), dma(2 + count // LANES)],
            [HBM] * 3,
        )
        return new_a, new_b, queries.reshape(steps, rows, width)

    return on_device


def solution(mesh):
    n_dp, n_roll, n_tp = (mesh.shape[a] for a in ("dp", "roll", "tp"))
    return jax.shard_map(
        build(n_dp, n_roll, n_tp),
        mesh=mesh,
        in_specs=(
            P(("dp", "roll"), "tp"),
            P(("dp", "roll"), "tp"),
            P("tp", None),
            P(None, "tp"),
            P("tp", None),
            P(None, ("dp", "roll"), "tp"),
            P("tp"),
            P(("dp", "roll")),
        ),
        out_specs=(P("tp", None), P(None, "tp"), P(None, ("dp", "roll"), "tp")),
        check_vma=False,
    )
```

```python
import functools

import jax
import jax.numpy as jnp
from jax import lax
from jax.experimental import pallas as pl
from jax.experimental.pallas import tpu as pltpu
from jax.sharding import PartitionSpec as P

D = 4096
HEAD = 128
SCALE = 2.0
LEARN = 3.0
EPS = 1e-05
NORM_EPS = 1e-06
LANES = 128
EXTRA = 32

BF = jnp.bfloat16
F32 = jnp.float32
VMEM = pl.BlockSpec(memory_space=pltpu.VMEM)
ANY = pl.BlockSpec(memory_space=pl.ANY)
HBM = pl.BlockSpec(memory_space=pltpu.HBM)


def shape(dims, dtype):
    return jax.ShapeDtypeStruct(dims, dtype)


def dot(a, b, dims=((1,), (0,))):
    return lax.dot_general(a, b, (dims, ((), ())), preferred_element_type=F32)


def swap(x, axis, n, k):
    return lax.ppermute(x, axis, [(i, i ^ k) for i in range(n)])


def split_terms(values):
    high = values.astype(BF)
    rest = values - high.astype(F32)
    middle = rest.astype(BF)
    last = (rest - middle.astype(F32)).astype(BF)
    return jnp.concatenate([high, middle, last, jnp.zeros_like(last)], axis=0)


def join_terms(terms):
    x = terms.astype(F32)
    return (x[0:8] + x[8:16]) + x[16:24]


def fetch(sources, targets, sems):
    copies = [pltpu.make_async_copy(s, t, sems.at[i]) for i, (s, t) in enumerate(zip(sources, targets))]
    for copy in copies:
        copy.start()
    return copies


def blocks_of(count):
    return [slice(i, i + LANES) for i in range(0, count, LANES)]


def rank_v_kernel(x_hbm, v_hbm, a_hbm, b_hbm, h_hbm, out_ref, x_ref, v_ref, a16_ref, h_ref, a_ref, b_ref, sems):
    copies = fetch((v_hbm, b_hbm, x_hbm, a_hbm, h_hbm), (v_ref, b_ref, x_ref, a_ref, h_ref), sems)
    copies[1].wait()
    b16 = b_ref[...].astype(BF)
    copies[0].wait()
    out_ref[...] = dot(v_ref[...], b16, ((1,), (1,))).astype(BF)
    copies[3].wait()
    a16_ref[...] = a_ref[...].astype(BF)
    copies[2].wait()
    copies[4].wait()


def rank_u_kernel(x_ref, a16_ref, out_ref):
    out_ref[...] = dot(x_ref[...], a16_ref[...]).astype(BF)


def weight_blocks(peers, w_hbm, w_ref):
    _, width, cut = w_ref.shape
    mine = lax.axis_index("tp")
    sources = []
    for peer in peers:
        for i in range(width // cut):
            start = (mine ^ peer) * width + i * cut
            sources.append(w_hbm.at[:, pl.ds(pl.multiple_of(start, cut), cut)])
    return sources, [w_ref.at[i] for i in range(len(sources))]


def prep_kernel(h_ref, gain_ref, a16_ref, hg_ref, low_ref, sums_ref):
    count, width = h_ref.shape
    rows = []
    for b in blocks_of(count):
        wide = h_ref[b].astype(F32)
        hg_ref[b] = (wide * gain_ref[...]).astype(BF)
        sums = jnp.sum(wide * wide, axis=-1, keepdims=True)
        rows.append(jnp.broadcast_to(sums, (LANES, LANES)).T[0:1])
    if len(rows) < 8:
        rows.append(jnp.zeros((8 - len(rows), LANES), F32))
    sums_ref[...] = jnp.concatenate(rows, axis=0)
    low_ref[...] = dot(hg_ref[...], a16_ref[...]).astype(BF)


def part_kernel(x_ref, got_ref, after_ref, out_ref):
    sum_kernel(x_ref, got_ref, out_ref)


def query_kernel(peers, hg_ref, w_hbm, after_ref, *rest):
    outs, (w_ref, sems) = rest[:-2], rest[-2:]
    _, width, cut = w_ref.shape
    copies = fetch(*weight_blocks(peers, w_hbm, w_ref), sems)
    per = width // cut
    for i, copy in enumerate(copies):
        copy.wait()
        outs[i // per][:, i % per * cut : (i % per + 1) * cut] = dot(hg_ref[...], w_ref[i]).astype(BF)


def diag_first_kernel(hg_ref, w_hbm, after_ref, out_ref, rest_ref, next_ref, w_ref, sems):
    width, cut = w_ref.shape
    mine, _ = weight_blocks((3,), w_hbm, next_ref)
    later, targets = weight_blocks((2,), w_hbm, next_ref)
    copies = fetch(mine + later, [w_ref] + [rest_ref.at[i] for i in range(len(mine) - 1)] + targets, sems)
    copies[0].wait()
    out_ref[...] = dot(hg_ref[...], w_ref[...]).astype(BF)
    for copy in copies[1:]:
        copy.wait()


def diag_kernel(hg_ref, w_ref, first_ref, low_ref, after_ref, out_ref):
    per, width, cut = w_ref.shape
    out_ref[:, :cut] = first_ref[...]
    for i in range(per):
        out_ref[:, (i + 1) * cut : (i + 2) * cut] = dot(hg_ref[...], w_ref[i]).astype(BF)
    out_ref[:, width:] = low_ref[...]


def distant_kernel(hg_ref, w_ref, after_ref, out_ref):
    per, _, cut = w_ref.shape
    for i in range(per):
        out_ref[:, i * cut : (i + 1) * cut] = dot(hg_ref[...], w_ref[i]).astype(BF)


def far_kernel(mine_ref, diag_ref, got_ref, after_ref, out_ref):
    width = mine_ref.shape[1]
    sum_kernel(mine_ref, got_ref.at[:, :width], out_ref.at[:, :width])
    sum_kernel(diag_ref.at[:, width:], got_ref.at[:, width:], out_ref.at[:, width:])


def merge_kernel(a_ref, b_ref, out_ref):
    count = a_ref.shape[0] - EXTRA
    out_ref[:count] = (a_ref[:count].astype(F32) + b_ref[:count].astype(F32)).astype(BF)
    out_ref[count:] = split_terms(join_terms(a_ref[count:]) + join_terms(b_ref[count:]))


def halves(axis, bit, size):
    mine = lax.rem(lax.axis_index(axis) // (1 << bit), 2) * size
    return pl.ds(pl.multiple_of(mine, size), size), pl.ds(pl.multiple_of(size - mine, size), size)


def join(axis, bit, mine_ref, got_ref, out_ref):
    mine, other = halves(axis, bit, mine_ref.shape[0])
    out_ref[mine] = mine_ref[...]
    out_ref[other] = got_ref[...]


def grad_a_kernel(way, x_ref, s_ref, r_ref, after_ref, keep_ref, send_ref):
    low = (s_ref[...].astype(F32) + r_ref[...].astype(F32)).astype(BF)
    mine, other = halves(*way, x_ref.shape[1] // 2)
    send_ref[...] = (SCALE * dot(x_ref[:, other], low, ((0,), (0,)))).astype(BF)
    keep_ref[...] = SCALE * dot(x_ref[:, mine], low, ((0,), (0,)))


def grad_b_kernel(way, v_ref, s_ref, r_ref, after_ref, keep_ref, send_ref):
    low = (s_ref[...].astype(F32) + r_ref[...].astype(F32)).astype(BF)
    mine, other = halves(*way, v_ref.shape[1] // 2)
    sent = (SCALE * dot(low, v_ref[:, other], ((0,), (0,)))).astype(BF)
    kept = SCALE * dot(low, v_ref[:, mine], ((0,), (0,)))
    for b in blocks_of(v_ref.shape[1] // 2):
        send_ref[b] = sent[:, b]
        keep_ref[b] = kept[:, b]


def sum_kernel(keep_ref, got_ref, out_ref):
    out_ref[...] = (keep_ref[...].astype(F32) + got_ref[...].astype(F32)).astype(BF)


def step_kernel(mine_ref, got_ref, *rest):
    sum_kernel(mine_ref, got_ref, rest[len(rest) // 2])


def place_kernel(pos_ref, after_ref, out_ref):
    out_ref[...] = pos_ref[...].astype(F32)


def square_sum(ref):
    x = ref[...].astype(F32)
    return jnp.broadcast_to(jnp.sum(x * x), (8, LANES))


def update_kernel(way, hg_ref, mine_a, got_a, mine_b, after_ref, low_ref, ga_ref, squares_ref):
    join(*way, mine_a, got_a, ga_ref)
    low_ref[...] = dot(hg_ref[...], ga_ref[...]).astype(BF)
    squares_ref[0] = square_sum(mine_a) + square_sum(got_a)
    squares_ref[1] = square_sum(mine_b)


def pack_kernel(way, low_ref, sums_ref, squares_ref, mine_b, got_b, pack_ref, gb_ref):
    count = low_ref.shape[0]
    pack_ref[:count] = low_ref[...]
    row = lax.broadcasted_iota(jnp.int32, (8, LANES), 0)
    squares = squares_ref[0] + (squares_ref[1] + square_sum(got_b))
    pack_ref[count:] = split_terms(jnp.where(row == 7, squares, sums_ref[...]))
    join(*way, mine_b, got_b, gb_ref)


def base_kernel(mine_ref, near_ref, far_ref, far_got, after_ref, base_ref, low_ref):
    width = mine_ref.shape[1]
    low_ref[...] = far_ref[:, width:].astype(F32) + far_got[:, width:].astype(F32)
    for c in blocks_of(width):
        base_ref[:, c] = mine_ref[:, c].astype(F32) + near_ref[:, c].astype(F32) + far_got[:, c].astype(F32)


def final_kernel(
    base_ref, low_ref, s_ref, r_ref, ga_ref, gb_ref, a_ref, b_ref, cos_ref, sin_ref,
    a_hbm, b_hbm, q_hbm, new_a, new_b, half_b, out, sems,
):
    count, width = base_ref.shape
    total = join_terms(s_ref[count:]) + join_terms(r_ref[count:])
    rate = (LEARN * lax.rsqrt(total + NORM_EPS))[7:8]
    scales = lax.rsqrt(total / D + EPS)
    for c in blocks_of(width):
        fresh = b_ref[:, c] - rate * gb_ref[c].astype(F32)
        new_b[:, c] = fresh
        half_b[:, c] = fresh.astype(BF)
    copies = [pltpu.make_async_copy(new_b, b_hbm, sems.at[0])]
    copies[-1].start()
    new_a[...] = a_ref[...] - rate * ga_ref[...].astype(F32)
    copies.append(pltpu.make_async_copy(new_a, a_hbm, sems.at[1]))
    copies[-1].start()
    for i, b in enumerate(blocks_of(count)):
        low = s_ref[b].astype(F32) + r_ref[b].astype(F32)
        scale = jnp.broadcast_to(scales[i : i + 1], (LANES, LANES)).T
        mix = (low_ref[b] - rate * low) * scale * SCALE
        update = dot(mix.astype(BF), half_b[...])
        cos, sin = cos_ref[b], sin_ref[b]
        for c in blocks_of(width):
            query = base_ref[b, c] * scale + update[:, c]
            other = pltpu.roll(query, HEAD // 2, 1)
            out[b, c] = (query * cos + other * sin).astype(BF)
        copies.append(pltpu.make_async_copy(out.at[b], q_hbm.at[b], sems.at[2 + i]))
        copies[-1].start()
    for copy in copies:
        copy.wait()


def keep_hbm(x):
    return pltpu.with_memory_space_constraint(x, pltpu.HBM)


WEIGHTS = {
    "rank_v": 2.4, "prep": 0.6, "diag_first": 40.0, "query_beside": 2.7, "query_close": 2.7, "grad_b": 40.0, "final": 1.8,
}
FLOPS_PER_WEIGHT = 1_150_000_000


def call(kernel, outs, in_specs, args, name, scratch=(), out_specs=None, limit=16, aliases=None):
    return pl.pallas_call(
        kernel,
        out_shape=outs,
        in_specs=in_specs,
        out_specs=out_specs if out_specs is not None else jax.tree.map(lambda _: VMEM, outs),
        scratch_shapes=list(scratch),
        compiler_params=pltpu.CompilerParams(vmem_limit_bytes=int(limit * 1024 * 1024)),
        input_output_aliases=aliases or {},
        cost_estimate=pl.CostEstimate(
            flops=int(WEIGHTS.get(name, 0.01) * FLOPS_PER_WEIGHT), bytes_accessed=0, transcendentals=0
        ),
        name=name,
    )(*args)


def turn_tables(places, steps):
    half = HEAD // 2
    freq = 10000.0 ** (-jnp.arange(half, dtype=F32) / half)
    cos, sin = [], []
    for step in range(steps):
        angle = (places + float(step))[:, None] * freq[None, :]
        c, s = jnp.cos(angle), jnp.sin(angle)
        cos.append(jnp.concatenate([c, c], axis=-1))
        sin.append(jnp.concatenate([-s, s], axis=-1))
    return jnp.concatenate(cos), jnp.concatenate(sin)


def bits_of(n):
    return [b for b in range(n.bit_length() - 1)]


def build(n_dp, n_roll, n_tp):
    z_bits = [("roll", b) for b in bits_of(n_roll)]
    x_bits = [("dp", b) for b in bits_of(n_dp)]
    sizes = {"dp": n_dp, "roll": n_roll}

    def cross(x, axis, bit):
        return swap(x, axis, sizes[axis], 1 << bit)

    path_a, path_b = z_bits + x_bits + z_bits[:1], x_bits[:1] + z_bits + x_bits[1:] + x_bits[:1]

    def on_device(
        train_inputs, train_cotangent, factor_a, factor_b, base_weight, incoming, norm_gain, positions
    ):
        steps, rows, width = incoming.shape
        tokens = train_inputs.shape[0]
        rank = factor_a.shape[1]
        count = steps * rows
        dma = lambda n: pltpu.SemaphoreType.DMA((n,))
        vmem = lambda n, dtype=F32: pltpu.VMEM((n, rank), dtype)

        tall = shape((count, width), BF)
        low_shape = shape((tokens, rank), BF)
        part_v, inputs, cotangent, half_a, hidden = call(
            rank_v_kernel,
            [low_shape, shape(train_inputs.shape, BF), shape(train_inputs.shape, BF), shape(factor_a.shape, BF), tall],
            [HBM] * 5,
            tuple(
                map(keep_hbm, (train_inputs, train_cotangent, factor_a, factor_b, incoming.reshape(count, width)))
            ),
            "rank_v",
            [pltpu.VMEM(factor_a.shape, F32), pltpu.VMEM(factor_b.shape, F32), dma(5)],
        )
        got_v = swap(part_v, "tp", n_tp, 1)
        part_u = call(rank_u_kernel, low_shape, [VMEM] * 2, (inputs, half_a), "rank_u")
        got_u = swap(part_u, "tp", n_tp, 1)
        cut = 512
        wide = shape((count, width + rank), BF)
        gained, low, sums = call(
            prep_kernel,
            [tall, shape((count, rank), BF), shape((8, LANES), F32)],
            [VMEM] * 3,
            (hidden, norm_gain[None, :], half_a),
            "prep",
        )
        low_v = call(part_kernel, low_shape, [VMEM] * 2 + [ANY], (part_v, got_v, low), "low_v")
        far_v = swap(low_v, "tp", n_tp, 2)
        low_u = call(part_kernel, low_shape, [VMEM] * 2 + [ANY], (part_u, got_u, low_v), "low_u")
        far_u = swap(low_u, "tp", n_tp, 2)

        def query(peers, outs, after, name):
            blocks = len(peers) * width // cut
            return call(
                functools.partial(query_kernel, peers),
                outs,
                [VMEM, HBM, ANY],
                (gained, keep_hbm(base_weight), after),
                "query_" + name,
                [pltpu.VMEM((blocks, width, cut), BF), dma(blocks)],
            )

        per = width // cut
        diag_first, rest, columns = call(
            diag_first_kernel,
            [shape((count, cut), BF), shape((per - 1, width, cut), BF), shape((per, width, cut), BF)],
            [VMEM, HBM, ANY],
            (gained, keep_hbm(base_weight), low_u),
            "diag_first",
            [pltpu.VMEM((width, cut), BF), dma(2 * per)],
        )
        half = width // 2
        keep_a, send_a = call(
            functools.partial(grad_a_kernel, path_a[0]),
            [shape((half, rank), F32), shape((half, rank), BF)],
            [VMEM] * 3 + [ANY],
            (inputs, low_v, far_v, diag_first),
            "grad_a",
        )
        diag = call(
            diag_kernel, wide, [VMEM] * 4 + [ANY], (gained, rest, diag_first, low, send_a), "query_diag"
        )
        diag_got = swap(diag, "tp", n_tp, 1)
        keep_b, send_b = call(
            functools.partial(grad_b_kernel, path_b[0]),
            [shape((half, rank), F32), shape((half, rank), BF)],
            [VMEM] * 3 + [ANY],
            (cotangent, low_u, far_u, diag),
            "grad_b",
        )
        distant = call(distant_kernel, tall, [VMEM, VMEM, ANY], (gained, columns, send_b), "query_distant")
        far = call(far_kernel, wide, [VMEM] * 3 + [ANY], (distant, diag, diag_got, send_b), "far")
        far_got = swap(far, "tp", n_tp, 2)

        def step(mine, send, way, after, passed, name):
            return call(
                step_kernel,
                [shape((half, rank), BF)] + [shape(x.shape, x.dtype) for x in passed],
                [VMEM] * 2 + [ANY] * (1 + len(passed)),
                (mine, cross(send, *way), after, *passed),
                name,
                out_specs=[VMEM] + [ANY] * len(passed),
                aliases={3 + k: 1 + k for k in range(len(passed))},
            )

        mine_a, mine_b, after, passed = keep_a, keep_b, far, []
        order = ["a", "b", "n", "b", "a", "c", "a", "b", "t"] if n_dp * n_roll == 8 else ["a", "b", "n", "b", "a", "c"] + ["a", "b"] * (len(path_a) - 3) + ["t"]
        steps_a, steps_b = iter(path_a[:-1]), iter(path_b[:-1])
        for i, which in enumerate(order):
            if which == "a":
                mine_a, *made = step(mine_a, send_a, next(steps_a), after, passed, f"step_a{i}")
                send_a = after = mine_a
                if made:
                    beside_got, passed = swap(made[0], "tp", n_tp, 1), []
            elif which == "b":
                mine_b = send_b = after = step(mine_b, send_b, next(steps_b), after, [], f"step_b{i}")[0]
            elif which == "t":
                pos = positions.reshape(-1, LANES)
                places = call(place_kernel, shape(pos.shape, F32), [VMEM, ANY], (pos, after), "places")
                cos, sin = turn_tables(places.reshape(rows), steps)
                after = sin
            elif which == "n":
                passed = query((1,), [tall], after, "beside")
            else:
                (close,) = query((0,), [tall], after, "close")
                after = close
        step_low, grad_a, squares = call(
            functools.partial(update_kernel, path_a[-1]),
            [shape((count, rank), BF), shape((width, rank), BF), shape((2, 8, LANES), F32)],
            [VMEM] * 4 + [ANY],
            (gained, mine_a, cross(mine_a, *path_a[-1]), mine_b, after),
            "update",
        )
        step_pack, grad_b = call(
            functools.partial(pack_kernel, path_b[-1]),
            [shape((count + EXTRA, rank), BF), shape((width, rank), BF)],
            [VMEM] * 5,
            (step_low, sums, squares, mine_b, cross(mine_b, *path_b[-1])),
            "pack",
        )
        step_got = swap(step_pack, "tp", n_tp, 1)
        step_sum = call(merge_kernel, shape((count + EXTRA, rank), BF), [VMEM] * 2, (step_pack, step_got), "merge")
        step_far = swap(step_sum, "tp", n_tp, 2)

        base, low_all = call(
            base_kernel,
            [shape((count, width), F32), shape((count, rank), F32)],
            [VMEM] * 4 + [ANY],
            (close, beside_got, far, far_got, step_sum),
            "base",
        )
        new_a, new_b, queries = call(
            final_kernel,
            [shape((width, rank), F32), shape((rank, width), F32), tall],
            [VMEM] * 10,
            (base, low_all, step_sum, step_far, grad_a, grad_b, factor_a, factor_b, cos, sin),
            "final",
            [pltpu.VMEM((width, rank), F32), pltpu.VMEM((rank, width), F32),
             pltpu.VMEM((rank, width), BF), pltpu.VMEM((count, width), BF), dma(2 + count // LANES)],
            [HBM] * 3,
        )
        return new_a, new_b, queries.reshape(steps, rows, width)

    return on_device


def solution(mesh):
    n_dp, n_roll, n_tp = (mesh.shape[a] for a in ("dp", "roll", "tp"))
    return jax.shard_map(
        build(n_dp, n_roll, n_tp),
        mesh=mesh,
        in_specs=(
            P(("dp", "roll"), "tp"),
            P(("dp", "roll"), "tp"),
            P("tp", None),
            P(None, "tp"),
            P("tp", None),
            P(None, ("dp", "roll"), "tp"),
            P("tp"),
            P(("dp", "roll")),
        ),
        out_specs=(P("tp", None), P(None, "tp"), P(None, ("dp", "roll"), "tp")),
        check_vma=False,
    )
```

```python
import functools

import jax
import jax.numpy as jnp
from jax import lax
from jax.experimental import pallas as pl
from jax.experimental.pallas import tpu as pltpu
from jax.sharding import PartitionSpec as P

D = 4096
HEAD = 128
SCALE = 2.0
LEARN = 3.0
EPS = 1e-05
NORM_EPS = 1e-06
LANES = 128
EXTRA = 32

BF = jnp.bfloat16
F32 = jnp.float32
VMEM = pl.BlockSpec(memory_space=pltpu.VMEM)
ANY = pl.BlockSpec(memory_space=pl.ANY)
HBM = pl.BlockSpec(memory_space=pltpu.HBM)


def shape(dims, dtype):
    return jax.ShapeDtypeStruct(dims, dtype)


def dot(a, b, dims=((1,), (0,))):
    return lax.dot_general(a, b, (dims, ((), ())), preferred_element_type=F32)


def swap(x, axis, n, k):
    return lax.ppermute(x, axis, [(i, i ^ k) for i in range(n)])


def split_terms(values):
    high = values.astype(BF)
    rest = values - high.astype(F32)
    middle = rest.astype(BF)
    last = (rest - middle.astype(F32)).astype(BF)
    return jnp.concatenate([high, middle, last, jnp.zeros_like(last)], axis=0)


def join_terms(terms):
    x = terms.astype(F32)
    return (x[0:8] + x[8:16]) + x[16:24]


def fetch(sources, targets, sems):
    copies = [pltpu.make_async_copy(s, t, sems.at[i]) for i, (s, t) in enumerate(zip(sources, targets))]
    for copy in copies:
        copy.start()
    return copies


def blocks_of(count):
    return [slice(i, i + LANES) for i in range(0, count, LANES)]


def rank_v_kernel(
    x_hbm, v_hbm, a_hbm, b_hbm, h_hbm, w_hbm, out_ref, x_ref, v_ref, a16_ref, h_ref, w_ref, a_ref, b_ref, sems
):
    first = weight_blocks((3,), w_hbm, w_ref.shape[1])[0]
    copies = fetch((v_hbm, b_hbm, x_hbm, a_hbm, h_hbm, first), (v_ref, b_ref, x_ref, a_ref, h_ref, w_ref), sems)
    copies[1].wait()
    b16 = b_ref[...].astype(BF)
    copies[0].wait()
    out_ref[...] = dot(v_ref[...], b16, ((1,), (1,))).astype(BF)
    copies[3].wait()
    a16_ref[...] = a_ref[...].astype(BF)
    for i in (2, 4, 5):
        copies[i].wait()


def rank_u_kernel(x_ref, a16_ref, out_ref):
    out_ref[...] = dot(x_ref[...], a16_ref[...]).astype(BF)


def weight_blocks(peers, w_hbm, cut):
    width = w_hbm.shape[0]
    mine = lax.axis_index("tp")
    sources = []
    for peer in peers:
        for i in range(width // cut):
            start = (mine ^ peer) * width + i * cut
            sources.append(w_hbm.at[:, pl.ds(pl.multiple_of(start, cut), cut)])
    return sources


def prep_kernel(h_ref, gain_ref, a16_ref, hg_ref, low_ref, sums_ref):
    count, width = h_ref.shape
    rows = []
    for b in blocks_of(count):
        wide = h_ref[b].astype(F32)
        hg_ref[b] = (wide * gain_ref[...]).astype(BF)
        sums = jnp.sum(wide * wide, axis=-1, keepdims=True)
        rows.append(jnp.broadcast_to(sums, (LANES, LANES)).T[0:1])
    if len(rows) < 8:
        rows.append(jnp.zeros((8 - len(rows), LANES), F32))
    sums_ref[...] = jnp.concatenate(rows, axis=0)
    low_ref[...] = dot(hg_ref[...], a16_ref[...]).astype(BF)


def part_kernel(x_ref, got_ref, after_ref, out_ref):
    sum_kernel(x_ref, got_ref, out_ref)


def query_kernel(peers, hg_ref, w_hbm, after_ref, *rest):
    outs, (w_ref, sems) = rest[:-2], rest[-2:]
    _, width, cut = w_ref.shape
    copies = fetch(weight_blocks(peers, w_hbm, cut), [w_ref.at[i] for i in range(w_ref.shape[0])], sems)
    per = width // cut
    for i, copy in enumerate(copies):
        copy.wait()
        outs[i // per][:, i % per * cut : (i % per + 1) * cut] = dot(hg_ref[...], w_ref[i]).astype(BF)


def diag_kernel(hg_ref, w_ref, w_hbm, low_ref, after_ref, out_ref, next_ref, rest_ref, sems):
    per, width, cut = next_ref.shape
    sources = weight_blocks((3, 2), w_hbm, cut)[1:]
    targets = [rest_ref.at[i] for i in range(per - 1)] + [next_ref.at[i] for i in range(per)]
    copies = fetch(sources, targets, sems)
    out_ref[:, :cut] = dot(hg_ref[...], w_ref[...]).astype(BF)
    out_ref[:, width:] = low_ref[...]
    for i in range(1, per):
        copies[i - 1].wait()
        out_ref[:, i * cut : (i + 1) * cut] = dot(hg_ref[...], rest_ref[i - 1]).astype(BF)
    for copy in copies[per - 1 :]:
        copy.wait()


def distant_kernel(hg_ref, w_ref, after_ref, out_ref):
    per, _, cut = w_ref.shape
    for i in range(per):
        out_ref[:, i * cut : (i + 1) * cut] = dot(hg_ref[...], w_ref[i]).astype(BF)


def far_kernel(mine_ref, diag_ref, got_ref, after_ref, out_ref):
    width = mine_ref.shape[1]
    sum_kernel(mine_ref, got_ref.at[:, :width], out_ref.at[:, :width])
    sum_kernel(diag_ref.at[:, width:], got_ref.at[:, width:], out_ref.at[:, width:])


def merge_kernel(a_ref, b_ref, out_ref):
    count = a_ref.shape[0] - EXTRA
    out_ref[:count] = (a_ref[:count].astype(F32) + b_ref[:count].astype(F32)).astype(BF)
    out_ref[count:] = split_terms(join_terms(a_ref[count:]) + join_terms(b_ref[count:]))


def halves(axis, bit, size):
    mine = lax.rem(lax.axis_index(axis) // (1 << bit), 2) * size
    return pl.ds(pl.multiple_of(mine, size), size), pl.ds(pl.multiple_of(size - mine, size), size)


def join(axis, bit, mine_ref, got_ref, out_ref):
    mine, other = halves(axis, bit, mine_ref.shape[0])
    out_ref[mine] = mine_ref[...]
    out_ref[other] = got_ref[...]


def grad_a_kernel(way, x_ref, s_ref, r_ref, after_ref, keep_ref, send_ref):
    low = (s_ref[...].astype(F32) + r_ref[...].astype(F32)).astype(BF)
    mine, other = halves(*way, x_ref.shape[1] // 2)
    send_ref[...] = (SCALE * dot(x_ref[:, other], low, ((0,), (0,)))).astype(BF)
    keep_ref[...] = SCALE * dot(x_ref[:, mine], low, ((0,), (0,)))


def grad_b_kernel(way, v_ref, s_ref, r_ref, after_ref, keep_ref, send_ref):
    low = (s_ref[...].astype(F32) + r_ref[...].astype(F32)).astype(BF)
    mine, other = halves(*way, v_ref.shape[1] // 2)
    sent = (SCALE * dot(low, v_ref[:, other], ((0,), (0,)))).astype(BF)
    kept = SCALE * dot(low, v_ref[:, mine], ((0,), (0,)))
    for b in blocks_of(v_ref.shape[1] // 2):
        send_ref[b] = sent[:, b]
        keep_ref[b] = kept[:, b]


def sum_kernel(keep_ref, got_ref, out_ref):
    out_ref[...] = (keep_ref[...].astype(F32) + got_ref[...].astype(F32)).astype(BF)


def step_kernel(mine_ref, got_ref, *rest):
    sum_kernel(mine_ref, got_ref, rest[len(rest) // 2])


def place_kernel(pos_ref, after_ref, out_ref):
    out_ref[...] = pos_ref[...].astype(F32)


def square_sum(ref):
    x = ref[...].astype(F32)
    return jnp.broadcast_to(jnp.sum(x * x), (8, LANES))


def update_kernel(way, hg_ref, mine_a, got_a, mine_b, after_ref, low_ref, ga_ref, squares_ref):
    join(*way, mine_a, got_a, ga_ref)
    low_ref[...] = dot(hg_ref[...], ga_ref[...]).astype(BF)
    squares_ref[0] = square_sum(mine_a) + square_sum(got_a)
    squares_ref[1] = square_sum(mine_b)


def pack_kernel(way, low_ref, sums_ref, squares_ref, mine_b, got_b, pack_ref, gb_ref):
    count = low_ref.shape[0]
    pack_ref[:count] = low_ref[...]
    row = lax.broadcasted_iota(jnp.int32, (8, LANES), 0)
    squares = squares_ref[0] + (squares_ref[1] + square_sum(got_b))
    pack_ref[count:] = split_terms(jnp.where(row == 7, squares, sums_ref[...]))
    join(*way, mine_b, got_b, gb_ref)


def base_kernel(mine_ref, near_ref, far_ref, far_got, after_ref, base_ref, low_ref):
    width = mine_ref.shape[1]
    low_ref[...] = far_ref[:, width:].astype(F32) + far_got[:, width:].astype(F32)
    for c in blocks_of(width):
        base_ref[:, c] = mine_ref[:, c].astype(F32) + near_ref[:, c].astype(F32) + far_got[:, c].astype(F32)


def final_kernel(
    base_ref, low_ref, s_ref, r_ref, ga_ref, gb_ref, a_ref, b_ref, cos_ref, sin_ref,
    a_hbm, b_hbm, q_hbm, new_a, new_b, half_b, out, sems,
):
    count, width = base_ref.shape
    total = join_terms(s_ref[count:]) + join_terms(r_ref[count:])
    rate = (LEARN * lax.rsqrt(total + NORM_EPS))[7:8]
    scales = lax.rsqrt(total / D + EPS)
    for c in blocks_of(width):
        fresh = b_ref[:, c] - rate * gb_ref[c].astype(F32)
        new_b[:, c] = fresh
        half_b[:, c] = fresh.astype(BF)
    copies = [pltpu.make_async_copy(new_b, b_hbm, sems.at[0])]
    copies[-1].start()
    new_a[...] = a_ref[...] - rate * ga_ref[...].astype(F32)
    copies.append(pltpu.make_async_copy(new_a, a_hbm, sems.at[1]))
    copies[-1].start()
    for i, b in enumerate(blocks_of(count)):
        low = s_ref[b].astype(F32) + r_ref[b].astype(F32)
        scale = jnp.broadcast_to(scales[i : i + 1], (LANES, LANES)).T
        mix = (low_ref[b] - rate * low) * scale * SCALE
        update = dot(mix.astype(BF), half_b[...])
        cos, sin = cos_ref[b], sin_ref[b]
        for c in blocks_of(width):
            query = base_ref[b, c] * scale + update[:, c]
            other = pltpu.roll(query, HEAD // 2, 1)
            out[b, c] = (query * cos + other * sin).astype(BF)
        copies.append(pltpu.make_async_copy(out.at[b], q_hbm.at[b], sems.at[2 + i]))
        copies[-1].start()
    for copy in copies:
        copy.wait()


def keep_hbm(x):
    return pltpu.with_memory_space_constraint(x, pltpu.HBM)


WEIGHTS = {"rank_v": 2.4, "prep": 0.6, "query_diag": 40.0, "query_beside": 2.7, "query_close": 2.7, "grad_b": 40.0, "final": 1.8}
FLOPS_PER_WEIGHT = 1_150_000_000


def call(kernel, outs, in_specs, args, name, scratch=(), out_specs=None, limit=16, aliases=None):
    return pl.pallas_call(
        kernel,
        out_shape=outs,
        in_specs=in_specs,
        out_specs=out_specs if out_specs is not None else jax.tree.map(lambda _: VMEM, outs),
        scratch_shapes=list(scratch),
        compiler_params=pltpu.CompilerParams(vmem_limit_bytes=int(limit * 1024 * 1024)),
        input_output_aliases=aliases or {},
        cost_estimate=pl.CostEstimate(
            flops=int(WEIGHTS.get(name, 0.01) * FLOPS_PER_WEIGHT), bytes_accessed=0, transcendentals=0
        ),
        name=name,
    )(*args)


def turn_tables(places, steps):
    half = HEAD // 2
    freq = 10000.0 ** (-jnp.arange(half, dtype=F32) / half)
    cos, sin = [], []
    for step in range(steps):
        angle = (places + float(step))[:, None] * freq[None, :]
        c, s = jnp.cos(angle), jnp.sin(angle)
        cos.append(jnp.concatenate([c, c], axis=-1))
        sin.append(jnp.concatenate([-s, s], axis=-1))
    return jnp.concatenate(cos), jnp.concatenate(sin)


def bits_of(n):
    return [b for b in range(n.bit_length() - 1)]


def build(n_dp, n_roll, n_tp):
    z_bits = [("roll", b) for b in bits_of(n_roll)]
    x_bits = [("dp", b) for b in bits_of(n_dp)]
    sizes = {"dp": n_dp, "roll": n_roll}

    def cross(x, axis, bit):
        return swap(x, axis, sizes[axis], 1 << bit)

    path_a, path_b = z_bits + x_bits + z_bits[:1], x_bits[:1] + z_bits + x_bits[1:] + x_bits[:1]

    def on_device(
        train_inputs, train_cotangent, factor_a, factor_b, base_weight, incoming, norm_gain, positions
    ):
        steps, rows, width = incoming.shape
        tokens = train_inputs.shape[0]
        rank = factor_a.shape[1]
        count = steps * rows
        dma = lambda n: pltpu.SemaphoreType.DMA((n,))
        vmem = lambda n, dtype=F32: pltpu.VMEM((n, rank), dtype)

        cut = 512
        tall = shape((count, width), BF)
        low_shape = shape((tokens, rank), BF)
        part_v, inputs, cotangent, half_a, hidden, first_columns = call(
            rank_v_kernel,
            [low_shape, shape(train_inputs.shape, BF), shape(train_inputs.shape, BF), shape(factor_a.shape, BF), tall,
             shape((width, cut), BF)],
            [HBM] * 6,
            tuple(
                map(
                    keep_hbm,
                    (train_inputs, train_cotangent, factor_a, factor_b, incoming.reshape(count, width), base_weight),
                )
            ),
            "rank_v",
            [pltpu.VMEM(factor_a.shape, F32), pltpu.VMEM(factor_b.shape, F32), dma(6)],
        )
        got_v = swap(part_v, "tp", n_tp, 1)
        part_u = call(rank_u_kernel, low_shape, [VMEM] * 2, (inputs, half_a), "rank_u")
        got_u = swap(part_u, "tp", n_tp, 1)
        wide = shape((count, width + rank), BF)
        gained, low, sums = call(
            prep_kernel,
            [tall, shape((count, rank), BF), shape((8, LANES), F32)],
            [VMEM] * 3,
            (hidden, norm_gain[None, :], half_a),
            "prep",
        )
        low_v = call(part_kernel, low_shape, [VMEM] * 2 + [ANY], (part_v, got_v, low), "low_v")
        far_v = swap(low_v, "tp", n_tp, 2)
        low_u = call(part_kernel, low_shape, [VMEM] * 2 + [ANY], (part_u, got_u, low_v), "low_u")
        far_u = swap(low_u, "tp", n_tp, 2)

        def query(peers, outs, after, name):
            blocks = len(peers) * width // cut
            return call(
                functools.partial(query_kernel, peers),
                outs,
                [VMEM, HBM, ANY],
                (gained, keep_hbm(base_weight), after),
                "query_" + name,
                [pltpu.VMEM((blocks, width, cut), BF), dma(blocks)],
            )

        per = width // cut
        diag, columns = call(
            diag_kernel,
            [wide, shape((per, width, cut), BF)],
            [VMEM, VMEM, HBM, VMEM, ANY],
            (gained, first_columns, keep_hbm(base_weight), low, low_u),
            "query_diag",
            [pltpu.VMEM((per - 1, width, cut), BF), dma(2 * per - 1)],
        )
        diag_got = swap(diag, "tp", n_tp, 1)

        half = width // 2
        keep_a, send_a = call(
            functools.partial(grad_a_kernel, path_a[0]),
            [shape((half, rank), F32), shape((half, rank), BF)],
            [VMEM] * 3 + [ANY],
            (inputs, low_v, far_v, diag),
            "grad_a",
        )
        keep_b, send_b = call(
            functools.partial(grad_b_kernel, path_b[0]),
            [shape((half, rank), F32), shape((half, rank), BF)],
            [VMEM] * 3 + [ANY],
            (cotangent, low_u, far_u, send_a),
            "grad_b",
        )
        distant = call(distant_kernel, tall, [VMEM, VMEM, ANY], (gained, columns, send_b), "query_distant")
        far = call(far_kernel, wide, [VMEM] * 3 + [ANY], (distant, diag, diag_got, send_b), "far")
        far_got = swap(far, "tp", n_tp, 2)

        def step(mine, send, way, after, passed, name):
            return call(
                step_kernel,
                [shape((half, rank), BF)] + [shape(x.shape, x.dtype) for x in passed],
                [VMEM] * 2 + [ANY] * (1 + len(passed)),
                (mine, cross(send, *way), after, *passed),
                name,
                out_specs=[VMEM] + [ANY] * len(passed),
                aliases={3 + k: 1 + k for k in range(len(passed))},
            )

        mine_a, mine_b, after, passed = keep_a, keep_b, far, []
        order = ["a", "b", "n", "b", "a", "c", "a", "b", "t"] if n_dp * n_roll == 8 else ["a", "b", "n", "b", "a", "c"] + ["a", "b"] * (len(path_a) - 3) + ["t"]
        steps_a, steps_b = iter(path_a[:-1]), iter(path_b[:-1])
        for i, which in enumerate(order):
            if which == "a":
                mine_a, *made = step(mine_a, send_a, next(steps_a), after, passed, f"step_a{i}")
                send_a = after = mine_a
                if made:
                    beside_got, passed = swap(made[0], "tp", n_tp, 1), []
            elif which == "b":
                mine_b = send_b = after = step(mine_b, send_b, next(steps_b), after, [], f"step_b{i}")[0]
            elif which == "t":
                pos = positions.reshape(-1, LANES)
                places = call(place_kernel, shape(pos.shape, F32), [VMEM, ANY], (pos, after), "places")
                cos, sin = turn_tables(places.reshape(rows), steps)
                after = sin
            elif which == "n":
                passed = query((1,), [tall], after, "beside")
            else:
                (close,) = query((0,), [tall], after, "close")
                after = close
        step_low, grad_a, squares = call(
            functools.partial(update_kernel, path_a[-1]),
            [shape((count, rank), BF), shape((width, rank), BF), shape((2, 8, LANES), F32)],
            [VMEM] * 4 + [ANY],
            (gained, mine_a, cross(mine_a, *path_a[-1]), mine_b, after),
            "update",
        )
        step_pack, grad_b = call(
            functools.partial(pack_kernel, path_b[-1]),
            [shape((count + EXTRA, rank), BF), shape((width, rank), BF)],
            [VMEM] * 5,
            (step_low, sums, squares, mine_b, cross(mine_b, *path_b[-1])),
            "pack",
        )
        step_got = swap(step_pack, "tp", n_tp, 1)
        step_sum = call(merge_kernel, shape((count + EXTRA, rank), BF), [VMEM] * 2, (step_pack, step_got), "merge")
        step_far = swap(step_sum, "tp", n_tp, 2)

        base, low_all = call(
            base_kernel,
            [shape((count, width), F32), shape((count, rank), F32)],
            [VMEM] * 4 + [ANY],
            (close, beside_got, far, far_got, step_sum),
            "base",
        )
        new_a, new_b, queries = call(
            final_kernel,
            [shape((width, rank), F32), shape((rank, width), F32), tall],
            [VMEM] * 10,
            (base, low_all, step_sum, step_far, grad_a, grad_b, factor_a, factor_b, cos, sin),
            "final",
            [pltpu.VMEM((width, rank), F32), pltpu.VMEM((rank, width), F32),
             pltpu.VMEM((rank, width), BF), pltpu.VMEM((count, width), BF), dma(2 + count // LANES)],
            [HBM] * 3,
        )
        return new_a, new_b, queries.reshape(steps, rows, width)

    return on_device


def solution(mesh):
    n_dp, n_roll, n_tp = (mesh.shape[a] for a in ("dp", "roll", "tp"))
    return jax.shard_map(
        build(n_dp, n_roll, n_tp),
        mesh=mesh,
        in_specs=(
            P(("dp", "roll"), "tp"),
            P(("dp", "roll"), "tp"),
            P("tp", None),
            P(None, "tp"),
            P("tp", None),
            P(None, ("dp", "roll"), "tp"),
            P("tp"),
            P(("dp", "roll")),
        ),
        out_specs=(P("tp", None), P(None, "tp"), P(None, ("dp", "roll"), "tp")),
        check_vma=False,
    )
```

```python
import functools

import jax
import jax.numpy as jnp
from jax import lax
from jax.experimental import pallas as pl
from jax.experimental.pallas import tpu as pltpu
from jax.sharding import PartitionSpec as P

D = 4096
HEAD = 128
SCALE = 2.0
LEARN = 3.0
EPS = 1e-05
NORM_EPS = 1e-06
LANES = 128
EXTRA = 32

BF = jnp.bfloat16
F32 = jnp.float32
VMEM = pl.BlockSpec(memory_space=pltpu.VMEM)
ANY = pl.BlockSpec(memory_space=pl.ANY)
HBM = pl.BlockSpec(memory_space=pltpu.HBM)


def shape(dims, dtype):
    return jax.ShapeDtypeStruct(dims, dtype)


def dot(a, b, dims=((1,), (0,))):
    return lax.dot_general(a, b, (dims, ((), ())), preferred_element_type=F32)


def swap(x, axis, n, k):
    return lax.ppermute(x, axis, [(i, i ^ k) for i in range(n)])


def split_terms(values):
    high = values.astype(BF)
    rest = values - high.astype(F32)
    middle = rest.astype(BF)
    last = (rest - middle.astype(F32)).astype(BF)
    return jnp.concatenate([high, middle, last, jnp.zeros_like(last)], axis=0)


def join_terms(terms):
    x = terms.astype(F32)
    return (x[0:8] + x[8:16]) + x[16:24]


def fetch(sources, targets, sems):
    copies = [pltpu.make_async_copy(s, t, sems.at[i]) for i, (s, t) in enumerate(zip(sources, targets))]
    for copy in copies:
        copy.start()
    return copies


def blocks_of(count):
    return [slice(i, i + LANES) for i in range(0, count, LANES)]


def rank_v_kernel(
    x_hbm, v_hbm, a_hbm, b_hbm, h_hbm, w_hbm, out_ref, x_ref, v_ref, a16_ref, h_ref, w_ref, a_ref, b_ref, sems
):
    first = weight_blocks((3,), w_hbm, w_ref.shape[1])[0]
    copies = fetch((v_hbm, b_hbm, x_hbm, a_hbm, h_hbm, first), (v_ref, b_ref, x_ref, a_ref, h_ref, w_ref), sems)
    copies[1].wait()
    b16 = b_ref[...].astype(BF)
    copies[0].wait()
    out_ref[...] = dot(v_ref[...], b16, ((1,), (1,))).astype(BF)
    copies[3].wait()
    a16_ref[...] = a_ref[...].astype(BF)
    for i in (2, 4, 5):
        copies[i].wait()


def rank_u_kernel(x_ref, a16_ref, out_ref):
    out_ref[...] = dot(x_ref[...], a16_ref[...]).astype(BF)


def weight_blocks(peers, w_hbm, cut):
    width = w_hbm.shape[0]
    mine = lax.axis_index("tp")
    sources = []
    for peer in peers:
        for i in range(width // cut):
            start = (mine ^ peer) * width + i * cut
            sources.append(w_hbm.at[:, pl.ds(pl.multiple_of(start, cut), cut)])
    return sources


def prep_kernel(h_ref, gain_ref, a16_ref, hg_ref, low_ref, sums_ref):
    count, width = h_ref.shape
    rows = []
    for b in blocks_of(count):
        wide = h_ref[b].astype(F32)
        hg_ref[b] = (wide * gain_ref[...]).astype(BF)
        sums = jnp.sum(wide * wide, axis=-1, keepdims=True)
        rows.append(jnp.broadcast_to(sums, (LANES, LANES)).T[0:1])
    if len(rows) < 8:
        rows.append(jnp.zeros((8 - len(rows), LANES), F32))
    sums_ref[...] = jnp.concatenate(rows, axis=0)
    low_ref[...] = dot(hg_ref[...], a16_ref[...]).astype(BF)


def part_kernel(x_ref, got_ref, after_ref, out_ref):
    sum_kernel(x_ref, got_ref, out_ref)


def query_kernel(peers, hg_ref, w_hbm, after_ref, *rest):
    outs, (w_ref, sems) = rest[:-2], rest[-2:]
    _, width, cut = w_ref.shape
    copies = fetch(weight_blocks(peers, w_hbm, cut), [w_ref.at[i] for i in range(w_ref.shape[0])], sems)
    per = width // cut
    for i, copy in enumerate(copies):
        copy.wait()
        outs[i // per][:, i % per * cut : (i % per + 1) * cut] = dot(hg_ref[...], w_ref[i]).astype(BF)


def diag_kernel(hg_ref, w_ref, w_hbm, low_ref, after_ref, out_ref, *refs):
    *next_refs, rest_ref, sems = refs
    width, cut = w_ref.shape
    per = width // cut
    sources = weight_blocks((3, 2), w_hbm, cut)[1:]
    targets = [rest_ref.at[i] for i in range(per - 1)] + next_refs
    copies = fetch(sources, targets, sems)
    out_ref[:, :cut] = dot(hg_ref[...], w_ref[...]).astype(BF)
    out_ref[:, width:] = low_ref[...]
    for i in range(1, per):
        copies[i - 1].wait()
        out_ref[:, i * cut : (i + 1) * cut] = dot(hg_ref[...], rest_ref[i - 1]).astype(BF)
    for copy in copies[per - 1 :]:
        copy.wait()


def block_kernel(hg_ref, w_ref, after_ref, out_ref):
    out_ref[...] = dot(hg_ref[...], w_ref[...]).astype(BF)


def far_kernel(first_ref, rest_ref, diag_ref, got_ref, out_ref):
    cut = first_ref.shape[1]
    width = 2 * cut
    sum_kernel(first_ref, got_ref.at[:, :cut], out_ref.at[:, :cut])
    sum_kernel(rest_ref, got_ref.at[:, cut:width], out_ref.at[:, cut:width])
    sum_kernel(diag_ref.at[:, width:], got_ref.at[:, width:], out_ref.at[:, width:])


def merge_kernel(a_ref, b_ref, out_ref):
    count = a_ref.shape[0] - EXTRA
    out_ref[:count] = (a_ref[:count].astype(F32) + b_ref[:count].astype(F32)).astype(BF)
    out_ref[count:] = split_terms(join_terms(a_ref[count:]) + join_terms(b_ref[count:]))


def halves(axis, bit, size):
    mine = lax.rem(lax.axis_index(axis) // (1 << bit), 2) * size
    return pl.ds(pl.multiple_of(mine, size), size), pl.ds(pl.multiple_of(size - mine, size), size)


def join(axis, bit, mine_ref, got_ref, out_ref):
    mine, other = halves(axis, bit, mine_ref.shape[0])
    out_ref[mine] = mine_ref[...]
    out_ref[other] = got_ref[...]


def grad_a_kernel(way, x_ref, s_ref, r_ref, after_ref, keep_ref, send_ref):
    low = (s_ref[...].astype(F32) + r_ref[...].astype(F32)).astype(BF)
    mine, other = halves(*way, x_ref.shape[1] // 2)
    send_ref[...] = (SCALE * dot(x_ref[:, other], low, ((0,), (0,)))).astype(BF)
    keep_ref[...] = SCALE * dot(x_ref[:, mine], low, ((0,), (0,)))


def grad_b_kernel(way, v_ref, s_ref, r_ref, after_ref, keep_ref, send_ref):
    low = (s_ref[...].astype(F32) + r_ref[...].astype(F32)).astype(BF)
    mine, other = halves(*way, v_ref.shape[1] // 2)
    sent = (SCALE * dot(low, v_ref[:, other], ((0,), (0,)))).astype(BF)
    kept = SCALE * dot(low, v_ref[:, mine], ((0,), (0,)))
    for b in blocks_of(v_ref.shape[1] // 2):
        send_ref[b] = sent[:, b]
        keep_ref[b] = kept[:, b]


def sum_kernel(keep_ref, got_ref, out_ref):
    out_ref[...] = (keep_ref[...].astype(F32) + got_ref[...].astype(F32)).astype(BF)


def step_kernel(mine_ref, got_ref, *rest):
    sum_kernel(mine_ref, got_ref, rest[len(rest) // 2])


def place_kernel(pos_ref, after_ref, out_ref):
    out_ref[...] = pos_ref[...].astype(F32)


def square_sum(ref):
    x = ref[...].astype(F32)
    return jnp.broadcast_to(jnp.sum(x * x), (8, LANES))


def update_kernel(way, hg_ref, mine_a, got_a, mine_b, after_ref, low_ref, ga_ref, squares_ref):
    join(*way, mine_a, got_a, ga_ref)
    low_ref[...] = dot(hg_ref[...], ga_ref[...]).astype(BF)
    squares_ref[0] = square_sum(mine_a) + square_sum(got_a)
    squares_ref[1] = square_sum(mine_b)


def pack_kernel(way, low_ref, sums_ref, squares_ref, mine_b, got_b, pack_ref, gb_ref):
    count = low_ref.shape[0]
    pack_ref[:count] = low_ref[...]
    row = lax.broadcasted_iota(jnp.int32, (8, LANES), 0)
    squares = squares_ref[0] + (squares_ref[1] + square_sum(got_b))
    pack_ref[count:] = split_terms(jnp.where(row == 7, squares, sums_ref[...]))
    join(*way, mine_b, got_b, gb_ref)


def base_kernel(mine_ref, near_ref, far_ref, far_got, after_ref, base_ref, low_ref):
    width = mine_ref.shape[1]
    low_ref[...] = far_ref[:, width:].astype(F32) + far_got[:, width:].astype(F32)
    for c in blocks_of(width):
        base_ref[:, c] = mine_ref[:, c].astype(F32) + near_ref[:, c].astype(F32) + far_got[:, c].astype(F32)


def final_kernel(
    base_ref, low_ref, s_ref, r_ref, ga_ref, gb_ref, a_ref, b_ref, cos_ref, sin_ref,
    a_hbm, b_hbm, q_hbm, new_a, new_b, half_b, out, sems,
):
    count, width = base_ref.shape
    total = join_terms(s_ref[count:]) + join_terms(r_ref[count:])
    rate = (LEARN * lax.rsqrt(total + NORM_EPS))[7:8]
    scales = lax.rsqrt(total / D + EPS)
    for c in blocks_of(width):
        fresh = b_ref[:, c] - rate * gb_ref[c].astype(F32)
        new_b[:, c] = fresh
        half_b[:, c] = fresh.astype(BF)
    copies = [pltpu.make_async_copy(new_b, b_hbm, sems.at[0])]
    copies[-1].start()
    new_a[...] = a_ref[...] - rate * ga_ref[...].astype(F32)
    copies.append(pltpu.make_async_copy(new_a, a_hbm, sems.at[1]))
    copies[-1].start()
    for i, b in enumerate(blocks_of(count)):
        low = s_ref[b].astype(F32) + r_ref[b].astype(F32)
        scale = jnp.broadcast_to(scales[i : i + 1], (LANES, LANES)).T
        mix = (low_ref[b] - rate * low) * scale * SCALE
        update = dot(mix.astype(BF), half_b[...])
        cos, sin = cos_ref[b], sin_ref[b]
        for c in blocks_of(width):
            query = base_ref[b, c] * scale + update[:, c]
            other = pltpu.roll(query, HEAD // 2, 1)
            out[b, c] = (query * cos + other * sin).astype(BF)
        copies.append(pltpu.make_async_copy(out.at[b], q_hbm.at[b], sems.at[2 + i]))
        copies[-1].start()
    for copy in copies:
        copy.wait()


def keep_hbm(x):
    return pltpu.with_memory_space_constraint(x, pltpu.HBM)


WEIGHTS = {"rank_v": 2.4, "prep": 0.6, "query_diag": 40.0, "query_beside": 2.7, "query_close": 2.7, "grad_b": 40.0, "final": 1.8}
FLOPS_PER_WEIGHT = 1_150_000_000


def call(kernel, outs, in_specs, args, name, scratch=(), out_specs=None, limit=16, aliases=None):
    return pl.pallas_call(
        kernel,
        out_shape=outs,
        in_specs=in_specs,
        out_specs=out_specs if out_specs is not None else jax.tree.map(lambda _: VMEM, outs),
        scratch_shapes=list(scratch),
        compiler_params=pltpu.CompilerParams(vmem_limit_bytes=int(limit * 1024 * 1024)),
        input_output_aliases=aliases or {},
        cost_estimate=pl.CostEstimate(
            flops=int(WEIGHTS.get(name, 0.01) * FLOPS_PER_WEIGHT), bytes_accessed=0, transcendentals=0
        ),
        name=name,
    )(*args)


def turn_tables(places, steps):
    half = HEAD // 2
    freq = 10000.0 ** (-jnp.arange(half, dtype=F32) / half)
    cos, sin = [], []
    for step in range(steps):
        angle = (places + float(step))[:, None] * freq[None, :]
        c, s = jnp.cos(angle), jnp.sin(angle)
        cos.append(jnp.concatenate([c, c], axis=-1))
        sin.append(jnp.concatenate([-s, s], axis=-1))
    return jnp.concatenate(cos), jnp.concatenate(sin)


def bits_of(n):
    return [b for b in range(n.bit_length() - 1)]


def build(n_dp, n_roll, n_tp):
    z_bits = [("roll", b) for b in bits_of(n_roll)]
    x_bits = [("dp", b) for b in bits_of(n_dp)]
    sizes = {"dp": n_dp, "roll": n_roll}

    def cross(x, axis, bit):
        return swap(x, axis, sizes[axis], 1 << bit)

    path_a, path_b = z_bits + x_bits + z_bits[:1], x_bits[:1] + z_bits + x_bits[1:] + x_bits[:1]

    def on_device(
        train_inputs, train_cotangent, factor_a, factor_b, base_weight, incoming, norm_gain, positions
    ):
        steps, rows, width = incoming.shape
        tokens = train_inputs.shape[0]
        rank = factor_a.shape[1]
        count = steps * rows
        dma = lambda n: pltpu.SemaphoreType.DMA((n,))
        vmem = lambda n, dtype=F32: pltpu.VMEM((n, rank), dtype)

        cut = 512
        tall = shape((count, width), BF)
        low_shape = shape((tokens, rank), BF)
        part_v, inputs, cotangent, half_a, hidden, first_columns = call(
            rank_v_kernel,
            [low_shape, shape(train_inputs.shape, BF), shape(train_inputs.shape, BF), shape(factor_a.shape, BF), tall,
             shape((width, cut), BF)],
            [HBM] * 6,
            tuple(
                map(
                    keep_hbm,
                    (train_inputs, train_cotangent, factor_a, factor_b, incoming.reshape(count, width), base_weight),
                )
            ),
            "rank_v",
            [pltpu.VMEM(factor_a.shape, F32), pltpu.VMEM(factor_b.shape, F32), dma(6)],
        )
        got_v = swap(part_v, "tp", n_tp, 1)
        part_u = call(rank_u_kernel, low_shape, [VMEM] * 2, (inputs, half_a), "rank_u")
        got_u = swap(part_u, "tp", n_tp, 1)
        wide = shape((count, width + rank), BF)
        gained, low, sums = call(
            prep_kernel,
            [tall, shape((count, rank), BF), shape((8, LANES), F32)],
            [VMEM] * 3,
            (hidden, norm_gain[None, :], half_a),
            "prep",
        )
        low_v = call(part_kernel, low_shape, [VMEM] * 2 + [ANY], (part_v, got_v, low), "low_v")
        far_v = swap(low_v, "tp", n_tp, 2)
        low_u = call(part_kernel, low_shape, [VMEM] * 2 + [ANY], (part_u, got_u, low_v), "low_u")
        far_u = swap(low_u, "tp", n_tp, 2)

        def query(peers, outs, after, name):
            blocks = len(peers) * width // cut
            return call(
                functools.partial(query_kernel, peers),
                outs,
                [VMEM, HBM, ANY],
                (gained, keep_hbm(base_weight), after),
                "query_" + name,
                [pltpu.VMEM((blocks, width, cut), BF), dma(blocks)],
            )

        per = width // cut
        diag, *columns = call(
            diag_kernel,
            [wide] + [shape((width, cut), BF)] * per,
            [VMEM, VMEM, HBM, VMEM, ANY],
            (gained, first_columns, keep_hbm(base_weight), low, low_u),
            "query_diag",
            [pltpu.VMEM((per - 1, width, cut), BF), dma(2 * per - 1)],
        )
        diag_got = swap(diag, "tp", n_tp, 1)

        block = shape((count, cut), BF)
        distant_first = call(block_kernel, block, [VMEM] * 2 + [ANY], (gained, columns[0], diag), "distant_first")
        half = width // 2
        keep_a, send_a = call(
            functools.partial(grad_a_kernel, path_a[0]),
            [shape((half, rank), F32), shape((half, rank), BF)],
            [VMEM] * 3 + [ANY],
            (inputs, low_v, far_v, distant_first),
            "grad_a",
        )
        keep_b, send_b = call(
            functools.partial(grad_b_kernel, path_b[0]),
            [shape((half, rank), F32), shape((half, rank), BF)],
            [VMEM] * 3 + [ANY],
            (cotangent, low_u, far_u, send_a),
            "grad_b",
        )
        distant_rest = call(block_kernel, block, [VMEM] * 2 + [ANY], (gained, columns[1], send_b), "distant_rest")
        far = call(far_kernel, wide, [VMEM] * 4, (distant_first, distant_rest, diag, diag_got), "far")
        far_got = swap(far, "tp", n_tp, 2)

        def step(mine, send, way, after, passed, name):
            return call(
                step_kernel,
                [shape((half, rank), BF)] + [shape(x.shape, x.dtype) for x in passed],
                [VMEM] * 2 + [ANY] * (1 + len(passed)),
                (mine, cross(send, *way), after, *passed),
                name,
                out_specs=[VMEM] + [ANY] * len(passed),
                aliases={3 + k: 1 + k for k in range(len(passed))},
            )

        mine_a, mine_b, after, passed = keep_a, keep_b, far, []
        order = ["a", "b", "n", "b", "a", "c", "a", "b", "t"] if n_dp * n_roll == 8 else ["a", "b", "n", "b", "a", "c"] + ["a", "b"] * (len(path_a) - 3) + ["t"]
        steps_a, steps_b = iter(path_a[:-1]), iter(path_b[:-1])
        for i, which in enumerate(order):
            if which == "a":
                mine_a, *made = step(mine_a, send_a, next(steps_a), after, passed, f"step_a{i}")
                send_a = after = mine_a
                if made:
                    beside_got, passed = swap(made[0], "tp", n_tp, 1), []
            elif which == "b":
                mine_b = send_b = after = step(mine_b, send_b, next(steps_b), after, [], f"step_b{i}")[0]
            elif which == "t":
                pos = positions.reshape(-1, LANES)
                places = call(place_kernel, shape(pos.shape, F32), [VMEM, ANY], (pos, after), "places")
                cos, sin = turn_tables(places.reshape(rows), steps)
                after = sin
            elif which == "n":
                passed = query((1,), [tall], after, "beside")
            else:
                (close,) = query((0,), [tall], after, "close")
                after = close
        step_low, grad_a, squares = call(
            functools.partial(update_kernel, path_a[-1]),
            [shape((count, rank), BF), shape((width, rank), BF), shape((2, 8, LANES), F32)],
            [VMEM] * 4 + [ANY],
            (gained, mine_a, cross(mine_a, *path_a[-1]), mine_b, after),
            "update",
        )
        step_pack, grad_b = call(
            functools.partial(pack_kernel, path_b[-1]),
            [shape((count + EXTRA, rank), BF), shape((width, rank), BF)],
            [VMEM] * 5,
            (step_low, sums, squares, mine_b, cross(mine_b, *path_b[-1])),
            "pack",
        )
        step_got = swap(step_pack, "tp", n_tp, 1)
        step_sum = call(merge_kernel, shape((count + EXTRA, rank), BF), [VMEM] * 2, (step_pack, step_got), "merge")
        step_far = swap(step_sum, "tp", n_tp, 2)

        base, low_all = call(
            base_kernel,
            [shape((count, width), F32), shape((count, rank), F32)],
            [VMEM] * 4 + [ANY],
            (close, beside_got, far, far_got, step_sum),
            "base",
        )
        new_a, new_b, queries = call(
            final_kernel,
            [shape((width, rank), F32), shape((rank, width), F32), tall],
            [VMEM] * 10,
            (base, low_all, step_sum, step_far, grad_a, grad_b, factor_a, factor_b, cos, sin),
            "final",
            [pltpu.VMEM((width, rank), F32), pltpu.VMEM((rank, width), F32),
             pltpu.VMEM((rank, width), BF), pltpu.VMEM((count, width), BF), dma(2 + count // LANES)],
            [HBM] * 3,
        )
        return new_a, new_b, queries.reshape(steps, rows, width)

    return on_device


def solution(mesh):
    n_dp, n_roll, n_tp = (mesh.shape[a] for a in ("dp", "roll", "tp"))
    return jax.shard_map(
        build(n_dp, n_roll, n_tp),
        mesh=mesh,
        in_specs=(
            P(("dp", "roll"), "tp"),
            P(("dp", "roll"), "tp"),
            P("tp", None),
            P(None, "tp"),
            P("tp", None),
            P(None, ("dp", "roll"), "tp"),
            P("tp"),
            P(("dp", "roll")),
        ),
        out_specs=(P("tp", None), P(None, "tp"), P(None, ("dp", "roll"), "tp")),
        check_vma=False,
    )
```

```python
import functools

import jax
import jax.numpy as jnp
from jax import lax
from jax.experimental import pallas as pl
from jax.experimental.pallas import tpu as pltpu
from jax.sharding import PartitionSpec as P

D = 4096
HEAD = 128
SCALE = 2.0
LEARN = 3.0
EPS = 1e-05
NORM_EPS = 1e-06
LANES = 128
EXTRA = 32

BF = jnp.bfloat16
F32 = jnp.float32
VMEM = pl.BlockSpec(memory_space=pltpu.VMEM)
ANY = pl.BlockSpec(memory_space=pl.ANY)
HBM = pl.BlockSpec(memory_space=pltpu.HBM)


def shape(dims, dtype):
    return jax.ShapeDtypeStruct(dims, dtype)


def dot(a, b, dims=((1,), (0,))):
    return lax.dot_general(a, b, (dims, ((), ())), preferred_element_type=F32)


def swap(x, axis, n, k):
    return lax.ppermute(x, axis, [(i, i ^ k) for i in range(n)])


def split_terms(values):
    high = values.astype(BF)
    rest = values - high.astype(F32)
    middle = rest.astype(BF)
    last = (rest - middle.astype(F32)).astype(BF)
    return jnp.concatenate([high, middle, last, jnp.zeros_like(last)], axis=0)


def join_terms(terms):
    x = terms.astype(F32)
    return (x[0:8] + x[8:16]) + x[16:24]


def fetch(sources, targets, sems):
    copies = [pltpu.make_async_copy(s, t, sems.at[i]) for i, (s, t) in enumerate(zip(sources, targets))]
    for copy in copies:
        copy.start()
    return copies


def blocks_of(count):
    return [slice(i, i + LANES) for i in range(0, count, LANES)]


def rank_v_kernel(
    x_hbm, v_hbm, a_hbm, b_hbm, h_hbm, w_hbm, out_ref, x_ref, v_ref, a16_ref, h_ref, w_ref, a_ref, b_ref, sems
):
    first = weight_blocks((3,), w_hbm, w_ref.shape[1])[0]
    copies = fetch((v_hbm, b_hbm, x_hbm, a_hbm, h_hbm, first), (v_ref, b_ref, x_ref, a_ref, h_ref, w_ref), sems)
    copies[1].wait()
    b16 = b_ref[...].astype(BF)
    copies[0].wait()
    out_ref[...] = dot(v_ref[...], b16, ((1,), (1,))).astype(BF)
    copies[3].wait()
    a16_ref[...] = a_ref[...].astype(BF)
    for i in (2, 4, 5):
        copies[i].wait()


def rank_u_kernel(x_ref, a16_ref, out_ref):
    out_ref[...] = dot(x_ref[...], a16_ref[...]).astype(BF)


def weight_blocks(peers, w_hbm, cut):
    width = w_hbm.shape[0]
    mine = lax.axis_index("tp")
    sources = []
    for peer in peers:
        for i in range(width // cut):
            start = (mine ^ peer) * width + i * cut
            sources.append(w_hbm.at[:, pl.ds(pl.multiple_of(start, cut), cut)])
    return sources


def prep_kernel(h_ref, gain_ref, a16_ref, hg_ref, low_ref, sums_ref):
    count, width = h_ref.shape
    rows = []
    for b in blocks_of(count):
        wide = h_ref[b].astype(F32)
        hg_ref[b] = (wide * gain_ref[...]).astype(BF)
        sums = jnp.sum(wide * wide, axis=-1, keepdims=True)
        rows.append(jnp.broadcast_to(sums, (LANES, LANES)).T[0:1])
    if len(rows) < 8:
        rows.append(jnp.zeros((8 - len(rows), LANES), F32))
    sums_ref[...] = jnp.concatenate(rows, axis=0)
    low_ref[...] = dot(hg_ref[...], a16_ref[...]).astype(BF)


def part_kernel(x_ref, got_ref, after_ref, out_ref):
    sum_kernel(x_ref, got_ref, out_ref)


def query_kernel(peers, hg_ref, w_hbm, after_ref, *rest):
    outs, (w_ref, sems) = rest[:-2], rest[-2:]
    _, width, cut = w_ref.shape
    copies = fetch(weight_blocks(peers, w_hbm, cut), [w_ref.at[i] for i in range(w_ref.shape[0])], sems)
    per = width // cut
    for i, copy in enumerate(copies):
        copy.wait()
        outs[i // per][:, i % per * cut : (i % per + 1) * cut] = dot(hg_ref[...], w_ref[i]).astype(BF)


def diag_kernel(hg_ref, w_ref, w_hbm, low_ref, after_ref, out_ref, next_ref, rest_ref, sems):
    per, width, cut = next_ref.shape
    sources = weight_blocks((3, 2), w_hbm, cut)[1:]
    targets = [rest_ref.at[i] for i in range(per - 1)] + [next_ref.at[i] for i in range(per)]
    copies = fetch(sources, targets, sems)
    out_ref[:, :cut] = dot(hg_ref[...], w_ref[...]).astype(BF)
    out_ref[:, width:] = low_ref[...]
    for i in range(1, per):
        copies[i - 1].wait()
        out_ref[:, i * cut : (i + 1) * cut] = dot(hg_ref[...], rest_ref[i - 1]).astype(BF)
    for copy in copies[per - 1 :]:
        copy.wait()


def distant_kernel(hg_ref, w_ref, after_ref, out_ref):
    per, _, cut = w_ref.shape
    for i in range(per):
        out_ref[:, i * cut : (i + 1) * cut] = dot(hg_ref[...], w_ref[i]).astype(BF)


def far_kernel(mine_ref, diag_ref, got_ref, after_ref, out_ref):
    width = mine_ref.shape[1]
    sum_kernel(mine_ref, got_ref.at[:, :width], out_ref.at[:, :width])
    sum_kernel(diag_ref.at[:, width:], got_ref.at[:, width:], out_ref.at[:, width:])


def merge_kernel(a_ref, b_ref, after_ref, out_ref):
    out_ref[...] = split_terms(join_terms(a_ref[...]) + join_terms(b_ref[...]))


def halves(axis, bit, size):
    mine = lax.rem(lax.axis_index(axis) // (1 << bit), 2) * size
    return pl.ds(pl.multiple_of(mine, size), size), pl.ds(pl.multiple_of(size - mine, size), size)


def join(axis, bit, mine_ref, got_ref, out_ref):
    mine, other = halves(axis, bit, mine_ref.shape[0])
    out_ref[mine] = mine_ref[...]
    out_ref[other] = got_ref[...]


def grad_a_kernel(way, x_ref, s_ref, r_ref, after_ref, keep_ref, send_ref):
    low = (s_ref[...].astype(F32) + r_ref[...].astype(F32)).astype(BF)
    mine, other = halves(*way, x_ref.shape[1] // 2)
    send_ref[...] = (SCALE * dot(x_ref[:, other], low, ((0,), (0,)))).astype(BF)
    keep_ref[...] = SCALE * dot(x_ref[:, mine], low, ((0,), (0,)))


def grad_b_kernel(way, v_ref, s_ref, r_ref, after_ref, keep_ref, send_ref):
    low = (s_ref[...].astype(F32) + r_ref[...].astype(F32)).astype(BF)
    mine, other = halves(*way, v_ref.shape[1] // 2)
    sent = (SCALE * dot(low, v_ref[:, other], ((0,), (0,)))).astype(BF)
    kept = SCALE * dot(low, v_ref[:, mine], ((0,), (0,)))
    for b in blocks_of(v_ref.shape[1] // 2):
        send_ref[b] = sent[:, b]
        keep_ref[b] = kept[:, b]


def sum_kernel(keep_ref, got_ref, out_ref):
    out_ref[...] = (keep_ref[...].astype(F32) + got_ref[...].astype(F32)).astype(BF)


def step_kernel(mine_ref, got_ref, *rest):
    sum_kernel(mine_ref, got_ref, rest[len(rest) // 2])


def place_kernel(pos_ref, after_ref, out_ref):
    out_ref[...] = pos_ref[...].astype(F32)


def square_sum(ref):
    x = ref[...].astype(F32)
    return jnp.broadcast_to(jnp.sum(x * x), (8, LANES))


def update_kernel(way, hg_ref, mine_a, got_a, mine_b, after_ref, low_ref, ga_ref, squares_ref):
    join(*way, mine_a, got_a, ga_ref)
    low_ref[...] = dot(hg_ref[...], ga_ref[...]).astype(BF)
    squares_ref[0] = square_sum(mine_a) + square_sum(got_a)
    squares_ref[1] = square_sum(mine_b)


def norm_kernel(way, sums_ref, squares_ref, mine_b, got_b, after_ref, norm_ref, gb_ref):
    row = lax.broadcasted_iota(jnp.int32, (8, LANES), 0)
    squares = squares_ref[0] + (squares_ref[1] + square_sum(got_b))
    norm_ref[...] = split_terms(jnp.where(row == 7, squares, sums_ref[...]))
    join(*way, mine_b, got_b, gb_ref)


def base_kernel(mine_ref, near_ref, far_ref, far_got, after_ref, base_ref, low_ref):
    width = mine_ref.shape[1]
    low_ref[...] = far_ref[:, width:].astype(F32) + far_got[:, width:].astype(F32)
    for c in blocks_of(width):
        base_ref[:, c] = mine_ref[:, c].astype(F32) + near_ref[:, c].astype(F32) + far_got[:, c].astype(F32)


def final_kernel(
    base_ref, low_ref, s_ref, r_ref, sn_ref, rn_ref, ga_ref, gb_ref, a_ref, b_ref, cos_ref, sin_ref,
    a_hbm, b_hbm, q_hbm, new_a, new_b, half_b, out, sems,
):
    count, width = base_ref.shape
    total = join_terms(sn_ref[...]) + join_terms(rn_ref[...])
    rate = (LEARN * lax.rsqrt(total + NORM_EPS))[7:8]
    scales = lax.rsqrt(total / D + EPS)
    for c in blocks_of(width):
        fresh = b_ref[:, c] - rate * gb_ref[c].astype(F32)
        new_b[:, c] = fresh
        half_b[:, c] = fresh.astype(BF)
    copies = [pltpu.make_async_copy(new_b, b_hbm, sems.at[0])]
    copies[-1].start()
    new_a[...] = a_ref[...] - rate * ga_ref[...].astype(F32)
    copies.append(pltpu.make_async_copy(new_a, a_hbm, sems.at[1]))
    copies[-1].start()
    for i, b in enumerate(blocks_of(count)):
        low = s_ref[b].astype(F32) + r_ref[b].astype(F32)
        scale = jnp.broadcast_to(scales[i : i + 1], (LANES, LANES)).T
        mix = (low_ref[b] - rate * low) * scale * SCALE
        update = dot(mix.astype(BF), half_b[...])
        cos, sin = cos_ref[b], sin_ref[b]
        for c in blocks_of(width):
            query = base_ref[b, c] * scale + update[:, c]
            other = pltpu.roll(query, HEAD // 2, 1)
            out[b, c] = (query * cos + other * sin).astype(BF)
        copies.append(pltpu.make_async_copy(out.at[b], q_hbm.at[b], sems.at[2 + i]))
        copies[-1].start()
    for copy in copies:
        copy.wait()


def keep_hbm(x):
    return pltpu.with_memory_space_constraint(x, pltpu.HBM)


WEIGHTS = {
    "rank_v": 2.4, "prep": 0.6, "query_diag": 40.0, "query_beside": 2.7, "query_close": 2.7, "base": 1.0, "grad_b": 40.0, "final": 1.8,
}
FLOPS_PER_WEIGHT = 1_150_000_000


def call(kernel, outs, in_specs, args, name, scratch=(), out_specs=None, limit=16, aliases=None):
    return pl.pallas_call(
        kernel,
        out_shape=outs,
        in_specs=in_specs,
        out_specs=out_specs if out_specs is not None else jax.tree.map(lambda _: VMEM, outs),
        scratch_shapes=list(scratch),
        compiler_params=pltpu.CompilerParams(vmem_limit_bytes=int(limit * 1024 * 1024)),
        input_output_aliases=aliases or {},
        cost_estimate=pl.CostEstimate(
            flops=int(WEIGHTS.get(name, 0.01) * FLOPS_PER_WEIGHT), bytes_accessed=0, transcendentals=0
        ),
        name=name,
    )(*args)


def turn_tables(places, steps):
    half = HEAD // 2
    freq = 10000.0 ** (-jnp.arange(half, dtype=F32) / half)
    cos, sin = [], []
    for step in range(steps):
        angle = (places + float(step))[:, None] * freq[None, :]
        c, s = jnp.cos(angle), jnp.sin(angle)
        cos.append(jnp.concatenate([c, c], axis=-1))
        sin.append(jnp.concatenate([-s, s], axis=-1))
    return jnp.concatenate(cos), jnp.concatenate(sin)


def bits_of(n):
    return [b for b in range(n.bit_length() - 1)]


def build(n_dp, n_roll, n_tp):
    z_bits = [("roll", b) for b in bits_of(n_roll)]
    x_bits = [("dp", b) for b in bits_of(n_dp)]
    sizes = {"dp": n_dp, "roll": n_roll}

    def cross(x, axis, bit):
        return swap(x, axis, sizes[axis], 1 << bit)

    path_a, path_b = z_bits + x_bits + z_bits[:1], x_bits[:1] + z_bits + x_bits[1:] + x_bits[:1]

    def on_device(
        train_inputs, train_cotangent, factor_a, factor_b, base_weight, incoming, norm_gain, positions
    ):
        steps, rows, width = incoming.shape
        tokens = train_inputs.shape[0]
        rank = factor_a.shape[1]
        count = steps * rows
        dma = lambda n: pltpu.SemaphoreType.DMA((n,))
        vmem = lambda n, dtype=F32: pltpu.VMEM((n, rank), dtype)

        cut = 512
        tall = shape((count, width), BF)
        low_shape = shape((tokens, rank), BF)
        part_v, inputs, cotangent, half_a, hidden, first_columns = call(
            rank_v_kernel,
            [low_shape, shape(train_inputs.shape, BF), shape(train_inputs.shape, BF), shape(factor_a.shape, BF), tall,
             shape((width, cut), BF)],
            [HBM] * 6,
            tuple(
                map(
                    keep_hbm,
                    (train_inputs, train_cotangent, factor_a, factor_b, incoming.reshape(count, width), base_weight),
                )
            ),
            "rank_v",
            [pltpu.VMEM(factor_a.shape, F32), pltpu.VMEM(factor_b.shape, F32), dma(6)],
        )
        got_v = swap(part_v, "tp", n_tp, 1)
        part_u = call(rank_u_kernel, low_shape, [VMEM] * 2, (inputs, half_a), "rank_u")
        got_u = swap(part_u, "tp", n_tp, 1)
        wide = shape((count, width + rank), BF)
        gained, low, sums = call(
            prep_kernel,
            [tall, shape((count, rank), BF), shape((8, LANES), F32)],
            [VMEM] * 3,
            (hidden, norm_gain[None, :], half_a),
            "prep",
        )
        low_v = call(part_kernel, low_shape, [VMEM] * 2 + [ANY], (part_v, got_v, low), "low_v")
        far_v = swap(low_v, "tp", n_tp, 2)
        low_u = call(part_kernel, low_shape, [VMEM] * 2 + [ANY], (part_u, got_u, low_v), "low_u")
        far_u = swap(low_u, "tp", n_tp, 2)

        def query(peers, outs, after, name):
            blocks = len(peers) * width // cut
            return call(
                functools.partial(query_kernel, peers),
                outs,
                [VMEM, HBM, ANY],
                (gained, keep_hbm(base_weight), after),
                "query_" + name,
                [pltpu.VMEM((blocks, width, cut), BF), dma(blocks)],
            )

        per = width // cut
        diag, columns = call(
            diag_kernel,
            [wide, shape((per, width, cut), BF)],
            [VMEM, VMEM, HBM, VMEM, ANY],
            (gained, first_columns, keep_hbm(base_weight), low, low_u),
            "query_diag",
            [pltpu.VMEM((per - 1, width, cut), BF), dma(2 * per - 1)],
        )
        diag_got = swap(diag, "tp", n_tp, 1)

        half = width // 2
        keep_a, send_a = call(
            functools.partial(grad_a_kernel, path_a[0]),
            [shape((half, rank), F32), shape((half, rank), BF)],
            [VMEM] * 3 + [ANY],
            (inputs, low_v, far_v, diag),
            "grad_a",
        )
        keep_b, send_b = call(
            functools.partial(grad_b_kernel, path_b[0]),
            [shape((half, rank), F32), shape((half, rank), BF)],
            [VMEM] * 3 + [ANY],
            (cotangent, low_u, far_u, send_a),
            "grad_b",
        )
        distant = call(distant_kernel, tall, [VMEM, VMEM, ANY], (gained, columns, send_b), "query_distant")
        far = call(far_kernel, wide, [VMEM] * 3 + [ANY], (distant, diag, diag_got, send_b), "far")
        far_got = swap(far, "tp", n_tp, 2)

        def step(mine, send, way, after, passed, name):
            return call(
                step_kernel,
                [shape((half, rank), BF)] + [shape(x.shape, x.dtype) for x in passed],
                [VMEM] * 2 + [ANY] * (1 + len(passed)),
                (mine, cross(send, *way), after, *passed),
                name,
                out_specs=[VMEM] + [ANY] * len(passed),
                aliases={3 + k: 1 + k for k in range(len(passed))},
            )

        mine_a, mine_b, after, passed = keep_a, keep_b, far, []
        order = ["a", "b", "n", "b", "a", "c", "a", "b", "t"] if n_dp * n_roll == 8 else ["a", "b", "n", "b", "a", "c"] + ["a", "b"] * (len(path_a) - 3) + ["t"]
        steps_a, steps_b = iter(path_a[:-1]), iter(path_b[:-1])
        for i, which in enumerate(order):
            if which == "a":
                mine_a, *made = step(mine_a, send_a, next(steps_a), after, passed, f"step_a{i}")
                send_a = after = mine_a
                if made:
                    beside_got, passed = swap(made[0], "tp", n_tp, 1), []
            elif which == "b":
                mine_b = send_b = after = step(mine_b, send_b, next(steps_b), after, [], f"step_b{i}")[0]
            elif which == "t":
                pos = positions.reshape(-1, LANES)
                places = call(place_kernel, shape(pos.shape, F32), [VMEM, ANY], (pos, after), "places")
                cos, sin = turn_tables(places.reshape(rows), steps)
                after = sin
            elif which == "n":
                passed = query((1,), [tall], after, "beside")
            else:
                (close,) = query((0,), [tall], after, "close")
                after = close
        step_low, grad_a, squares = call(
            functools.partial(update_kernel, path_a[-1]),
            [shape((count, rank), BF), shape((width, rank), BF), shape((2, 8, LANES), F32)],
            [VMEM] * 4 + [ANY],
            (gained, mine_a, cross(mine_a, *path_a[-1]), mine_b, after),
            "update",
        )
        step_got = swap(step_low, "tp", n_tp, 1)
        norm, grad_b = call(
            functools.partial(norm_kernel, path_b[-1]),
            [shape((EXTRA, LANES), BF), shape((width, rank), BF)],
            [VMEM] * 4 + [ANY],
            (sums, squares, mine_b, cross(mine_b, *path_b[-1]), step_low),
            "norm",
        )
        norm_got = swap(norm, "tp", n_tp, 1)
        step_sum = call(
            part_kernel, shape((count, rank), BF), [VMEM] * 2 + [ANY], (step_low, step_got, norm), "merge"
        )
        step_far = swap(step_sum, "tp", n_tp, 2)
        norm_sum = call(
            merge_kernel, shape((EXTRA, LANES), BF), [VMEM] * 2 + [ANY], (norm, norm_got, step_sum), "norm_merge"
        )
        norm_far = swap(norm_sum, "tp", n_tp, 2)
        base, low_all = call(
            base_kernel,
            [shape((count, width), F32), shape((count, rank), F32)],
            [VMEM] * 4 + [ANY],
            (close, beside_got, far, far_got, step_sum),
            "base",
        )
        new_a, new_b, queries = call(
            final_kernel,
            [shape((width, rank), F32), shape((rank, width), F32), tall],
            [VMEM] * 12,
            (base, low_all, step_sum, step_far, norm_sum, norm_far, grad_a, grad_b, factor_a, factor_b, cos, sin),
            "final",
            [pltpu.VMEM((width, rank), F32), pltpu.VMEM((rank, width), F32),
             pltpu.VMEM((rank, width), BF), pltpu.VMEM((count, width), BF), dma(2 + count // LANES)],
            [HBM] * 3,
        )
        return new_a, new_b, queries.reshape(steps, rows, width)

    return on_device


def solution(mesh):
    n_dp, n_roll, n_tp = (mesh.shape[a] for a in ("dp", "roll", "tp"))
    return jax.shard_map(
        build(n_dp, n_roll, n_tp),
        mesh=mesh,
        in_specs=(
            P(("dp", "roll"), "tp"),
            P(("dp", "roll"), "tp"),
            P("tp", None),
            P(None, "tp"),
            P("tp", None),
            P(None, ("dp", "roll"), "tp"),
            P("tp"),
            P(("dp", "roll")),
        ),
        out_specs=(P("tp", None), P(None, "tp"), P(None, ("dp", "roll"), "tp")),
        check_vma=False,
    )
```

```python
import functools

import jax
import jax.numpy as jnp
from jax import lax
from jax.experimental import pallas as pl
from jax.experimental.pallas import tpu as pltpu
from jax.sharding import PartitionSpec as P

D = 4096
HEAD = 128
SCALE = 2.0
LEARN = 3.0
EPS = 1e-05
NORM_EPS = 1e-06
LANES = 128
EXTRA = 32

BF = jnp.bfloat16
F32 = jnp.float32
VMEM = pl.BlockSpec(memory_space=pltpu.VMEM)
ANY = pl.BlockSpec(memory_space=pl.ANY)
HBM = pl.BlockSpec(memory_space=pltpu.HBM)


def shape(dims, dtype):
    return jax.ShapeDtypeStruct(dims, dtype)


def dot(a, b, dims=((1,), (0,))):
    return lax.dot_general(a, b, (dims, ((), ())), preferred_element_type=F32)


def swap(x, axis, n, k):
    return lax.ppermute(x, axis, [(i, i ^ k) for i in range(n)])


def split_terms(values):
    high = values.astype(BF)
    rest = values - high.astype(F32)
    middle = rest.astype(BF)
    last = (rest - middle.astype(F32)).astype(BF)
    return jnp.concatenate([high, middle, last, jnp.zeros_like(last)], axis=0)


def join_terms(terms):
    x = terms.astype(F32)
    return (x[0:8] + x[8:16]) + x[16:24]


def fetch(sources, targets, sems):
    copies = [pltpu.make_async_copy(s, t, sems.at[i]) for i, (s, t) in enumerate(zip(sources, targets))]
    for copy in copies:
        copy.start()
    return copies


def blocks_of(count):
    return [slice(i, i + LANES) for i in range(0, count, LANES)]


def rank_v_kernel(
    x_hbm, v_hbm, a_hbm, b_hbm, h_hbm, w_hbm, out_ref, x_ref, v_ref, a16_ref, h_ref, w_ref, a_ref, b_ref, sems
):
    first = weight_blocks((3,), w_hbm, w_ref.shape[1])[0]
    copies = fetch((v_hbm, b_hbm, x_hbm, a_hbm, h_hbm, first), (v_ref, b_ref, x_ref, a_ref, h_ref, w_ref), sems)
    copies[1].wait()
    b16 = b_ref[...].astype(BF)
    copies[0].wait()
    out_ref[...] = dot(v_ref[...], b16, ((1,), (1,))).astype(BF)
    copies[3].wait()
    a16_ref[...] = a_ref[...].astype(BF)
    for i in (2, 4, 5):
        copies[i].wait()


def rank_u_kernel(x_ref, a16_ref, out_ref):
    out_ref[...] = dot(x_ref[...], a16_ref[...]).astype(BF)


def weight_blocks(peers, w_hbm, cut):
    width = w_hbm.shape[0]
    mine = lax.axis_index("tp")
    sources = []
    for peer in peers:
        for i in range(width // cut):
            start = (mine ^ peer) * width + i * cut
            sources.append(w_hbm.at[:, pl.ds(pl.multiple_of(start, cut), cut)])
    return sources


def prep_kernel(h_ref, gain_ref, a16_ref, hg_ref, low_ref, sums_ref):
    count, width = h_ref.shape
    rows = []
    for b in blocks_of(count):
        wide = h_ref[b].astype(F32)
        hg_ref[b] = (wide * gain_ref[...]).astype(BF)
        sums = jnp.sum(wide * wide, axis=-1, keepdims=True)
        rows.append(jnp.broadcast_to(sums, (LANES, LANES)).T[0:1])
    if len(rows) < 8:
        rows.append(jnp.zeros((8 - len(rows), LANES), F32))
    sums_ref[...] = jnp.concatenate(rows, axis=0)
    low_ref[...] = dot(hg_ref[...], a16_ref[...]).astype(BF)


def part_kernel(x_ref, got_ref, after_ref, out_ref):
    sum_kernel(x_ref, got_ref, out_ref)


def query_kernel(peers, hg_ref, w_hbm, after_ref, *rest):
    outs, (w_ref, sems) = rest[:-2], rest[-2:]
    _, width, cut = w_ref.shape
    copies = fetch(weight_blocks(peers, w_hbm, cut), [w_ref.at[i] for i in range(w_ref.shape[0])], sems)
    per = width // cut
    for i, copy in enumerate(copies):
        copy.wait()
        outs[i // per][:, i % per * cut : (i % per + 1) * cut] = dot(hg_ref[...], w_ref[i]).astype(BF)


def diag_kernel(hg_ref, w_ref, w_hbm, low_ref, after_ref, out_ref, next_ref, rest_ref, sems):
    per, width, cut = next_ref.shape
    sources = weight_blocks((3, 2), w_hbm, cut)[1:]
    targets = [rest_ref.at[i] for i in range(per - 1)] + [next_ref.at[i] for i in range(per)]
    copies = fetch(sources, targets, sems)
    out_ref[:, :cut] = dot(hg_ref[...], w_ref[...]).astype(BF)
    out_ref[:, width:] = low_ref[...]
    for i in range(1, per):
        copies[i - 1].wait()
        out_ref[:, i * cut : (i + 1) * cut] = dot(hg_ref[...], rest_ref[i - 1]).astype(BF)
    for copy in copies[per - 1 :]:
        copy.wait()


def distant_kernel(hg_ref, w_ref, after_ref, out_ref):
    per, _, cut = w_ref.shape
    for i in range(per):
        out_ref[:, i * cut : (i + 1) * cut] = dot(hg_ref[...], w_ref[i]).astype(BF)


def far_kernel(mine_ref, diag_ref, got_ref, after_ref, out_ref):
    width = mine_ref.shape[1]
    sum_kernel(mine_ref, got_ref.at[:, :width], out_ref.at[:, :width])
    sum_kernel(diag_ref.at[:, width:], got_ref.at[:, width:], out_ref.at[:, width:])


def merge_kernel(a_ref, b_ref, after_ref, out_ref):
    out_ref[...] = split_terms(join_terms(a_ref[...]) + join_terms(b_ref[...]))


def halves(axis, bit, size):
    mine = lax.rem(lax.axis_index(axis) // (1 << bit), 2) * size
    return pl.ds(pl.multiple_of(mine, size), size), pl.ds(pl.multiple_of(size - mine, size), size)


def join(axis, bit, mine_ref, got_ref, out_ref):
    mine, other = halves(axis, bit, mine_ref.shape[0])
    out_ref[mine] = mine_ref[...]
    out_ref[other] = got_ref[...]


def grad_a_kernel(way, x_ref, s_ref, r_ref, after_ref, keep_ref, send_ref):
    low = (s_ref[...].astype(F32) + r_ref[...].astype(F32)).astype(BF)
    mine, other = halves(*way, x_ref.shape[1] // 2)
    send_ref[...] = (SCALE * dot(x_ref[:, other], low, ((0,), (0,)))).astype(BF)
    keep_ref[...] = SCALE * dot(x_ref[:, mine], low, ((0,), (0,)))


def grad_b_kernel(way, v_ref, s_ref, r_ref, after_ref, keep_ref, send_ref):
    low = (s_ref[...].astype(F32) + r_ref[...].astype(F32)).astype(BF)
    mine, other = halves(*way, v_ref.shape[1] // 2)
    sent = (SCALE * dot(low, v_ref[:, other], ((0,), (0,)))).astype(BF)
    kept = SCALE * dot(low, v_ref[:, mine], ((0,), (0,)))
    for b in blocks_of(v_ref.shape[1] // 2):
        send_ref[b] = sent[:, b]
        keep_ref[b] = kept[:, b]


def sum_kernel(keep_ref, got_ref, out_ref):
    out_ref[...] = (keep_ref[...].astype(F32) + got_ref[...].astype(F32)).astype(BF)


def step_kernel(mine_ref, got_ref, *rest):
    sum_kernel(mine_ref, got_ref, rest[len(rest) // 2])


def place_kernel(pos_ref, after_ref, out_ref):
    out_ref[...] = pos_ref[...].astype(F32)


def square_sum(ref):
    x = ref[...].astype(F32)
    return jnp.broadcast_to(jnp.sum(x * x), (8, LANES))


def update_kernel(way, hg_ref, mine_a, got_a, mine_b, after_ref, low_ref, ga_ref, squares_ref):
    join(*way, mine_a, got_a, ga_ref)
    low_ref[...] = dot(hg_ref[...], ga_ref[...]).astype(BF)
    squares_ref[0] = square_sum(mine_a) + square_sum(got_a)
    squares_ref[1] = square_sum(mine_b)


def norm_kernel(way, sums_ref, squares_ref, mine_b, got_b, after_ref, norm_ref, gb_ref):
    row = lax.broadcasted_iota(jnp.int32, (8, LANES), 0)
    squares = squares_ref[0] + (squares_ref[1] + square_sum(got_b))
    norm_ref[...] = split_terms(jnp.where(row == 7, squares, sums_ref[...]))
    join(*way, mine_b, got_b, gb_ref)


def base_kernel(mine_ref, near_ref, far_ref, far_got, after_ref, base_ref, low_ref):
    width = mine_ref.shape[1]
    low_ref[...] = far_ref[:, width:].astype(F32) + far_got[:, width:].astype(F32)
    for c in blocks_of(width):
        base_ref[:, c] = mine_ref[:, c].astype(F32) + near_ref[:, c].astype(F32) + far_got[:, c].astype(F32)


def final_kernel(
    base_ref, low_ref, s_ref, r_ref, sn_ref, rn_ref, ga_ref, gb_ref, a_ref, b_ref, cos_ref, sin_ref,
    a_hbm, b_hbm, q_hbm, new_a, new_b, half_b, out, sems,
):
    count, width = base_ref.shape
    total = join_terms(sn_ref[...]) + join_terms(rn_ref[...])
    rate = (LEARN * lax.rsqrt(total + NORM_EPS))[7:8]
    scales = lax.rsqrt(total / D + EPS)
    for c in blocks_of(width):
        fresh = b_ref[:, c] - rate * gb_ref[c].astype(F32)
        new_b[:, c] = fresh
        half_b[:, c] = fresh.astype(BF)
    copies = [pltpu.make_async_copy(new_b, b_hbm, sems.at[0])]
    copies[-1].start()
    new_a[...] = a_ref[...] - rate * ga_ref[...].astype(F32)
    copies.append(pltpu.make_async_copy(new_a, a_hbm, sems.at[1]))
    copies[-1].start()
    for i, b in enumerate(blocks_of(count)):
        low = s_ref[b].astype(F32) + r_ref[b].astype(F32)
        scale = jnp.broadcast_to(scales[i : i + 1], (LANES, LANES)).T
        mix = (low_ref[b] - rate * low) * scale * SCALE
        update = dot(mix.astype(BF), half_b[...])
        cos, sin = cos_ref[b], sin_ref[b]
        for c in blocks_of(width):
            query = base_ref[b, c] * scale + update[:, c]
            other = pltpu.roll(query, HEAD // 2, 1)
            out[b, c] = (query * cos + other * sin).astype(BF)
        copies.append(pltpu.make_async_copy(out.at[b], q_hbm.at[b], sems.at[2 + i]))
        copies[-1].start()
    for copy in copies:
        copy.wait()


def keep_hbm(x):
    return pltpu.with_memory_space_constraint(x, pltpu.HBM)


WEIGHTS = {"rank_v": 2.4, "prep": 0.6, "query_diag": 40.0, "query_beside": 1.8, "query_close": 2.7, "base": 1.0, "grad_b": 40.0, "final": 1.8, "update": 3.0}
FLOPS_PER_WEIGHT = 1_150_000_000


def call(kernel, outs, in_specs, args, name, scratch=(), out_specs=None, limit=16, aliases=None):
    return pl.pallas_call(
        kernel,
        out_shape=outs,
        in_specs=in_specs,
        out_specs=out_specs if out_specs is not None else jax.tree.map(lambda _: VMEM, outs),
        scratch_shapes=list(scratch),
        compiler_params=pltpu.CompilerParams(vmem_limit_bytes=int(limit * 1024 * 1024)),
        input_output_aliases=aliases or {},
        cost_estimate=pl.CostEstimate(
            flops=int(WEIGHTS.get(name, 0.01) * FLOPS_PER_WEIGHT), bytes_accessed=0, transcendentals=0
        ),
        name=name,
    )(*args)


def turn_tables(places, steps):
    half = HEAD // 2
    freq = 10000.0 ** (-jnp.arange(half, dtype=F32) / half)
    cos, sin = [], []
    for step in range(steps):
        angle = (places + float(step))[:, None] * freq[None, :]
        c, s = jnp.cos(angle), jnp.sin(angle)
        cos.append(jnp.concatenate([c, c], axis=-1))
        sin.append(jnp.concatenate([-s, s], axis=-1))
    return jnp.concatenate(cos), jnp.concatenate(sin)


def bits_of(n):
    return [b for b in range(n.bit_length() - 1)]


def build(n_dp, n_roll, n_tp):
    z_bits = [("roll", b) for b in bits_of(n_roll)]
    x_bits = [("dp", b) for b in bits_of(n_dp)]
    sizes = {"dp": n_dp, "roll": n_roll}

    def cross(x, axis, bit):
        return swap(x, axis, sizes[axis], 1 << bit)

    path_a, path_b = z_bits + x_bits + z_bits[:1], x_bits[:1] + z_bits + x_bits[1:] + x_bits[:1]

    def on_device(
        train_inputs, train_cotangent, factor_a, factor_b, base_weight, incoming, norm_gain, positions
    ):
        steps, rows, width = incoming.shape
        tokens = train_inputs.shape[0]
        rank = factor_a.shape[1]
        count = steps * rows
        dma = lambda n: pltpu.SemaphoreType.DMA((n,))
        vmem = lambda n, dtype=F32: pltpu.VMEM((n, rank), dtype)

        cut = 512
        tall = shape((count, width), BF)
        low_shape = shape((tokens, rank), BF)
        part_v, inputs, cotangent, half_a, hidden, first_columns = call(
            rank_v_kernel,
            [low_shape, shape(train_inputs.shape, BF), shape(train_inputs.shape, BF), shape(factor_a.shape, BF), tall,
             shape((width, cut), BF)],
            [HBM] * 6,
            tuple(
                map(
                    keep_hbm,
                    (train_inputs, train_cotangent, factor_a, factor_b, incoming.reshape(count, width), base_weight),
                )
            ),
            "rank_v",
            [pltpu.VMEM(factor_a.shape, F32), pltpu.VMEM(factor_b.shape, F32), dma(6)],
        )
        got_v = swap(part_v, "tp", n_tp, 1)
        part_u = call(rank_u_kernel, low_shape, [VMEM] * 2, (inputs, half_a), "rank_u")
        got_u = swap(part_u, "tp", n_tp, 1)
        wide = shape((count, width + rank), BF)
        gained, low, sums = call(
            prep_kernel,
            [tall, shape((count, rank), BF), shape((8, LANES), F32)],
            [VMEM] * 3,
            (hidden, norm_gain[None, :], half_a),
            "prep",
        )
        low_v = call(part_kernel, low_shape, [VMEM] * 2 + [ANY], (part_v, got_v, low), "low_v")
        far_v = swap(low_v, "tp", n_tp, 2)
        low_u = call(part_kernel, low_shape, [VMEM] * 2 + [ANY], (part_u, got_u, low_v), "low_u")
        far_u = swap(low_u, "tp", n_tp, 2)

        def query(peers, outs, after, name):
            blocks = len(peers) * width // cut
            return call(
                functools.partial(query_kernel, peers),
                outs,
                [VMEM, HBM, ANY],
                (gained, keep_hbm(base_weight), after),
                "query_" + name,
                [pltpu.VMEM((blocks, width, cut), BF), dma(blocks)],
            )

        per = width // cut
        diag, columns = call(
            diag_kernel,
            [wide, shape((per, width, cut), BF)],
            [VMEM, VMEM, HBM, VMEM, ANY],
            (gained, first_columns, keep_hbm(base_weight), low, low_u),
            "query_diag",
            [pltpu.VMEM((per - 1, width, cut), BF), dma(2 * per - 1)],
        )
        diag_got = swap(diag, "tp", n_tp, 1)

        half = width // 2
        keep_a, send_a = call(
            functools.partial(grad_a_kernel, path_a[0]),
            [shape((half, rank), F32), shape((half, rank), BF)],
            [VMEM] * 3 + [ANY],
            (inputs, low_v, far_v, diag),
            "grad_a",
        )
        keep_b, send_b = call(
            functools.partial(grad_b_kernel, path_b[0]),
            [shape((half, rank), F32), shape((half, rank), BF)],
            [VMEM] * 3 + [ANY],
            (cotangent, low_u, far_u, send_a),
            "grad_b",
        )
        distant = call(distant_kernel, tall, [VMEM, VMEM, ANY], (gained, columns, send_b), "query_distant")
        far = call(far_kernel, wide, [VMEM] * 3 + [ANY], (distant, diag, diag_got, send_b), "far")
        far_got = swap(far, "tp", n_tp, 2)

        def step(mine, send, way, after, passed, name):
            return call(
                step_kernel,
                [shape((half, rank), BF)] + [shape(x.shape, x.dtype) for x in passed],
                [VMEM] * 2 + [ANY] * (1 + len(passed)),
                (mine, cross(send, *way), after, *passed),
                name,
                out_specs=[VMEM] + [ANY] * len(passed),
                aliases={3 + k: 1 + k for k in range(len(passed))},
            )

        mine_a, mine_b, after, passed = keep_a, keep_b, far, []
        order = ["a", "b", "n", "b", "a", "c", "a", "b", "t"] if n_dp * n_roll == 8 else ["a", "b", "n", "b", "a", "c"] + ["a", "b"] * (len(path_a) - 3) + ["t"]
        steps_a, steps_b = iter(path_a[:-1]), iter(path_b[:-1])
        for i, which in enumerate(order):
            if which == "a":
                mine_a, *made = step(mine_a, send_a, next(steps_a), after, passed, f"step_a{i}")
                send_a = after = mine_a
                if made:
                    beside_got, passed = swap(made[0], "tp", n_tp, 1), []
            elif which == "b":
                mine_b = send_b = after = step(mine_b, send_b, next(steps_b), after, [], f"step_b{i}")[0]
            elif which == "t":
                pos = positions.reshape(-1, LANES)
                places = call(place_kernel, shape(pos.shape, F32), [VMEM, ANY], (pos, after), "places")
                cos, sin = turn_tables(places.reshape(rows), steps)
                after = sin
            elif which == "n":
                passed = query((1,), [tall], after, "beside")
            else:
                (close,) = query((0,), [tall], after, "close")
                after = close
        step_low, grad_a, squares = call(
            functools.partial(update_kernel, path_a[-1]),
            [shape((count, rank), BF), shape((width, rank), BF), shape((2, 8, LANES), F32)],
            [VMEM] * 4 + [ANY],
            (gained, mine_a, cross(mine_a, *path_a[-1]), mine_b, after),
            "update",
        )
        step_got = swap(step_low, "tp", n_tp, 1)
        norm, grad_b = call(
            functools.partial(norm_kernel, path_b[-1]),
            [shape((EXTRA, LANES), BF), shape((width, rank), BF)],
            [VMEM] * 4 + [ANY],
            (sums, squares, mine_b, cross(mine_b, *path_b[-1]), step_low),
            "norm",
        )
        norm_got = swap(norm, "tp", n_tp, 1)
        step_sum = call(
            part_kernel, shape((count, rank), BF), [VMEM] * 2 + [ANY], (step_low, step_got, norm), "merge"
        )
        step_far = swap(step_sum, "tp", n_tp, 2)
        norm_sum = call(
            merge_kernel, shape((EXTRA, LANES), BF), [VMEM] * 2 + [ANY], (norm, norm_got, step_sum), "norm_merge"
        )
        norm_far = swap(norm_sum, "tp", n_tp, 2)
        base, low_all = call(
            base_kernel,
            [shape((count, width), F32), shape((count, rank), F32)],
            [VMEM] * 4 + [ANY],
            (close, beside_got, far, far_got, step_sum),
            "base",
        )
        new_a, new_b, queries = call(
            final_kernel,
            [shape((width, rank), F32), shape((rank, width), F32), tall],
            [VMEM] * 12,
            (base, low_all, step_sum, step_far, norm_sum, norm_far, grad_a, grad_b, factor_a, factor_b, cos, sin),
            "final",
            [pltpu.VMEM((width, rank), F32), pltpu.VMEM((rank, width), F32),
             pltpu.VMEM((rank, width), BF), pltpu.VMEM((count, width), BF), dma(2 + count // LANES)],
            [HBM] * 3,
        )
        return new_a, new_b, queries.reshape(steps, rows, width)

    return on_device


def solution(mesh):
    n_dp, n_roll, n_tp = (mesh.shape[a] for a in ("dp", "roll", "tp"))
    return jax.shard_map(
        build(n_dp, n_roll, n_tp),
        mesh=mesh,
        in_specs=(
            P(("dp", "roll"), "tp"),
            P(("dp", "roll"), "tp"),
            P("tp", None),
            P(None, "tp"),
            P("tp", None),
            P(None, ("dp", "roll"), "tp"),
            P("tp"),
            P(("dp", "roll")),
        ),
        out_specs=(P("tp", None), P(None, "tp"), P(None, ("dp", "roll"), "tp")),
        check_vma=False,
    )
```

```python
import functools

import jax
import jax.numpy as jnp
from jax import lax
from jax.experimental import pallas as pl
from jax.experimental.pallas import tpu as pltpu
from jax.sharding import PartitionSpec as P

D = 4096
HEAD = 128
SCALE = 2.0
LEARN = 3.0
EPS = 1e-05
NORM_EPS = 1e-06
LANES = 128
EXTRA = 32

BF = jnp.bfloat16
F32 = jnp.float32
VMEM = pl.BlockSpec(memory_space=pltpu.VMEM)
ANY = pl.BlockSpec(memory_space=pl.ANY)
HBM = pl.BlockSpec(memory_space=pltpu.HBM)


def shape(dims, dtype):
    return jax.ShapeDtypeStruct(dims, dtype)


def dot(a, b, dims=((1,), (0,))):
    return lax.dot_general(a, b, (dims, ((), ())), preferred_element_type=F32)


def swap(x, axis, n, k):
    return lax.ppermute(x, axis, [(i, i ^ k) for i in range(n)])


def split_terms(values):
    high = values.astype(BF)
    rest = values - high.astype(F32)
    middle = rest.astype(BF)
    last = (rest - middle.astype(F32)).astype(BF)
    return jnp.concatenate([high, middle, last, jnp.zeros_like(last)], axis=0)


def join_terms(terms):
    x = terms.astype(F32)
    return (x[0:8] + x[8:16]) + x[16:24]


def fetch(sources, targets, sems):
    copies = [pltpu.make_async_copy(s, t, sems.at[i]) for i, (s, t) in enumerate(zip(sources, targets))]
    for copy in copies:
        copy.start()
    return copies


def blocks_of(count):
    return [slice(i, i + LANES) for i in range(0, count, LANES)]


def rank_v_kernel(
    x_hbm, v_hbm, a_hbm, b_hbm, h_hbm, w_hbm, out_ref, x_ref, v_ref, a16_ref, h_ref, w_ref, a_ref, b_ref, sems
):
    first = weight_blocks((3,), w_hbm, w_ref.shape[1])[0]
    copies = fetch((v_hbm, b_hbm, x_hbm, a_hbm, h_hbm, first), (v_ref, b_ref, x_ref, a_ref, h_ref, w_ref), sems)
    copies[1].wait()
    b16 = b_ref[...].astype(BF)
    copies[0].wait()
    out_ref[...] = dot(v_ref[...], b16, ((1,), (1,))).astype(BF)
    copies[3].wait()
    a16_ref[...] = a_ref[...].astype(BF)
    for i in (2, 4, 5):
        copies[i].wait()


def rank_u_kernel(x_ref, a16_ref, out_ref):
    out_ref[...] = dot(x_ref[...], a16_ref[...]).astype(BF)


def weight_blocks(peers, w_hbm, cut):
    width = w_hbm.shape[0]
    mine = lax.axis_index("tp")
    sources = []
    for peer in peers:
        for i in range(width // cut):
            start = (mine ^ peer) * width + i * cut
            sources.append(w_hbm.at[:, pl.ds(pl.multiple_of(start, cut), cut)])
    return sources


def prep_kernel(h_ref, gain_ref, a16_ref, hg_ref, low_ref, sums_ref):
    count, width = h_ref.shape
    rows = []
    for b in blocks_of(count):
        wide = h_ref[b].astype(F32)
        hg_ref[b] = (wide * gain_ref[...]).astype(BF)
        sums = jnp.sum(wide * wide, axis=-1, keepdims=True)
        rows.append(jnp.broadcast_to(sums, (LANES, LANES)).T[0:1])
    if len(rows) < 8:
        rows.append(jnp.zeros((8 - len(rows), LANES), F32))
    sums_ref[...] = jnp.concatenate(rows, axis=0)
    low_ref[...] = dot(hg_ref[...], a16_ref[...]).astype(BF)


def part_kernel(x_ref, got_ref, after_ref, out_ref):
    sum_kernel(x_ref, got_ref, out_ref)


def query_kernel(peers, hg_ref, w_hbm, after_ref, *rest):
    outs, (w_ref, sems) = rest[:-2], rest[-2:]
    _, width, cut = w_ref.shape
    copies = fetch(weight_blocks(peers, w_hbm, cut), [w_ref.at[i] for i in range(w_ref.shape[0])], sems)
    per = width // cut
    for i, copy in enumerate(copies):
        copy.wait()
        outs[i // per][:, i % per * cut : (i % per + 1) * cut] = dot(hg_ref[...], w_ref[i]).astype(BF)


def diag_kernel(hg_ref, w_ref, w_hbm, low_ref, after_ref, out_ref, *refs):
    *next_refs, rest_ref, sems = refs
    width, cut = w_ref.shape
    per = width // cut
    sources = weight_blocks((3, 2), w_hbm, cut)[1:]
    targets = [rest_ref.at[i] for i in range(per - 1)] + next_refs
    copies = fetch(sources, targets, sems)
    out_ref[:, :cut] = dot(hg_ref[...], w_ref[...]).astype(BF)
    out_ref[:, width:] = low_ref[...]
    for i in range(1, per):
        copies[i - 1].wait()
        out_ref[:, i * cut : (i + 1) * cut] = dot(hg_ref[...], rest_ref[i - 1]).astype(BF)
    for copy in copies[per - 1 :]:
        copy.wait()


def block_kernel(hg_ref, w_ref, after_ref, out_ref):
    out_ref[...] = dot(hg_ref[...], w_ref[...]).astype(BF)


def far_kernel(first_ref, rest_ref, diag_ref, got_ref, out_ref):
    cut = first_ref.shape[1]
    width = 2 * cut
    sum_kernel(first_ref, got_ref.at[:, :cut], out_ref.at[:, :cut])
    sum_kernel(rest_ref, got_ref.at[:, cut:width], out_ref.at[:, cut:width])
    sum_kernel(diag_ref.at[:, width:], got_ref.at[:, width:], out_ref.at[:, width:])


def merge_kernel(a_ref, b_ref, after_ref, out_ref):
    out_ref[...] = split_terms(join_terms(a_ref[...]) + join_terms(b_ref[...]))


def halves(axis, bit, size):
    mine = lax.rem(lax.axis_index(axis) // (1 << bit), 2) * size
    return pl.ds(pl.multiple_of(mine, size), size), pl.ds(pl.multiple_of(size - mine, size), size)


def join(axis, bit, mine_ref, got_ref, out_ref):
    mine, other = halves(axis, bit, mine_ref.shape[0])
    out_ref[mine] = mine_ref[...]
    out_ref[other] = got_ref[...]


def grad_a_kernel(way, x_ref, s_ref, r_ref, after_ref, keep_ref, send_ref):
    low = (s_ref[...].astype(F32) + r_ref[...].astype(F32)).astype(BF)
    mine, other = halves(*way, x_ref.shape[1] // 2)
    send_ref[...] = (SCALE * dot(x_ref[:, other], low, ((0,), (0,)))).astype(BF)
    keep_ref[...] = SCALE * dot(x_ref[:, mine], low, ((0,), (0,)))


def grad_b_kernel(way, v_ref, s_ref, r_ref, after_ref, keep_ref, send_ref):
    low = (s_ref[...].astype(F32) + r_ref[...].astype(F32)).astype(BF)
    mine, other = halves(*way, v_ref.shape[1] // 2)
    sent = (SCALE * dot(low, v_ref[:, other], ((0,), (0,)))).astype(BF)
    kept = SCALE * dot(low, v_ref[:, mine], ((0,), (0,)))
    for b in blocks_of(v_ref.shape[1] // 2):
        send_ref[b] = sent[:, b]
        keep_ref[b] = kept[:, b]


def sum_kernel(keep_ref, got_ref, out_ref):
    out_ref[...] = (keep_ref[...].astype(F32) + got_ref[...].astype(F32)).astype(BF)


def step_kernel(mine_ref, got_ref, *rest):
    sum_kernel(mine_ref, got_ref, rest[len(rest) // 2])


def place_kernel(pos_ref, after_ref, out_ref):
    out_ref[...] = pos_ref[...].astype(F32)


def square_sum(ref):
    x = ref[...].astype(F32)
    return jnp.broadcast_to(jnp.sum(x * x), (8, LANES))


def update_kernel(way, hg_ref, mine_a, got_a, mine_b, after_ref, low_ref, ga_ref, squares_ref):
    join(*way, mine_a, got_a, ga_ref)
    low_ref[...] = dot(hg_ref[...], ga_ref[...]).astype(BF)
    squares_ref[0] = square_sum(mine_a) + square_sum(got_a)
    squares_ref[1] = square_sum(mine_b)


def norm_kernel(way, sums_ref, squares_ref, mine_b, got_b, after_ref, norm_ref, gb_ref):
    row = lax.broadcasted_iota(jnp.int32, (8, LANES), 0)
    squares = squares_ref[0] + (squares_ref[1] + square_sum(got_b))
    norm_ref[...] = split_terms(jnp.where(row == 7, squares, sums_ref[...]))
    join(*way, mine_b, got_b, gb_ref)


def base_kernel(mine_ref, near_ref, far_ref, far_got, after_ref, base_ref, low_ref):
    width = mine_ref.shape[1]
    low_ref[...] = far_ref[:, width:].astype(F32) + far_got[:, width:].astype(F32)
    for c in blocks_of(width):
        base_ref[:, c] = mine_ref[:, c].astype(F32) + near_ref[:, c].astype(F32) + far_got[:, c].astype(F32)


def final_kernel(
    base_ref, low_ref, s_ref, r_ref, sn_ref, rn_ref, ga_ref, gb_ref, a_ref, b_ref, cos_ref, sin_ref,
    a_hbm, b_hbm, q_hbm, new_a, new_b, half_b, out, sems,
):
    count, width = base_ref.shape
    total = join_terms(sn_ref[...]) + join_terms(rn_ref[...])
    rate = (LEARN * lax.rsqrt(total + NORM_EPS))[7:8]
    scales = lax.rsqrt(total / D + EPS)
    for c in blocks_of(width):
        fresh = b_ref[:, c] - rate * gb_ref[c].astype(F32)
        new_b[:, c] = fresh
        half_b[:, c] = fresh.astype(BF)
    copies = [pltpu.make_async_copy(new_b, b_hbm, sems.at[0])]
    copies[-1].start()
    new_a[...] = a_ref[...] - rate * ga_ref[...].astype(F32)
    copies.append(pltpu.make_async_copy(new_a, a_hbm, sems.at[1]))
    copies[-1].start()
    for i, b in enumerate(blocks_of(count)):
        low = s_ref[b].astype(F32) + r_ref[b].astype(F32)
        scale = jnp.broadcast_to(scales[i : i + 1], (LANES, LANES)).T
        mix = (low_ref[b] - rate * low) * scale * SCALE
        update = dot(mix.astype(BF), half_b[...])
        cos, sin = cos_ref[b], sin_ref[b]
        for c in blocks_of(width):
            query = base_ref[b, c] * scale + update[:, c]
            other = pltpu.roll(query, HEAD // 2, 1)
            out[b, c] = (query * cos + other * sin).astype(BF)
        copies.append(pltpu.make_async_copy(out.at[b], q_hbm.at[b], sems.at[2 + i]))
        copies[-1].start()
    for copy in copies:
        copy.wait()


def keep_hbm(x):
    return pltpu.with_memory_space_constraint(x, pltpu.HBM)


WEIGHTS = {"rank_v": 2.4, "prep": 0.6, "query_diag": 40.0, "query_beside": 1.8, "query_close": 2.7, "base": 1.0, "grad_b": 40.0, "final": 1.8, "update": 3.0}
FLOPS_PER_WEIGHT = 1_150_000_000


def call(kernel, outs, in_specs, args, name, scratch=(), out_specs=None, limit=16, aliases=None):
    return pl.pallas_call(
        kernel,
        out_shape=outs,
        in_specs=in_specs,
        out_specs=out_specs if out_specs is not None else jax.tree.map(lambda _: VMEM, outs),
        scratch_shapes=list(scratch),
        compiler_params=pltpu.CompilerParams(vmem_limit_bytes=int(limit * 1024 * 1024)),
        input_output_aliases=aliases or {},
        cost_estimate=pl.CostEstimate(
            flops=int(WEIGHTS.get(name, 0.01) * FLOPS_PER_WEIGHT), bytes_accessed=0, transcendentals=0
        ),
        name=name,
    )(*args)


def turn_tables(places, steps):
    half = HEAD // 2
    freq = 10000.0 ** (-jnp.arange(half, dtype=F32) / half)
    cos, sin = [], []
    for step in range(steps):
        angle = (places + float(step))[:, None] * freq[None, :]
        c, s = jnp.cos(angle), jnp.sin(angle)
        cos.append(jnp.concatenate([c, c], axis=-1))
        sin.append(jnp.concatenate([-s, s], axis=-1))
    return jnp.concatenate(cos), jnp.concatenate(sin)


def bits_of(n):
    return [b for b in range(n.bit_length() - 1)]


def build(n_dp, n_roll, n_tp):
    z_bits = [("roll", b) for b in bits_of(n_roll)]
    x_bits = [("dp", b) for b in bits_of(n_dp)]
    sizes = {"dp": n_dp, "roll": n_roll}

    def cross(x, axis, bit):
        return swap(x, axis, sizes[axis], 1 << bit)

    path_a, path_b = z_bits + x_bits + z_bits[:1], x_bits[:1] + z_bits + x_bits[1:] + x_bits[:1]

    def on_device(
        train_inputs, train_cotangent, factor_a, factor_b, base_weight, incoming, norm_gain, positions
    ):
        steps, rows, width = incoming.shape
        tokens = train_inputs.shape[0]
        rank = factor_a.shape[1]
        count = steps * rows
        dma = lambda n: pltpu.SemaphoreType.DMA((n,))
        vmem = lambda n, dtype=F32: pltpu.VMEM((n, rank), dtype)

        cut = 512
        tall = shape((count, width), BF)
        low_shape = shape((tokens, rank), BF)
        part_v, inputs, cotangent, half_a, hidden, first_columns = call(
            rank_v_kernel,
            [low_shape, shape(train_inputs.shape, BF), shape(train_inputs.shape, BF), shape(factor_a.shape, BF), tall,
             shape((width, cut), BF)],
            [HBM] * 6,
            tuple(
                map(
                    keep_hbm,
                    (train_inputs, train_cotangent, factor_a, factor_b, incoming.reshape(count, width), base_weight),
                )
            ),
            "rank_v",
            [pltpu.VMEM(factor_a.shape, F32), pltpu.VMEM(factor_b.shape, F32), dma(6)],
        )
        got_v = swap(part_v, "tp", n_tp, 1)
        part_u = call(rank_u_kernel, low_shape, [VMEM] * 2, (inputs, half_a), "rank_u")
        got_u = swap(part_u, "tp", n_tp, 1)
        wide = shape((count, width + rank), BF)
        gained, low, sums = call(
            prep_kernel,
            [tall, shape((count, rank), BF), shape((8, LANES), F32)],
            [VMEM] * 3,
            (hidden, norm_gain[None, :], half_a),
            "prep",
        )
        low_v = call(part_kernel, low_shape, [VMEM] * 2 + [ANY], (part_v, got_v, low), "low_v")
        far_v = swap(low_v, "tp", n_tp, 2)
        low_u = call(part_kernel, low_shape, [VMEM] * 2 + [ANY], (part_u, got_u, low_v), "low_u")
        far_u = swap(low_u, "tp", n_tp, 2)

        def query(peers, outs, after, name):
            blocks = len(peers) * width // cut
            return call(
                functools.partial(query_kernel, peers),
                outs,
                [VMEM, HBM, ANY],
                (gained, keep_hbm(base_weight), after),
                "query_" + name,
                [pltpu.VMEM((blocks, width, cut), BF), dma(blocks)],
            )

        per = width // cut
        diag, *columns = call(
            diag_kernel,
            [wide] + [shape((width, cut), BF)] * per,
            [VMEM, VMEM, HBM, VMEM, ANY],
            (gained, first_columns, keep_hbm(base_weight), low, low_u),
            "query_diag",
            [pltpu.VMEM((per - 1, width, cut), BF), dma(2 * per - 1)],
        )
        diag_got = swap(diag, "tp", n_tp, 1)

        block = shape((count, cut), BF)
        distant_first = call(block_kernel, block, [VMEM] * 2 + [ANY], (gained, columns[0], diag), "distant_first")
        half = width // 2
        keep_a, send_a = call(
            functools.partial(grad_a_kernel, path_a[0]),
            [shape((half, rank), F32), shape((half, rank), BF)],
            [VMEM] * 3 + [ANY],
            (inputs, low_v, far_v, distant_first),
            "grad_a",
        )
        keep_b, send_b = call(
            functools.partial(grad_b_kernel, path_b[0]),
            [shape((half, rank), F32), shape((half, rank), BF)],
            [VMEM] * 3 + [ANY],
            (cotangent, low_u, far_u, send_a),
            "grad_b",
        )
        distant_rest = call(block_kernel, block, [VMEM] * 2 + [ANY], (gained, columns[1], send_b), "distant_rest")
        far = call(far_kernel, wide, [VMEM] * 4, (distant_first, distant_rest, diag, diag_got), "far")
        far_got = swap(far, "tp", n_tp, 2)

        def step(mine, send, way, after, passed, name):
            return call(
                step_kernel,
                [shape((half, rank), BF)] + [shape(x.shape, x.dtype) for x in passed],
                [VMEM] * 2 + [ANY] * (1 + len(passed)),
                (mine, cross(send, *way), after, *passed),
                name,
                out_specs=[VMEM] + [ANY] * len(passed),
                aliases={3 + k: 1 + k for k in range(len(passed))},
            )

        mine_a, mine_b, after, passed = keep_a, keep_b, far, []
        order = ["a", "b", "n", "b", "a", "c", "a", "b", "t"] if n_dp * n_roll == 8 else ["a", "b", "n", "b", "a", "c"] + ["a", "b"] * (len(path_a) - 3) + ["t"]
        steps_a, steps_b = iter(path_a[:-1]), iter(path_b[:-1])
        for i, which in enumerate(order):
            if which == "a":
                mine_a, *made = step(mine_a, send_a, next(steps_a), after, passed, f"step_a{i}")
                send_a = after = mine_a
                if made:
                    beside_got, passed = swap(made[0], "tp", n_tp, 1), []
            elif which == "b":
                mine_b = send_b = after = step(mine_b, send_b, next(steps_b), after, [], f"step_b{i}")[0]
            elif which == "t":
                pos = positions.reshape(-1, LANES)
                places = call(place_kernel, shape(pos.shape, F32), [VMEM, ANY], (pos, after), "places")
                cos, sin = turn_tables(places.reshape(rows), steps)
                after = sin
            elif which == "n":
                passed = query((1,), [tall], after, "beside")
            else:
                (close,) = query((0,), [tall], after, "close")
                after = close
        step_low, grad_a, squares = call(
            functools.partial(update_kernel, path_a[-1]),
            [shape((count, rank), BF), shape((width, rank), BF), shape((2, 8, LANES), F32)],
            [VMEM] * 4 + [ANY],
            (gained, mine_a, cross(mine_a, *path_a[-1]), mine_b, after),
            "update",
        )
        step_got = swap(step_low, "tp", n_tp, 1)
        norm, grad_b = call(
            functools.partial(norm_kernel, path_b[-1]),
            [shape((EXTRA, LANES), BF), shape((width, rank), BF)],
            [VMEM] * 4 + [ANY],
            (sums, squares, mine_b, cross(mine_b, *path_b[-1]), step_low),
            "norm",
        )
        norm_got = swap(norm, "tp", n_tp, 1)
        step_sum = call(
            part_kernel, shape((count, rank), BF), [VMEM] * 2 + [ANY], (step_low, step_got, norm), "merge"
        )
        step_far = swap(step_sum, "tp", n_tp, 2)
        norm_sum = call(
            merge_kernel, shape((EXTRA, LANES), BF), [VMEM] * 2 + [ANY], (norm, norm_got, step_sum), "norm_merge"
        )
        norm_far = swap(norm_sum, "tp", n_tp, 2)
        base, low_all = call(
            base_kernel,
            [shape((count, width), F32), shape((count, rank), F32)],
            [VMEM] * 4 + [ANY],
            (close, beside_got, far, far_got, step_sum),
            "base",
        )
        new_a, new_b, queries = call(
            final_kernel,
            [shape((width, rank), F32), shape((rank, width), F32), tall],
            [VMEM] * 12,
            (base, low_all, step_sum, step_far, norm_sum, norm_far, grad_a, grad_b, factor_a, factor_b, cos, sin),
            "final",
            [pltpu.VMEM((width, rank), F32), pltpu.VMEM((rank, width), F32),
             pltpu.VMEM((rank, width), BF), pltpu.VMEM((count, width), BF), dma(2 + count // LANES)],
            [HBM] * 3,
        )
        return new_a, new_b, queries.reshape(steps, rows, width)

    return on_device


def solution(mesh):
    n_dp, n_roll, n_tp = (mesh.shape[a] for a in ("dp", "roll", "tp"))
    return jax.shard_map(
        build(n_dp, n_roll, n_tp),
        mesh=mesh,
        in_specs=(
            P(("dp", "roll"), "tp"),
            P(("dp", "roll"), "tp"),
            P("tp", None),
            P(None, "tp"),
            P("tp", None),
            P(None, ("dp", "roll"), "tp"),
            P("tp"),
            P(("dp", "roll")),
        ),
        out_specs=(P("tp", None), P(None, "tp"), P(None, ("dp", "roll"), "tp")),
        check_vma=False,
    )
```

```python
import functools

import jax
import jax.numpy as jnp
from jax import lax
from jax.experimental import pallas as pl
from jax.experimental.pallas import tpu as pltpu
from jax.sharding import PartitionSpec as P

D = 4096
HEAD = 128
SCALE = 2.0
LEARN = 3.0
EPS = 1e-05
NORM_EPS = 1e-06
LANES = 128
EXTRA = 32

BF = jnp.bfloat16
F32 = jnp.float32
VMEM = pl.BlockSpec(memory_space=pltpu.VMEM)
ANY = pl.BlockSpec(memory_space=pl.ANY)
HBM = pl.BlockSpec(memory_space=pltpu.HBM)


def shape(dims, dtype):
    return jax.ShapeDtypeStruct(dims, dtype)


def dot(a, b, dims=((1,), (0,))):
    return lax.dot_general(a, b, (dims, ((), ())), preferred_element_type=F32)


def swap(x, axis, n, k):
    return lax.ppermute(x, axis, [(i, i ^ k) for i in range(n)])


def split_terms(values):
    high = values.astype(BF)
    rest = values - high.astype(F32)
    middle = rest.astype(BF)
    last = (rest - middle.astype(F32)).astype(BF)
    return jnp.concatenate([high, middle, last, jnp.zeros_like(last)], axis=0)


def join_terms(terms):
    x = terms.astype(F32)
    return (x[0:8] + x[8:16]) + x[16:24]


def fetch(sources, targets, sems):
    copies = [pltpu.make_async_copy(s, t, sems.at[i]) for i, (s, t) in enumerate(zip(sources, targets))]
    for copy in copies:
        copy.start()
    return copies


def blocks_of(count):
    return [slice(i, i + LANES) for i in range(0, count, LANES)]


def rank_v_kernel(
    x_hbm, v_hbm, a_hbm, b_hbm, h_hbm, w_hbm, out_ref, x_ref, v_ref, a16_ref, h_ref, w_ref, a_ref, b_ref, sems
):
    first = weight_blocks((3,), w_hbm, w_ref.shape[1])[0]
    copies = fetch((v_hbm, b_hbm, x_hbm, a_hbm, h_hbm, first), (v_ref, b_ref, x_ref, a_ref, h_ref, w_ref), sems)
    copies[1].wait()
    b16 = b_ref[...].astype(BF)
    copies[0].wait()
    out_ref[...] = dot(v_ref[...], b16, ((1,), (1,))).astype(BF)
    copies[3].wait()
    a16_ref[...] = a_ref[...].astype(BF)
    for i in (2, 4, 5):
        copies[i].wait()


def rank_u_kernel(x_ref, a16_ref, out_ref):
    out_ref[...] = dot(x_ref[...], a16_ref[...]).astype(BF)


def weight_blocks(peers, w_hbm, cut):
    width = w_hbm.shape[0]
    mine = lax.axis_index("tp")
    sources = []
    for peer in peers:
        for i in range(width // cut):
            start = (mine ^ peer) * width + i * cut
            sources.append(w_hbm.at[:, pl.ds(pl.multiple_of(start, cut), cut)])
    return sources


def prep_kernel(h_ref, gain_ref, a16_ref, hg_ref, low_ref, sums_ref):
    count, width = h_ref.shape
    rows = []
    for b in blocks_of(count):
        wide = h_ref[b].astype(F32)
        hg_ref[b] = (wide * gain_ref[...]).astype(BF)
        sums = jnp.sum(wide * wide, axis=-1, keepdims=True)
        rows.append(jnp.broadcast_to(sums, (LANES, LANES)).T[0:1])
    if len(rows) < 8:
        rows.append(jnp.zeros((8 - len(rows), LANES), F32))
    sums_ref[...] = jnp.concatenate(rows, axis=0)
    low_ref[...] = dot(hg_ref[...], a16_ref[...]).astype(BF)


def part_kernel(x_ref, got_ref, after_ref, out_ref):
    sum_kernel(x_ref, got_ref, out_ref)


def query_kernel(peers, hg_ref, w_hbm, after_ref, *rest):
    outs, (w_ref, sems) = rest[:-2], rest[-2:]
    _, width, cut = w_ref.shape
    copies = fetch(weight_blocks(peers, w_hbm, cut), [w_ref.at[i] for i in range(w_ref.shape[0])], sems)
    per = width // cut
    for i, copy in enumerate(copies):
        copy.wait()
        outs[i // per][:, i % per * cut : (i % per + 1) * cut] = dot(hg_ref[...], w_ref[i]).astype(BF)


def diag_kernel(hg_ref, w_ref, w_hbm, low_ref, after_ref, out_ref, next_ref, rest_ref, sems):
    per, width, cut = next_ref.shape
    sources = weight_blocks((3, 2), w_hbm, cut)[1:]
    targets = [rest_ref.at[i] for i in range(per - 1)] + [next_ref.at[i] for i in range(per)]
    copies = fetch(sources, targets, sems)
    out_ref[:, :cut] = dot(hg_ref[...], w_ref[...]).astype(BF)
    out_ref[:, width:] = low_ref[...]
    for i in range(1, per):
        copies[i - 1].wait()
        out_ref[:, i * cut : (i + 1) * cut] = dot(hg_ref[...], rest_ref[i - 1]).astype(BF)
    for copy in copies[per - 1 :]:
        copy.wait()


def distant_kernel(hg_ref, w_ref, after_ref, out_ref):
    per, _, cut = w_ref.shape
    for i in range(per):
        out_ref[:, i * cut : (i + 1) * cut] = dot(hg_ref[...], w_ref[i]).astype(BF)


def far_kernel(mine_ref, diag_ref, got_ref, after_ref, out_ref):
    width = mine_ref.shape[1]
    sum_kernel(mine_ref, got_ref.at[:, :width], out_ref.at[:, :width])
    sum_kernel(diag_ref.at[:, width:], got_ref.at[:, width:], out_ref.at[:, width:])


def merge_kernel(a_ref, b_ref, after_ref, out_ref):
    out_ref[...] = split_terms(join_terms(a_ref[...]) + join_terms(b_ref[...]))


def halves(axis, bit, size):
    mine = lax.rem(lax.axis_index(axis) // (1 << bit), 2) * size
    return pl.ds(pl.multiple_of(mine, size), size), pl.ds(pl.multiple_of(size - mine, size), size)


def join(axis, bit, mine_ref, got_ref, out_ref):
    mine, other = halves(axis, bit, mine_ref.shape[0])
    out_ref[mine] = mine_ref[...]
    out_ref[other] = got_ref[...]


def grad_a_kernel(way, x_ref, s_ref, r_ref, after_ref, keep_ref, send_ref):
    low = (s_ref[...].astype(F32) + r_ref[...].astype(F32)).astype(BF)
    mine, other = halves(*way, x_ref.shape[1] // 2)
    send_ref[...] = (SCALE * dot(x_ref[:, other], low, ((0,), (0,)))).astype(BF)
    keep_ref[...] = SCALE * dot(x_ref[:, mine], low, ((0,), (0,)))


def grad_b_kernel(way, v_ref, s_ref, r_ref, after_ref, keep_ref, send_ref):
    low = (s_ref[...].astype(F32) + r_ref[...].astype(F32)).astype(BF)
    mine, other = halves(*way, v_ref.shape[1] // 2)
    sent = (SCALE * dot(low, v_ref[:, other], ((0,), (0,)))).astype(BF)
    kept = SCALE * dot(low, v_ref[:, mine], ((0,), (0,)))
    for b in blocks_of(v_ref.shape[1] // 2):
        send_ref[b] = sent[:, b]
        keep_ref[b] = kept[:, b]


def sum_kernel(keep_ref, got_ref, out_ref):
    out_ref[...] = (keep_ref[...].astype(F32) + got_ref[...].astype(F32)).astype(BF)


def step_kernel(mine_ref, got_ref, *rest):
    sum_kernel(mine_ref, got_ref, rest[len(rest) // 2])


def place_kernel(pos_ref, after_ref, out_ref):
    out_ref[...] = pos_ref[...].astype(F32)


def square_sum(ref):
    x = ref[...].astype(F32)
    return jnp.broadcast_to(jnp.sum(x * x), (8, LANES))


def update_kernel(way, hg_ref, mine_a, got_a, mine_b, after_ref, low_ref, ga_ref, squares_ref):
    join(*way, mine_a, got_a, ga_ref)
    low_ref[...] = dot(hg_ref[...], ga_ref[...]).astype(BF)
    squares_ref[0] = square_sum(mine_a) + square_sum(got_a)
    squares_ref[1] = square_sum(mine_b)


def norm_kernel(way, sums_ref, squares_ref, mine_b, got_b, after_ref, norm_ref, gb_ref):
    row = lax.broadcasted_iota(jnp.int32, (8, LANES), 0)
    squares = squares_ref[0] + (squares_ref[1] + square_sum(got_b))
    norm_ref[...] = split_terms(jnp.where(row == 7, squares, sums_ref[...]))
    join(*way, mine_b, got_b, gb_ref)


def base_kernel(mine_ref, near_ref, far_ref, far_got, after_ref, base_ref, low_ref):
    width = mine_ref.shape[1]
    low_ref[...] = far_ref[:, width:].astype(F32) + far_got[:, width:].astype(F32)
    for c in blocks_of(width):
        base_ref[:, c] = mine_ref[:, c].astype(F32) + near_ref[:, c].astype(F32) + far_got[:, c].astype(F32)


def final_kernel(
    base_ref, low_ref, s_ref, r_ref, sn_ref, rn_ref, ga_ref, gb_ref, a_ref, b_ref, cos_ref, sin_ref,
    a_hbm, b_hbm, q_hbm, new_a, new_b, half_b, out, sems,
):
    count, width = base_ref.shape
    total = join_terms(sn_ref[...]) + join_terms(rn_ref[...])
    rate = (LEARN * lax.rsqrt(total + NORM_EPS))[7:8]
    scales = lax.rsqrt(total / D + EPS)
    for c in blocks_of(width):
        fresh = b_ref[:, c] - rate * gb_ref[c].astype(F32)
        new_b[:, c] = fresh
        half_b[:, c] = fresh.astype(BF)
    copies = [pltpu.make_async_copy(new_b, b_hbm, sems.at[0])]
    copies[-1].start()
    for i, b in enumerate(blocks_of(count)):
        low = s_ref[b].astype(F32) + r_ref[b].astype(F32)
        scale = jnp.broadcast_to(scales[i : i + 1], (LANES, LANES)).T
        mix = (low_ref[b] - rate * low) * scale * SCALE
        update = dot(mix.astype(BF), half_b[...])
        cos, sin = cos_ref[b], sin_ref[b]
        for c in blocks_of(width):
            query = base_ref[b, c] * scale + update[:, c]
            other = pltpu.roll(query, HEAD // 2, 1)
            out[b, c] = (query * cos + other * sin).astype(BF)
        copies.append(pltpu.make_async_copy(out.at[b], q_hbm.at[b], sems.at[1 + i]))
        copies[-1].start()
        part = a_ref.shape[0] * LANES // count
        rows = slice(i * part, (i + 1) * part)
        new_a[rows] = a_ref[rows] - rate * ga_ref[rows].astype(F32)
        copies.append(pltpu.make_async_copy(new_a.at[rows], a_hbm.at[rows], sems.at[1 + count // LANES + i]))
        copies[-1].start()
    for copy in copies:
        copy.wait()


def keep_hbm(x):
    return pltpu.with_memory_space_constraint(x, pltpu.HBM)


WEIGHTS = {"rank_v": 2.4, "prep": 0.6, "query_diag": 40.0, "query_beside": 1.8, "query_close": 2.7, "base": 1.0, "grad_b": 40.0, "final": 1.8, "update": 3.0}
FLOPS_PER_WEIGHT = 1_150_000_000


def call(kernel, outs, in_specs, args, name, scratch=(), out_specs=None, limit=16, aliases=None):
    return pl.pallas_call(
        kernel,
        out_shape=outs,
        in_specs=in_specs,
        out_specs=out_specs if out_specs is not None else jax.tree.map(lambda _: VMEM, outs),
        scratch_shapes=list(scratch),
        compiler_params=pltpu.CompilerParams(vmem_limit_bytes=int(limit * 1024 * 1024)),
        input_output_aliases=aliases or {},
        cost_estimate=pl.CostEstimate(
            flops=int(WEIGHTS.get(name, 0.01) * FLOPS_PER_WEIGHT), bytes_accessed=0, transcendentals=0
        ),
        name=name,
    )(*args)


def turn_tables(places, steps):
    half = HEAD // 2
    freq = 10000.0 ** (-jnp.arange(half, dtype=F32) / half)
    cos, sin = [], []
    for step in range(steps):
        angle = (places + float(step))[:, None] * freq[None, :]
        c, s = jnp.cos(angle), jnp.sin(angle)
        cos.append(jnp.concatenate([c, c], axis=-1))
        sin.append(jnp.concatenate([-s, s], axis=-1))
    return jnp.concatenate(cos), jnp.concatenate(sin)


def bits_of(n):
    return [b for b in range(n.bit_length() - 1)]


def build(n_dp, n_roll, n_tp):
    z_bits = [("roll", b) for b in bits_of(n_roll)]
    x_bits = [("dp", b) for b in bits_of(n_dp)]
    sizes = {"dp": n_dp, "roll": n_roll}

    def cross(x, axis, bit):
        return swap(x, axis, sizes[axis], 1 << bit)

    path_a, path_b = z_bits + x_bits + z_bits[:1], x_bits[:1] + z_bits + x_bits[1:] + x_bits[:1]

    def on_device(
        train_inputs, train_cotangent, factor_a, factor_b, base_weight, incoming, norm_gain, positions
    ):
        steps, rows, width = incoming.shape
        tokens = train_inputs.shape[0]
        rank = factor_a.shape[1]
        count = steps * rows
        dma = lambda n: pltpu.SemaphoreType.DMA((n,))
        vmem = lambda n, dtype=F32: pltpu.VMEM((n, rank), dtype)

        cut = 512
        tall = shape((count, width), BF)
        low_shape = shape((tokens, rank), BF)
        part_v, inputs, cotangent, half_a, hidden, first_columns = call(
            rank_v_kernel,
            [low_shape, shape(train_inputs.shape, BF), shape(train_inputs.shape, BF), shape(factor_a.shape, BF), tall,
             shape((width, cut), BF)],
            [HBM] * 6,
            tuple(
                map(
                    keep_hbm,
                    (train_inputs, train_cotangent, factor_a, factor_b, incoming.reshape(count, width), base_weight),
                )
            ),
            "rank_v",
            [pltpu.VMEM(factor_a.shape, F32), pltpu.VMEM(factor_b.shape, F32), dma(6)],
        )
        got_v = swap(part_v, "tp", n_tp, 1)
        part_u = call(rank_u_kernel, low_shape, [VMEM] * 2, (inputs, half_a), "rank_u")
        got_u = swap(part_u, "tp", n_tp, 1)
        wide = shape((count, width + rank), BF)
        gained, low, sums = call(
            prep_kernel,
            [tall, shape((count, rank), BF), shape((8, LANES), F32)],
            [VMEM] * 3,
            (hidden, norm_gain[None, :], half_a),
            "prep",
        )
        low_v = call(part_kernel, low_shape, [VMEM] * 2 + [ANY], (part_v, got_v, low), "low_v")
        far_v = swap(low_v, "tp", n_tp, 2)
        low_u = call(part_kernel, low_shape, [VMEM] * 2 + [ANY], (part_u, got_u, low_v), "low_u")
        far_u = swap(low_u, "tp", n_tp, 2)

        def query(peers, outs, after, name):
            blocks = len(peers) * width // cut
            return call(
                functools.partial(query_kernel, peers),
                outs,
                [VMEM, HBM, ANY],
                (gained, keep_hbm(base_weight), after),
                "query_" + name,
                [pltpu.VMEM((blocks, width, cut), BF), dma(blocks)],
            )

        per = width // cut
        diag, columns = call(
            diag_kernel,
            [wide, shape((per, width, cut), BF)],
            [VMEM, VMEM, HBM, VMEM, ANY],
            (gained, first_columns, keep_hbm(base_weight), low, low_u),
            "query_diag",
            [pltpu.VMEM((per - 1, width, cut), BF), dma(2 * per - 1)],
        )
        diag_got = swap(diag, "tp", n_tp, 1)

        half = width // 2
        keep_a, send_a = call(
            functools.partial(grad_a_kernel, path_a[0]),
            [shape((half, rank), F32), shape((half, rank), BF)],
            [VMEM] * 3 + [ANY],
            (inputs, low_v, far_v, diag),
            "grad_a",
        )
        keep_b, send_b = call(
            functools.partial(grad_b_kernel, path_b[0]),
            [shape((half, rank), F32), shape((half, rank), BF)],
            [VMEM] * 3 + [ANY],
            (cotangent, low_u, far_u, send_a),
            "grad_b",
        )
        distant = call(distant_kernel, tall, [VMEM, VMEM, ANY], (gained, columns, send_b), "query_distant")
        far = call(far_kernel, wide, [VMEM] * 3 + [ANY], (distant, diag, diag_got, send_b), "far")
        far_got = swap(far, "tp", n_tp, 2)

        def step(mine, send, way, after, passed, name):
            return call(
                step_kernel,
                [shape((half, rank), BF)] + [shape(x.shape, x.dtype) for x in passed],
                [VMEM] * 2 + [ANY] * (1 + len(passed)),
                (mine, cross(send, *way), after, *passed),
                name,
                out_specs=[VMEM] + [ANY] * len(passed),
                aliases={3 + k: 1 + k for k in range(len(passed))},
            )

        mine_a, mine_b, after, passed = keep_a, keep_b, far, []
        order = ["a", "b", "n", "b", "a", "c", "a", "b", "t"] if n_dp * n_roll == 8 else ["a", "b", "n", "b", "a", "c"] + ["a", "b"] * (len(path_a) - 3) + ["t"]
        steps_a, steps_b = iter(path_a[:-1]), iter(path_b[:-1])
        for i, which in enumerate(order):
            if which == "a":
                mine_a, *made = step(mine_a, send_a, next(steps_a), after, passed, f"step_a{i}")
                send_a = after = mine_a
                if made:
                    beside_got, passed = swap(made[0], "tp", n_tp, 1), []
            elif which == "b":
                mine_b = send_b = after = step(mine_b, send_b, next(steps_b), after, [], f"step_b{i}")[0]
            elif which == "t":
                pos = positions.reshape(-1, LANES)
                places = call(place_kernel, shape(pos.shape, F32), [VMEM, ANY], (pos, after), "places")
                cos, sin = turn_tables(places.reshape(rows), steps)
                after = sin
            elif which == "n":
                passed = query((1,), [tall], after, "beside")
            else:
                (close,) = query((0,), [tall], after, "close")
                after = close
        step_low, grad_a, squares = call(
            functools.partial(update_kernel, path_a[-1]),
            [shape((count, rank), BF), shape((width, rank), BF), shape((2, 8, LANES), F32)],
            [VMEM] * 4 + [ANY],
            (gained, mine_a, cross(mine_a, *path_a[-1]), mine_b, after),
            "update",
        )
        step_got = swap(step_low, "tp", n_tp, 1)
        norm, grad_b = call(
            functools.partial(norm_kernel, path_b[-1]),
            [shape((EXTRA, LANES), BF), shape((width, rank), BF)],
            [VMEM] * 4 + [ANY],
            (sums, squares, mine_b, cross(mine_b, *path_b[-1]), step_low),
            "norm",
        )
        norm_got = swap(norm, "tp", n_tp, 1)
        step_sum = call(
            part_kernel, shape((count, rank), BF), [VMEM] * 2 + [ANY], (step_low, step_got, norm), "merge"
        )
        step_far = swap(step_sum, "tp", n_tp, 2)
        norm_sum = call(
            merge_kernel, shape((EXTRA, LANES), BF), [VMEM] * 2 + [ANY], (norm, norm_got, step_sum), "norm_merge"
        )
        norm_far = swap(norm_sum, "tp", n_tp, 2)
        base, low_all = call(
            base_kernel,
            [shape((count, width), F32), shape((count, rank), F32)],
            [VMEM] * 4 + [ANY],
            (close, beside_got, far, far_got, step_sum),
            "base",
        )
        new_a, new_b, queries = call(
            final_kernel,
            [shape((width, rank), F32), shape((rank, width), F32), tall],
            [VMEM] * 12,
            (base, low_all, step_sum, step_far, norm_sum, norm_far, grad_a, grad_b, factor_a, factor_b, cos, sin),
            "final",
            [pltpu.VMEM((width, rank), F32), pltpu.VMEM((rank, width), F32),
             pltpu.VMEM((rank, width), BF), pltpu.VMEM((count, width), BF), dma(1 + 2 * (count // LANES))],
            [HBM] * 3,
        )
        return new_a, new_b, queries.reshape(steps, rows, width)

    return on_device


def solution(mesh):
    n_dp, n_roll, n_tp = (mesh.shape[a] for a in ("dp", "roll", "tp"))
    return jax.shard_map(
        build(n_dp, n_roll, n_tp),
        mesh=mesh,
        in_specs=(
            P(("dp", "roll"), "tp"),
            P(("dp", "roll"), "tp"),
            P("tp", None),
            P(None, "tp"),
            P("tp", None),
            P(None, ("dp", "roll"), "tp"),
            P("tp"),
            P(("dp", "roll")),
        ),
        out_specs=(P("tp", None), P(None, "tp"), P(None, ("dp", "roll"), "tp")),
        check_vma=False,
    )
```
